256 devices in a mesh: frame: 32 (over z, x), row: 8 (over y, core).
Axes of the slice: x: 4, y: 4, z: 8, core: 2. Of those that a mesh axis runs over, the one named last changes fastest.
Arguments:
- frames_in: bfloat16 [64, 16, 64, 256], P('frame', 'row'), may hold values from -6 to 6
- w_space: bfloat16 [2304, 256], replicated, may hold values from -0.125 to 0.125
- w_time: bfloat16 [768, 256], replicated, may hold values from -0.21875 to 0.21875
- w_qkv: bfloat16 [256, 768], replicated, may hold values from -11 to 11
- w_out: bfloat16 [256, 256], replicated, may hold values from -0.375 to 0.375
- w_down: bfloat16 [2304, 512], replicated, may hold values from -0.125 to 0.125
- cotangent: bfloat16 [64, 8, 32, 512], P('frame', 'row'), may hold values from -0.046875 to 0.046875
Outputs:
- latent: bfloat16 [64, 8, 32, 512], P('frame', 'row')
- grad_space: float32 [589824], P(('frame', 'row'))
- grad_time: float32 [196608], P(('frame', 'row'))
- grad_qkv: float32 [196608], P(('frame', 'row'))
- grad_proj: float32 [65536], P(('frame', 'row'))
- grad_down: float32 [1179648], P(('frame', 'row'))
The draws below stay inside these ranges and needn't reach their ends.
All inputs are finite; a program needn't handle non-finite values.
Results may differ from the reference program's by a relative error of at most 0.024.
Values may be sent and summed in bfloat16 or wider, within the bound.
A program may use at most 64 MiB of HBM per device.

```python
import math
import jax
import jax.numpy as jnp
from jax import lax

C = 256
C2 = 512
W = 64
F = 64
H = 16


def draw_w_qkv(key, part):
    key = jax.random.fold_in(key, 7)
    main_key = jax.random.fold_in(key, 0)
    initial = jax.random.truncated_normal(main_key, -3.0, 3.0, (C, 3 * C), jnp.float32) / math.sqrt(C)
    return initial.astype(jnp.bfloat16)


def shard_levels(key, dims, cuts, least, largest):
    def one(position, shards_of):
        draws = jax.random.uniform(jax.random.fold_in(jax.random.fold_in(key, 6), position), (shards_of,), jnp.float32, least / len(cuts), largest / len(cuts))
        return jnp.repeat(jnp.exp(draws), dims[position] // shards_of).reshape((-1,) + (1,) * (len(dims) - position - 1))

    factor_of = one(*cuts[0])
    for cut in cuts[1:]:
        factor_of = factor_of * one(*cut)
    return factor_of


def normal_values(rng, shape, scale, bound, pieces=(), dtype=jnp.bfloat16):
    entries = jax.random.normal(rng, shape, jnp.float32) * scale
    if len(pieces) > 0:
        entries = shard_levels(rng, shape, pieces, -0.22, 0.18) * entries
    return jnp.clip(entries, min=-bound, max=bound).astype(dtype)


def setup_inputs(seed: int = 0) -> dict:
    streams_of = jax.random.split(jax.random.key(seed), 8)
    frames_in = normal_values(streams_of[0], (F, H, W, C), 1.0, 6.0, ((0, 32), (1, 8)))
    w_space = normal_values(streams_of[1], (9 * C, C), (9 * C) ** -0.5, 0.125)
    w_time = normal_values(streams_of[2], (3 * C, C), (3 * C) ** -0.5, 0.21875)
    w_qkv = draw_w_qkv(jax.random.fold_in(streams_of[7], 71), 0)
    w_out = normal_values(streams_of[4], (C, C), C ** -0.5, 0.375)
    w_down = normal_values(streams_of[5], (9 * C, C2), (9 * C) ** -0.5, 0.125)
    cotangent = normal_values(streams_of[6], (F, H // 2, W // 2, C2), (F * (H // 2) * (W // 2)) ** -0.5, 0.046875, ((0, 32), (1, 8)))
    return dict(frames_in=frames_in, w_space=w_space, w_time=w_time, w_qkv=w_qkv, w_out=w_out, w_down=w_down, cotangent=cotangent)


epsilon = 1e-06

def normed(activity):
    activity = activity.astype(jnp.float32)
    return activity * lax.rsqrt(lax.optimization_barrier(jnp.mean(activity * activity, axis=-1, keepdims=True)) + epsilon)

def activate(activity):
    return jax.nn.silu(normed(activity))

def activate_grad(activity, upstream):
    return jax.vjp(activate, activity.astype(jnp.float32))[1](upstream)[0]

def normed_grad(activity, upstream):
    return jax.vjp(normed, activity.astype(jnp.float32))[1](upstream)[0]

def taps_conv(padded, weight, row_count, col_count, stride):
    width_in = padded.shape[-1]
    frame_count = padded.shape[0]
    summed = jnp.zeros((frame_count * row_count * col_count, weight.shape[1]), jnp.float32)
    for a in range(3):
        for b in range(3):
            tap_slice = padded[:, a:a + stride * (row_count - 1) + 1:stride, b:b + stride * (col_count - 1) + 1:stride, :]
            weight_block = weight[(3 * a + b) * width_in:(3 * a + b + 1) * width_in]
            summed = summed + jnp.dot(tap_slice.reshape(-1, width_in), weight_block, preferred_element_type=jnp.float32)
    return summed.reshape(frame_count, row_count, col_count, weight.shape[1])

def conv_weight_grad(padded, upstream, row_count, col_count, stride):
    width_in = padded.shape[-1]
    flat_grad = upstream.reshape(-1, upstream.shape[-1])
    partials = []
    for a in range(3):
        for b in range(3):
            tap_slice = padded[:, a:a + stride * (row_count - 1) + 1:stride, b:b + stride * (col_count - 1) + 1:stride, :]
            partials.append(lax.dot_general(tap_slice.reshape(-1, width_in), flat_grad, (((0,), (0,)), ((), ())), preferred_element_type=jnp.float32))
    return jnp.concatenate(partials, axis=0)

def time_conv(extended, weight, frame_count):
    width_in = extended.shape[-1]
    summed = jnp.zeros((frame_count * extended.shape[1] * extended.shape[2], weight.shape[1]), jnp.float32)
    for k in range(3):
        frame_slice = extended[k:k + frame_count].reshape(-1, width_in)
        summed = summed + jnp.dot(frame_slice, weight[k * width_in:(k + 1) * width_in], preferred_element_type=jnp.float32)
    return summed.reshape(frame_count, extended.shape[1], extended.shape[2], weight.shape[1])

def time_transposed(ext_grad, weight, frame_count):
    width_in = weight.shape[0] // 3
    summed = jnp.zeros((frame_count * ext_grad.shape[1] * ext_grad.shape[2], width_in), jnp.float32)
    for k in range(3):
        frame_slice = ext_grad[2 - k:2 - k + frame_count].reshape(-1, ext_grad.shape[-1])
        summed = summed + lax.dot_general(frame_slice, weight[k * width_in:(k + 1) * width_in], (((1,), (1,)), ((), ())), preferred_element_type=jnp.float32)
    return summed.reshape(frame_count, ext_grad.shape[1], ext_grad.shape[2], width_in)

def time_weight_grad(extended, upstream, frame_count):
    width_in = extended.shape[-1]
    flat_grad = upstream.reshape(-1, upstream.shape[-1])
    partials = []
    for k in range(3):
        frame_slice = extended[k:k + frame_count].reshape(-1, width_in)
        partials.append(lax.dot_general(frame_slice, flat_grad, (((0,), (0,)), ((), ())), preferred_element_type=jnp.float32))
    return jnp.concatenate(partials, axis=0)

def down_transposed(grad_ext, weight, half_rows, half_cols):
    channels = weight.shape[0] // 9
    frame_count = grad_ext.shape[0]
    parity_taps = {0: ((1, 0),), 1: ((0, 1), (2, 0))}
    row_groups = []
    for row_parity in range(2):
        row_blocks = []
        for col_parity in range(2):
            summed = jnp.zeros((frame_count * half_rows * half_cols, channels), jnp.float32)
            for a, row_shift in parity_taps[row_parity]:
                for b, col_shift in parity_taps[col_parity]:
                    grad_slice = grad_ext[:, row_shift:row_shift + half_rows, col_shift:col_shift + half_cols, :].reshape(-1, grad_ext.shape[-1])
                    weight_block = weight[(3 * a + b) * channels:(3 * a + b + 1) * channels]
                    summed = summed + lax.dot_general(grad_slice, weight_block, (((1,), (1,)), ((), ())), preferred_element_type=jnp.float32)
            row_blocks.append(summed.reshape(frame_count, half_rows, half_cols, channels))
        row_groups.append(jnp.stack(row_blocks, axis=3))
    stacked = jnp.stack(row_groups, axis=2)
    return stacked.reshape(frame_count, 2 * half_rows, 2 * half_cols, channels)

def to_sequence(block):
    return block.transpose(1, 2, 0, 3).reshape(-1, block.shape[0], block.shape[3])

def from_sequence(sequence, shape):
    return sequence.reshape(shape[1], shape[2], shape[0], shape[3]).transpose(2, 0, 1, 3)

def attention_forward(sequence, w_qkv, w_out):
    positions, frame_count, channels = sequence.shape
    projected = jnp.dot(sequence.reshape(-1, channels), w_qkv, preferred_element_type=jnp.float32).astype(jnp.bfloat16)
    projected = projected.reshape(positions, frame_count, 3 * channels)
    query_rows = projected[..., :channels]
    key_matrix = projected[..., channels:2 * channels]
    value_matrix = projected[..., 2 * channels:]
    logit_scale = 1.0 / math.sqrt(channels)
    attention_logits = jnp.einsum('wkr,wjr->wkj', query_rows.astype(jnp.float32), key_matrix.astype(jnp.float32)) * logit_scale
    causal = jnp.arange(frame_count)[:, None] >= jnp.arange(frame_count)[None, :]
    attention_logits = jnp.where(causal[None], attention_logits, -1e+30)
    row_peak = lax.optimization_barrier(jnp.max(attention_logits, axis=-1, keepdims=True))
    exponent = jnp.exp(attention_logits - row_peak)
    weights = exponent / lax.optimization_barrier(jnp.sum(exponent, axis=-1, keepdims=True))
    attention_probabilities = weights.astype(jnp.bfloat16)
    mixture_output = jnp.einsum('lev,lvj->lej', attention_probabilities.astype(jnp.float32), value_matrix.astype(jnp.float32)).astype(jnp.bfloat16)
    attended = jnp.dot(mixture_output.reshape(-1, channels), w_out, preferred_element_type=jnp.float32).astype(jnp.bfloat16)
    return (attended.reshape(positions, frame_count, channels), (query_rows, key_matrix, value_matrix, weights, attention_probabilities, mixture_output))

def attention_backward(sequence, w_qkv, w_out, grad_att):
    positions, frame_count, channels = sequence.shape
    saved = attention_forward(sequence, w_qkv, w_out)[1]
    query_rows, key_matrix, value_matrix, weights, attention_probabilities, mixture_output = saved
    flat_grad = grad_att.reshape(-1, channels)
    grad_proj = lax.dot_general(mixture_output.reshape(-1, channels), flat_grad, (((0,), (0,)), ((), ())), preferred_element_type=jnp.float32)
    mixture_gradient = lax.dot_general(flat_grad, w_out, (((1,), (1,)), ((), ())), preferred_element_type=jnp.float32).astype(jnp.bfloat16)
    mixture_gradient = mixture_gradient.reshape(positions, frame_count, channels).astype(jnp.float32)
    probability_gradient = jnp.einsum('wkr,wjr->wkj', mixture_gradient, value_matrix.astype(jnp.float32))
    value_gradient = jnp.einsum('uyl,uyk->ulk', attention_probabilities.astype(jnp.float32), mixture_gradient)
    logit_scale = 1.0 / math.sqrt(channels)
    logit_gradient = (weights * (probability_gradient - lax.optimization_barrier(jnp.sum(probability_gradient * weights, axis=-1, keepdims=True))) * logit_scale).astype(jnp.bfloat16)
    query_gradient = jnp.einsum('lev,lvj->lej', logit_gradient.astype(jnp.float32), key_matrix.astype(jnp.float32))
    key_gradient = jnp.einsum('uyl,uyk->ulk', logit_gradient.astype(jnp.float32), query_rows.astype(jnp.float32))
    grad_projected = jnp.concatenate([query_gradient, key_gradient, value_gradient], axis=-1).astype(jnp.bfloat16).reshape(-1, 3 * channels)
    grad_qkv = lax.dot_general(sequence.reshape(-1, channels), grad_projected, (((0,), (0,)), ((), ())), preferred_element_type=jnp.float32)
    grad_seq = lax.dot_general(grad_projected, w_qkv, (((1,), (1,)), ((), ())), preferred_element_type=jnp.float32).astype(jnp.bfloat16)
    return (grad_seq.reshape(positions, frame_count, channels), grad_qkv, grad_proj)

def reference(frames_in, w_space, w_time, w_qkv, w_out, w_down, cotangent):
    frame_total, height, width_all, channels = frames_in.shape
    first_act = activate(frames_in).astype(jnp.bfloat16)
    padded_first = jnp.pad(first_act, ((0, 0), (1, 1), (1, 1), (0, 0)))
    spatial = (frames_in.astype(jnp.float32) + taps_conv(padded_first, w_space, height, width_all, 1)).astype(jnp.bfloat16)
    second_act = activate(spatial).astype(jnp.bfloat16)
    extended = jnp.pad(second_act, ((2, 0), (0, 0), (0, 0), (0, 0)))
    temporal = (spatial.astype(jnp.float32) + time_conv(extended, w_time, frame_total)).astype(jnp.bfloat16)
    normal_t = normed(temporal).astype(jnp.bfloat16)
    sequence = to_sequence(normal_t)
    attended = from_sequence(attention_forward(sequence, w_qkv, w_out)[0], normal_t.shape)
    residual = (temporal.astype(jnp.float32) + attended.astype(jnp.float32)).astype(jnp.bfloat16)
    fourth_act = activate(residual).astype(jnp.bfloat16)
    padded_fourth = jnp.pad(fourth_act, ((0, 0), (1, 0), (1, 0), (0, 0)))
    latent = taps_conv(padded_fourth, w_down, height // 2, width_all // 2, 2).astype(jnp.bfloat16)
    grad_ext = jnp.pad(cotangent, ((0, 0), (0, 1), (0, 1), (0, 0)))
    grad_fourth = down_transposed(grad_ext, w_down, height // 2, width_all // 2)
    grad_residual = activate_grad(residual, grad_fourth)
    grad_res_b = grad_residual.astype(jnp.bfloat16)
    grad_seq, grad_qkv, grad_proj = attention_backward(sequence, w_qkv, w_out, to_sequence(grad_res_b))
    grad_normed = from_sequence(grad_seq, normal_t.shape)
    grad_temporal = grad_residual + normed_grad(temporal, grad_normed.astype(jnp.float32))
    grad_temp_b = grad_temporal.astype(jnp.bfloat16)
    grad_second = time_transposed(jnp.pad(grad_temp_b, ((0, 2), (0, 0), (0, 0), (0, 0))), w_time, frame_total)
    grad_spatial = grad_temporal + activate_grad(spatial, grad_second)
    grad_spat_b = grad_spatial.astype(jnp.bfloat16)
    grad_space = conv_weight_grad(padded_first, grad_spat_b, height, width_all, 1)
    grad_time = time_weight_grad(extended, grad_temp_b, frame_total)
    grad_down = conv_weight_grad(padded_fourth, cotangent, height // 2, width_all // 2, 2)
    return (latent, grad_space.reshape(-1), grad_time.reshape(-1), grad_qkv.reshape(-1), grad_proj.reshape(-1), grad_down.reshape(-1))
```

```python
import math

import jax
import jax.numpy as jnp
from jax import lax
from jax.experimental import pallas as pl
from jax.experimental.pallas import tpu as pltpu
from jax.sharding import PartitionSpec as P

epsilon = 1e-06
f32 = jnp.float32
bf16 = jnp.bfloat16
MESH = pl.DeviceIdType.MESH
C = 256
FR, XS, ZS, YS, RS = 32, 4, 8, 4, 8


def nn(a, b):
    return jnp.dot(a, b, preferred_element_type=f32)


def nt(a, b):
    return lax.dot_general(a, b, (((1,), (1,)), ((), ())), preferred_element_type=f32)


def tn(a, b):
    return lax.dot_general(a, b, (((0,), (0,)), ((), ())), preferred_element_type=f32)


def inv_rms(v):
    return lax.rsqrt(jnp.mean(v * v, axis=-1, keepdims=True) + epsilon)


def sigmoid(n):
    return 1.0 / (1.0 + jnp.exp(-n))


def act(v):
    n = v * inv_rms(v)
    return n * sigmoid(n)


def rms_grad(normal, inv, upstream):
    return inv * (upstream - normal * jnp.mean(upstream * normal, axis=-1, keepdims=True))


def act_grad(v, upstream):
    inv = inv_rms(v)
    n = v * inv
    s = sigmoid(n)
    return rms_grad(n, inv, upstream * (s * (1.0 + n * (1.0 - s))))


def iota2(rows, cols):
    return (
        lax.broadcasted_iota(jnp.int32, (rows, cols), 0),
        lax.broadcasted_iota(jnp.int32, (rows, cols), 1),
    )


def one_at(hit):
    return jnp.where(hit, 1.0, 0.0).astype(bf16)


def row_shift(v, by):
    rows = v.shape[0]
    i = lax.broadcasted_iota(jnp.int32, v.shape, 0)
    moved = pltpu.roll(v, by % rows, axis=0)
    keep = i >= by if by > 0 else i < rows + by
    return jnp.where(keep, moved, 0.0)


def pack(m):
    m = m.reshape(FR, 8, C)
    return jnp.concatenate([m[:, :, :128], m[:, :, 128:]], axis=1)


def unpack(t):
    low = t[:, :8, :].reshape(C, 128)
    high = t[:, 8:16, :].reshape(C, 128)
    return jnp.concatenate([low, high], axis=1)


def put(ref, m):
    ref[0] = m[:, :128]
    ref[1] = m[:, 128:]


def every_fourth(ref, start):
    return jnp.concatenate([ref[u, pl.ds(start, 64, stride=4), :] for u in range(2)], axis=1)


def kernel(
    x_hbm, wsp_hbm, wt_hbm, wq_hbm, wo_hbm, wd_hbm, cot_hbm,
    lat_out, g_out,
    xv, wsp, wt, wq, wo, wd, cotv,
    halo_x, halo_c,
    a1s, a1r, a2s, a2r, a3s, a3r, a4s, a4r,
    tmp, tmp2, fc, fcl, halo_f, cotc, at_,
    gd, gt, gq_, gp_, gs_,
    cD, rcD, yD, ryD, zD, rzD,
    c1, rc1, y1, ry1,
    c2, rc2, y2, ry2,
    zE, rzE,
    fin_s, fin_r,
    lsem, hs, hr, as_, ar, cs_s, cs_r, ys_s, ys_r, zs_s, zs_r, fs_s, fs_r,
):
    fr = lax.axis_index("frame")
    r = lax.axis_index("row")
    z, x = fr >> 2, fr & 3
    y, c = r >> 1, r & 1

    def remote(src, dst, ssem, rsem, dev):
        cp = pltpu.make_async_remote_copy(
            src_ref=src, dst_ref=dst, send_sem=ssem, recv_sem=rsem, device_id=dev, device_id_type=MESH
        )
        cp.start()
        return cp

    def wait_for(ref, sem):
        pltpu.make_async_copy(ref, ref, sem).wait()

    up, down = (r + RS - 1) & 7, (r + 1) & 7
    halo = [
        remote(x_hbm.at[:, 1], halo_x.at[0], hs.at[0], hr.at[0], (fr, down)),
        remote(x_hbm.at[:, 0], halo_x.at[1], hs.at[1], hr.at[1], (fr, up)),
        remote(cot_hbm, halo_c, hs.at[2], hr.at[2], (fr, up)),
    ]
    loads = []
    for i, (src, dst) in enumerate(
        ((x_hbm, xv), (wsp_hbm, wsp), (cot_hbm, cotv), (wd_hbm, wd), (wt_hbm, wt), (wq_hbm, wq), (wo_hbm, wo))
    ):
        cp = pltpu.make_async_copy(src, dst, lsem.at[i])
        cp.start()
        loads.append(cp)

    def a2a_start(send, recv, i):
        def step(s, carry):
            k = (fr + s) & (FR - 1)
            remote(send.at[k], recv.at[fr], as_.at[i], ar.at[i], (k, r))
            return carry

        lax.fori_loop(1, FR, step, 0)
        recv[fr] = send[fr]

    def a2a_wait(recv, i):
        wait_for(recv.at[pl.ds(0, FR - 1)], ar.at[i])

    i256, j256 = iota2(C, C)
    k8, f8, h8, w8 = i256 >> 3, (i256 >> 2) & 1, (i256 >> 1) & 1, i256 & 1
    perm_cells = one_at(j256 == h8 * 128 + f8 * 64 + 2 * k8 + w8)
    loads[0].wait()
    xf = jnp.concatenate([xv[0, 0], xv[1, 0], xv[0, 1], xv[1, 1]], axis=0).astype(f32)
    first = act(xf).astype(bf16)
    loads[1].wait()

    def tap(a, b):
        return wsp[(3 * a + b) * C : (3 * a + b + 1) * C, :]

    parts = []
    for b in range(3):
        own = nn(first, tap(1, b))
        other = jnp.concatenate([nn(first[128:], tap(2, b)), nn(first[:128], tap(0, b))], axis=0)
        parts.append(own + other)
    halo[0].wait_recv()
    halo[1].wait_recv()
    top = act(jnp.concatenate([halo_x[0, 0], halo_x[0, 1]], axis=0).astype(f32))
    top = jnp.where(r > 0, top, 0.0).astype(bf16)
    bottom = act(jnp.concatenate([halo_x[1, 0], halo_x[1, 1]], axis=0).astype(f32))
    bottom = jnp.where(r < RS - 1, bottom, 0.0).astype(bf16)
    for b in range(3):
        parts[b] = parts[b] + jnp.concatenate([nn(top, tap(0, b)), nn(bottom, tap(2, b))], axis=0)
    col = i256 & 63
    spatial = xf + parts[1]
    spatial = spatial + jnp.where(col > 0, pltpu.roll(parts[0], 1, axis=0), 0.0)
    spatial = spatial + jnp.where(col < 63, pltpu.roll(parts[2], C - 1, axis=0), 0.0)
    a1s[...] = pack(nn(perm_cells, spatial.astype(bf16))).astype(bf16)
    a2a_start(a1s, a1r, 0)

    loads[2].wait()
    loads[3].wait()
    halo[2].wait_recv()
    own = jnp.concatenate([cotv[0, 0], cotv[1, 0]], axis=0)
    below = jnp.concatenate([halo_c[0, 0], halo_c[1, 0]], axis=0)
    below = jnp.where(r < RS - 1, below.astype(f32), 0.0)
    jcol = lax.broadcasted_iota(jnp.int32, (64, 512), 0) & 31
    shifted = []
    for v in (own.astype(f32), below):
        moved = jnp.where(jcol < 31, pltpu.roll(v, 63, axis=0), 0.0)
        shifted.append((v.astype(bf16), moved.astype(bf16)))
    taps_of = {0: ((1, 0),), 1: ((0, 1), (2, 0))}
    blocks = []
    for rp in range(2):
        for cp_ in range(2):
            total = None
            for a, rs in taps_of[rp]:
                for b, cs in taps_of[cp_]:
                    term = nt(shifted[rs][cs], wd[(3 * a + b) * C : (3 * a + b + 1) * C, :])
                    total = term if total is None else total + term
            blocks.append(total)
    gf = jnp.concatenate(blocks, axis=0).astype(bf16)
    perm_gf = one_at(j256 == h8 * 128 + w8 * 64 + f8 * 32 + k8)
    i512, j512 = iota2(512, C)
    u16 = i512 & 15
    f16, q16 = u16 >> 2, u16 & 3
    perm_cot = one_at((u16 < 8) & (j512 == q16 * 64 + f16 * 32 + (i512 >> 4)))
    cot_rows = jnp.concatenate([own[:, 128 * q : 128 * q + 128] for q in range(4)], axis=0)
    cot_tiles = nn(perm_cot, cot_rows).reshape(FR, 16, 128)
    a2s[...] = jnp.concatenate([pack(nn(perm_gf, gf)), cot_tiles], axis=1).astype(bf16)
    a2a_start(a2s, a2r, 1)

    ip, jp = iota2(C, 128)
    wpos = 2 * (ip >> 3) - 1 + (ip & 3)
    perm_patch = one_at((wpos >= 0) & (wpos < 64) & (jp == ((ip >> 2) & 1) * 64 + wpos))
    rows_ext = (top, first[:128], first[128:], bottom)
    a3s[...] = jnp.concatenate([pack(nn(perm_patch, v)) for v in rows_ext], axis=1).astype(bf16)
    a2a_start(a3s, a3r, 2)

    for i in range(4, 7):
        loads[i].wait()
    a2a_wait(a1r, 0)
    sp = unpack(a1r[...].astype(f32))
    second = act(sp).astype(bf16)
    wtk = [wt[k * C : (k + 1) * C, :] for k in range(3)]
    temporal = sp + nn(second, wtk[2])
    temporal = temporal + row_shift(nn(second, wtk[1]), 4)
    temporal = temporal + row_shift(nn(second, wtk[0]), 8)
    temporal = temporal.astype(bf16).astype(f32)
    inv_t = inv_rms(temporal)
    norm_t = temporal * inv_t
    norm_b = norm_t.astype(bf16)

    proj = nn(norm_b, wq[...]).astype(bf16)
    query, key, value = proj[:, :C], proj[:, C : 2 * C], proj[:, 2 * C :]
    scale = 1.0 / math.sqrt(C)
    logits = nt(query, key) * scale
    allowed = ((i256 & 3) == (j256 & 3)) & (i256 >= j256)
    logits = jnp.where(allowed, logits, -1e30)
    exponent = jnp.exp(logits - jnp.max(logits, axis=-1, keepdims=True))
    weights = exponent / jnp.sum(exponent, axis=-1, keepdims=True)
    weights_b = weights.astype(bf16)
    mixed = nn(weights_b, value).astype(bf16)
    attended = nn(mixed, wo[...]).astype(bf16).astype(f32)
    residual = (temporal + attended).astype(bf16).astype(f32)
    fourth = act(residual)

    put(tmp, fourth)
    for cell in range(4):
        fc[cell] = every_fourth(tmp, cell).astype(bf16)
    fcl[0] = fc[1]
    fcl[1] = fc[3]
    right = (fr + 1) & (FR - 1)
    fhalo = [
        remote(fc.at[pl.ds(2, 2)], halo_f.at[pl.ds(0, 2)], hs.at[3], hr.at[3], (fr, down)),
        remote(fcl, halo_f.at[pl.ds(2, 2)], hs.at[4], hr.at[4], (right, r)),
        remote(fc.at[3], halo_f.at[4], hs.at[5], hr.at[5], (right, down)),
    ]

    a2a_wait(a2r, 1)
    got = a2r[...].astype(f32)
    grad_res = act_grad(residual, unpack(got))
    grad_res_b = grad_res.astype(bf16)
    cotc[...] = got[:, 16:24, :].reshape(C, 128)
    cot_cell = jnp.concatenate(
        [cotc[pl.ds(q, 64, stride=4), :] for q in range(4)], axis=1
    ).astype(bf16)
    gp_[...] = tn(mixed, grad_res_b)
    grad_mixed = nt(grad_res_b, wo[...]).astype(bf16)

    for h in fhalo:
        h.wait_recv()
    not_top, not_left = r > 0, fr > 0

    def masked(v, keep):
        return jnp.where(keep, v.astype(f32), 0.0).astype(bf16)

    taps_in = [
        masked(halo_f[4], not_top & not_left), masked(halo_f[0], not_top), masked(halo_f[1], not_top),
        masked(halo_f[2], not_left), fc[0], fc[1],
        masked(halo_f[3], not_left), fc[2], fc[3],
    ]
    for t in range(9):
        gd[t * C : (t + 1) * C, :] = tn(taps_in[t], cot_cell)

    def pack_rows(read, cbuf, rows):
        def step(p, carry):
            xd, zp = p >> 2, p & 3
            for cc in range(2):
                both = jnp.concatenate(
                    [read(8 * zp + xd, cc), read(8 * zp + 4 + xd, cc)], axis=0
                )
                at = pl.multiple_of(zp * (2 * rows), 16)
                cbuf[cc, xd, pl.ds(at, 2 * rows), :] = both.astype(bf16)
            return carry

        lax.fori_loop(0, 16, step, 0)

    def read_d(block, cc):
        at = pl.multiple_of(block * 72, 8)
        return jnp.concatenate(
            [gd[pl.ds(at, 72), cc * 256 + q * 128 : cc * 256 + q * 128 + 128] for q in range(2)], axis=0
        )

    def read_1(block, cc):
        a24, a8 = pl.multiple_of(block * 24, 8), pl.multiple_of(block * 8, 8)
        pieces = [gt[pl.ds(a24, 24), cc * 128 : cc * 128 + 128]]
        pieces += [gq_[pl.ds(a8, 8), cc * 384 + m * 128 : cc * 384 + m * 128 + 128] for m in range(3)]
        pieces += [gp_[pl.ds(a8, 8), cc * 128 : cc * 128 + 128]]
        return jnp.concatenate(pieces, axis=0)

    def read_2(block, cc):
        at = pl.multiple_of(block * 72, 8)
        return gs_[pl.ds(at, 72), cc * 128 : cc * 128 + 128]

    def core_start(cbuf, rc, i):
        remote(cbuf.at[1 - c], rc, cs_s.at[i], cs_r.at[i], (fr, r ^ 1))

    def y_start(cbuf, rc, ybuf, ry, i, rows):
        wait_for(rc, cs_r.at[i])
        for s in (1, 2, 3, 0):
            j = (y + s) & 3

            def step(p, carry, j=j):
                at = pl.multiple_of(p * (2 * rows), 16)
                here = pl.ds(at, 2 * rows)
                total = cbuf[c, j, here, :].astype(f32) + rc[j, here, :].astype(f32)
                ybuf[j, here, :] = total.astype(bf16)
                return carry

            lax.fori_loop(0, 4, step, 0)
            if s:
                remote(ybuf.at[j], ry.at[s - 1], ys_s.at[i], ys_r.at[3 * i + s - 1], (fr, 2 * j + c))

    def y_total(ybuf, ry, p, rows):
        here = slice(2 * rows * p, 2 * rows * (p + 1))
        total = ybuf[y, here, :].astype(f32)
        for s in range(3):
            total = total + ry[s, here, :].astype(f32)
        return total

    def y_wait(ry, i):
        for s in range(3):
            wait_for(ry.at[s], ys_r.at[3 * i + s])

    def z_start(zbuf, rz, i):
        for s in range(1, ZS):
            zd = (z + s) & 7
            remote(zbuf.at[zd], rz.at[s - 1], zs_s.at[i], zs_r.at[7 * i + s - 1], (zd * 4 + x, r))

    def z_total(zbuf, rz, i):
        total = zbuf[z].astype(f32)
        for s in range(7):
            wait_for(rz.at[s], zs_r.at[7 * i + s])
            total = total + rz[s].astype(f32)
        return total

    pack_rows(read_d, cD, 144)
    core_start(cD, rcD, 0)

    grad_w = nt(grad_mixed, value)
    grad_s = (
        weights * (grad_w - jnp.sum(grad_w * weights, axis=-1, keepdims=True)) * scale
    ).astype(bf16)
    grad_v = tn(weights_b, grad_mixed).astype(bf16)
    grad_q = nn(grad_s, key).astype(bf16)
    grad_k = tn(grad_s, query).astype(bf16)
    grad_proj = jnp.concatenate([grad_q, grad_k, grad_v], axis=1)
    grad_n = nt(grad_proj, wq[...]).astype(bf16).astype(f32)
    gq_[...] = tn(norm_b, grad_proj)
    grad_t = grad_res + rms_grad(norm_t, inv_t, grad_n)
    grad_tb = grad_t.astype(bf16)
    grad_tb32 = grad_tb.astype(f32)

    y_start(cD, rcD, yD, ryD, 0, 144)

    grad_second = nt(grad_tb, wtk[2])
    grad_second = grad_second + row_shift(nt(grad_tb, wtk[1]), -4)
    grad_second = grad_second + row_shift(nt(grad_tb, wtk[0]), -8)
    gt[0:C, :] = tn(second, row_shift(grad_tb32, -8).astype(bf16))
    gt[C : 2 * C, :] = tn(second, row_shift(grad_tb32, -4).astype(bf16))
    gt[2 * C :, :] = tn(second, grad_tb)
    pack_rows(read_1, c1, 56)
    core_start(c1, rc1, 1)
    put(tmp, grad_t + act_grad(sp, grad_second))

    a2a_wait(a3r, 2)
    for hh in range(4):
        put(tmp2, unpack(a3r[:, 16 * hh : 16 * hh + 16, :].astype(f32)))
        cells = [every_fourth(tmp2, ww) for ww in range(4)]
        for b in range(3):
            pair = jnp.concatenate([cells[b], cells[b + 1]], axis=0)
            at_[b, :, 128 * hh : 128 * hh + 128] = pair.T.astype(bf16)
    grad_sb = jnp.concatenate([every_fourth(tmp, cell) for cell in range(4)], axis=0).astype(bf16)
    for a in range(3):
        for b in range(3):
            gs_[(3 * a + b) * C : (3 * a + b + 1) * C, :] = nn(at_[b, :, 128 * a : 128 * a + 256], grad_sb)
    pack_rows(read_2, c2, 72)
    core_start(c2, rc2, 2)
    y_start(c1, rc1, y1, ry1, 1, 56)

    latent = None
    for t in range(9):
        term = nn(taps_in[t], wd[t * C : (t + 1) * C, :])
        latent = term if latent is None else latent + term
    latent = latent.astype(bf16)
    lat_rows = jnp.concatenate([latent[:, 128 * q : 128 * q + 128] for q in range(4)], axis=0)
    perm_lat = one_at((u16 < 8) & (j512 == q16 * 64 + 2 * (i512 >> 4) + f16))
    a4s[...] = nn(perm_lat, lat_rows).reshape(FR, 16, 128).astype(bf16)
    a2a_start(a4s, a4r, 3)

    y_start(c2, rc2, y2, ry2, 2, 72)
    y_wait(ryD, 0)
    for p in range(4):
        total = y_total(yD, ryD, p, 144).astype(bf16)
        zD[2 * p] = total[:144]
        zD[2 * p + 1] = total[144:]
    z_start(zD, rzD, 0)

    a2a_wait(a4r, 3)
    cotc[...] = a4r[...].astype(f32)[:, :8, :].reshape(C, 128)
    for f in range(2):
        for q in range(4):
            lat_out[f, 0, :, 128 * q : 128 * q + 128] = cotc[pl.ds(4 * f + q, 32, stride=8), :].astype(bf16)

    y_wait(ry1, 1)
    y_wait(ry2, 2)
    for p in range(4):
        t1 = y_total(y1, ry1, p, 56)
        t2 = y_total(y2, ry2, p, 72)
        zE[2 * p] = jnp.concatenate([t2[:72], t1[:56]], axis=0).astype(bf16)
        zE[2 * p + 1] = jnp.concatenate([t2[72:], t1[56:]], axis=0).astype(bf16)
    z_start(zE, rzE, 1)

    total_d = z_total(zD, rzD, 0).astype(bf16)
    total_d = jnp.concatenate([total_d, jnp.zeros((112, 128), bf16)], axis=0)
    d32, u32 = i256 >> 5, i256 & 31
    q32 = jnp.where(u32 >= 9, 1, 0)
    perm_d = one_at((u32 < 18) & (j256 == q32 * 72 + d32 * 9 + u32 - 9 * q32))
    fin_d = nn(perm_d, total_d).reshape(RS, 32, 128)
    ie, je = iota2(128, 128)
    de, ue = ie >> 4, ie & 15
    source = jnp.where(
        ue < 9, de * 9 + ue,
        jnp.where(ue < 12, 72 + de * 3 + ue - 9, jnp.where(ue < 15, 96 + (ue - 12) * 8 + de, 120 + de)),
    )
    perm_e = one_at(je == source)
    total_e = z_total(zE, rzE, 1).astype(bf16)
    fin_e = nn(perm_e, total_e).reshape(RS, 16, 128)
    fin_s[...] = jnp.concatenate([fin_e, fin_d], axis=1).astype(bf16)

    same = x == y
    mine = 2 * x + c
    for s in range(RS):
        dest = (r + s) & 7

        def send(dest=dest):
            remote(fin_s.at[dest], fin_r.at[mine], fs_s, fs_r.at[mine], (z * 4 + y, dest))

        if s:
            send()
        else:
            pl.when(jnp.logical_not(same))(send)

            @pl.when(same)
            def _():
                fin_r[mine] = fin_s[r]

    sums = []
    for cc in range(2):
        total = None
        for xs in range(4):
            slot = 2 * xs + cc

            @pl.when(jnp.logical_not(same & (mine == slot)))
            def _(slot=slot):
                wait_for(fin_r.at[slot], fs_r.at[slot])

    for cc in range(2):
        total = None
        for xs in range(4):
            term = fin_r[2 * xs + cc].astype(f32)
            total = term if total is None else total + term
        g_out[pl.ds(cc, 9, stride=2), :] = total[0:9]
        g_out[pl.ds(18 + cc, 3, stride=2), :] = total[9:12]
        g_out[24 + 3 * cc : 27 + 3 * cc, :] = total[12:15]
        g_out[30 + cc : 31 + cc, :] = total[15:16]
        for q in range(2):
            g_out[pl.ds(32 + 2 * cc + q, 9, stride=4), :] = total[16 + 9 * q : 25 + 9 * q]

    for h in halo + fhalo:
        h.wait_send()
    for i, send in enumerate((a1s, a2s, a3s, a4s)):
        wait_for(send.at[pl.ds(0, FR - 1)], as_.at[i])
    for i, (rc, ry) in enumerate(((rcD, ryD), (rc1, ry1), (rc2, ry2))):
        wait_for(rc, cs_s.at[i])
        wait_for(ry, ys_s.at[i])
    wait_for(rzD, zs_s.at[0])
    wait_for(rzE, zs_s.at[1])
    wait_for(fin_s.at[pl.ds(0, 7)], fs_s)
    pl.when(jnp.logical_not(same))(lambda: wait_for(fin_s.at[0], fs_s))


def per_device(frames_in, w_space, w_time, w_qkv, w_out, w_down, cotangent):
    def vb(*shape):
        return pltpu.VMEM(shape, bf16)

    def vf(*shape):
        return pltpu.VMEM(shape, f32)

    dma = pltpu.SemaphoreType.DMA
    scratch = [
        vb(2, 2, 64, C), vb(9 * C, C), vb(3 * C, C), vb(C, 3 * C), vb(C, C), vb(9 * C, 512), vb(2, 1, 32, 512),
        vb(2, 2, 64, C), vb(2, 1, 32, 512),
        vb(FR, 16, 128), vb(FR, 16, 128), vb(FR, 32, 128), vb(FR, 32, 128),
        vb(FR, 64, 128), vb(FR, 64, 128), vb(FR, 16, 128), vb(FR, 16, 128),
        vf(2, C, 128), vf(2, C, 128), vb(4, 64, C), vb(2, 64, C), vb(5, 64, C), vf(C, 128), vb(3, C, 512),
        vf(9 * C, 512), vf(3 * C, C), vf(C, 3 * C), vf(C, C), vf(9 * C, C),
    ]
    for rows in (144, 56, 72):
        n = 8 * rows
        scratch += [vb(2, 4, n, 128), vb(4, n, 128), vb(4, n, 128), vb(3, n, 128)]
        if rows == 144:
            scratch += [vb(8, 144, 128), vb(7, 144, 128)]
    scratch += [vb(8, 128, 128), vb(7, 128, 128), vb(8, 48, 128), vb(8, 48, 128)]
    scratch += [
        dma((7,)), dma((6,)), dma((6,)), dma((4,)), dma((4,)), dma((3,)), dma((3,)),
        dma((3,)), dma((9,)), dma((2,)), dma((14,)), dma, dma((8,)),
    ]
    anywhere = pl.BlockSpec(memory_space=pl.ANY)
    inside = pl.BlockSpec(memory_space=pltpu.VMEM)
    latent, grads = pl.pallas_call(
        kernel,
        out_shape=(jax.ShapeDtypeStruct((2, 1, 32, 512), bf16), jax.ShapeDtypeStruct((68, 128), f32)),
        in_specs=[anywhere] * 7,
        out_specs=(inside, inside),
        scratch_shapes=scratch,
        compiler_params=pltpu.CompilerParams(has_side_effects=True, vmem_limit_bytes=56 * 1024 * 1024),
        cost_estimate=pl.CostEstimate(flops=3 * 10**9, bytes_accessed=10**7, transcendentals=10**6),
    )(frames_in, w_space, w_time, w_qkv, w_out, w_down, cotangent)
    cuts = (0, 18, 24, 30, 32, 68)
    return (latent,) + tuple(grads[a:b].reshape(-1) for a, b in zip(cuts[:-1], cuts[1:]))


def solution(mesh):
    held = P("frame", "row", None, None)
    flat = P(("frame", "row"))
    return jax.shard_map(
        per_device,
        mesh=mesh,
        in_specs=(held, P(), P(), P(), P(), P(), held),
        out_specs=(held, flat, flat, flat, flat, flat),
        check_vma=False,
    )
```

```python
import math

import jax
import jax.numpy as jnp
from jax import lax
from jax.experimental import pallas as pl
from jax.experimental.pallas import tpu as pltpu
from jax.sharding import PartitionSpec as P

epsilon = 1e-06
f32 = jnp.float32
bf16 = jnp.bfloat16
MESH = pl.DeviceIdType.MESH
C = 256
FR, XS, ZS, YS, RS = 32, 4, 8, 4, 8


def nn(a, b):
    return jnp.dot(a, b, preferred_element_type=f32)


def nt(a, b):
    return lax.dot_general(a, b, (((1,), (1,)), ((), ())), preferred_element_type=f32)


def tn(a, b):
    return lax.dot_general(a, b, (((0,), (0,)), ((), ())), preferred_element_type=f32)


def inv_rms(v):
    return lax.rsqrt(jnp.mean(v * v, axis=-1, keepdims=True) + epsilon)


def sigmoid(n):
    return 1.0 / (1.0 + jnp.exp(-n))


def act(v):
    n = v * inv_rms(v)
    return n * sigmoid(n)


def rms_grad(normal, inv, upstream):
    return inv * (upstream - normal * jnp.mean(upstream * normal, axis=-1, keepdims=True))


def act_grad(v, upstream):
    inv = inv_rms(v)
    n = v * inv
    s = sigmoid(n)
    return rms_grad(n, inv, upstream * (s * (1.0 + n * (1.0 - s))))


def iota2(rows, cols):
    return (
        lax.broadcasted_iota(jnp.int32, (rows, cols), 0),
        lax.broadcasted_iota(jnp.int32, (rows, cols), 1),
    )


def one_at(hit):
    return jnp.where(hit, 1.0, 0.0).astype(bf16)


def row_shift(v, by):
    rows = v.shape[0]
    i = lax.broadcasted_iota(jnp.int32, v.shape, 0)
    moved = pltpu.roll(v, by % rows, axis=0)
    keep = i >= by if by > 0 else i < rows + by
    return jnp.where(keep, moved, 0.0)


def pack(m):
    m = m.reshape(FR, 8, C)
    return jnp.concatenate([m[:, :, :128], m[:, :, 128:]], axis=1)


def unpack(t):
    low = t[:, :8, :].reshape(C, 128)
    high = t[:, 8:16, :].reshape(C, 128)
    return jnp.concatenate([low, high], axis=1)


def put(ref, m):
    ref[0] = m[:, :128]
    ref[1] = m[:, 128:]


def every_fourth(ref, start):
    return jnp.concatenate([ref[u, pl.ds(start, 64, stride=4), :] for u in range(2)], axis=1)


def kernel(
    x_hbm, wsp_hbm, wt_hbm, wq_hbm, wo_hbm, wd_hbm, cot_hbm,
    lat_out, g_out,
    xv, wsp, wt, wq, wo, wd, cotv,
    halo_x, halo_c,
    a1s, a1r, a2s, a2r, a3s, a3r, a4s, a4r, hp,
    tmp, tmp2, fc, fcl, halo_f, cotc, at_,
    gd, gt, gq_, gp_, gs_,
    cD, rcD, yD, ryD, zD, rzD,
    c1, rc1, y1, ry1,
    c2, rc2, y2, ry2,
    zE, rzE,
    finD_s, finD_r, finE_s, finE_r,
    lsem, hs, hr, as_, ar, cs_s, cs_r, ys_s, ys_r, zs_s, zs_r, fs_s, fs_r,
):
    fr = lax.axis_index("frame")
    r = lax.axis_index("row")
    z, x = fr >> 2, fr & 3
    y, c = r >> 1, r & 1

    def remote(src, dst, ssem, rsem, dev):
        cp = pltpu.make_async_remote_copy(
            src_ref=src, dst_ref=dst, send_sem=ssem, recv_sem=rsem, device_id=dev, device_id_type=MESH
        )
        cp.start()
        return cp

    def wait_for(ref, sem):
        pltpu.make_async_copy(ref, ref, sem).wait()

    up, down = (r + RS - 1) & 7, (r + 1) & 7
    left, right = (fr + FR - 1) & (FR - 1), (fr + 1) & (FR - 1)
    last = (x * 4 + y, (4 + y) * 4 + x)
    own = (last[0] == fr, last[1] == fr)

    barrier = pltpu.get_barrier_semaphore()

    def tell(dev):
        pl.semaphore_signal(barrier, inc=1, device_id=dev, device_id_type=MESH)

    for dest in (up, down):
        tell((fr, dest))
    for s in range(2, RS - 1):
        tell((fr, (r + s) & 7))
    lax.fori_loop(1, FR, lambda s, carry: (tell(((fr + s) & (FR - 1), r)), carry)[1], 0)
    tell((left, up))
    low = z < 4
    src_x = jnp.where(low, z, x)
    src_y = jnp.where(low, x, z - 4)
    for s in range(ZS):
        for cc in range(2):
            source = ((((z + s) & 7) * 4 + src_x), 2 * src_y + (c ^ cc))
            if s or cc:
                tell(source)
            else:
                pl.when(jnp.logical_not(own[0] | own[1]))(lambda source=source: tell(source))
    loads = []
    for i, (src, dst) in enumerate(
        ((x_hbm, xv), (wsp_hbm, wsp), (cot_hbm, cotv), (wd_hbm, wd), (wt_hbm, wt), (wq_hbm, wq), (wo_hbm, wo))
    ):
        cp = pltpu.make_async_copy(src, dst, lsem.at[i])
        cp.start()
        loads.append(cp)

    def a2a_start(send, recv, i):
        def step(s, carry):
            k = (fr + s) & (FR - 1)
            remote(send.at[k], recv.at[fr], as_.at[i], ar.at[i], (k, r))
            return carry

        lax.fori_loop(1, FR, step, 0)
        recv[fr] = send[fr]

    def a2a_wait(recv, i):
        wait_for(recv.at[pl.ds(0, FR - 1)], ar.at[i])

    i256, j256 = iota2(C, C)
    k8, f8, h8, w8 = i256 >> 3, (i256 >> 2) & 1, (i256 >> 1) & 1, i256 & 1
    perm_cells = one_at(j256 == h8 * 128 + f8 * 64 + 2 * k8 + w8)
    loads[0].wait()
    xf = jnp.concatenate([xv[0, 0], xv[1, 0], xv[0, 1], xv[1, 1]], axis=0).astype(f32)
    first = act(xf).astype(bf16)
    loads[1].wait()

    def tap(a, b):
        return wsp[(3 * a + b) * C : (3 * a + b + 1) * C, :]

    parts = []
    for b in range(3):
        mid = nn(first, tap(1, b))
        other = jnp.concatenate([nn(first[128:], tap(2, b)), nn(first[:128], tap(0, b))], axis=0)
        parts.append(mid + other)
    pl.semaphore_wait(
        barrier, (FR - 1) + (RS - 1) + 1 + 2 * RS - jnp.where(own[0], 1, 0) - jnp.where(own[1], 1, 0)
    )
    halo = [
        remote(x_hbm.at[:, 1], halo_x.at[0], hs.at[0], hr.at[0], (fr, down)),
        remote(x_hbm.at[:, 0], halo_x.at[1], hs.at[1], hr.at[1], (fr, up)),
        remote(cot_hbm, halo_c, hs.at[2], hr.at[2], (fr, up)),
    ]
    halo[0].wait_recv()
    halo[1].wait_recv()
    top = act(jnp.concatenate([halo_x[0, 0], halo_x[0, 1]], axis=0).astype(f32))
    top = jnp.where(r > 0, top, 0.0).astype(bf16)
    bottom = act(jnp.concatenate([halo_x[1, 0], halo_x[1, 1]], axis=0).astype(f32))
    bottom = jnp.where(r < RS - 1, bottom, 0.0).astype(bf16)
    for b in range(3):
        parts[b] = parts[b] + jnp.concatenate([nn(top, tap(0, b)), nn(bottom, tap(2, b))], axis=0)
    col = i256 & 63
    spatial = xf + parts[1]
    spatial = spatial + jnp.where(col > 0, pltpu.roll(parts[0], 1, axis=0), 0.0)
    spatial = spatial + jnp.where(col < 63, pltpu.roll(parts[2], C - 1, axis=0), 0.0)
    a1s[...] = pack(nn(perm_cells, spatial.astype(bf16))).astype(bf16)
    a2a_start(a1s, a1r, 0)

    loads[2].wait()
    loads[3].wait()
    halo[2].wait_recv()
    cot_own = jnp.concatenate([cotv[0, 0], cotv[1, 0]], axis=0)
    below = jnp.concatenate([halo_c[0, 0], halo_c[1, 0]], axis=0)
    below = jnp.where(r < RS - 1, below.astype(f32), 0.0)
    jcol = lax.broadcasted_iota(jnp.int32, (64, 512), 0) & 31
    shifted = []
    for v in (cot_own.astype(f32), below):
        moved = jnp.where(jcol < 31, pltpu.roll(v, 63, axis=0), 0.0)
        shifted.append((v.astype(bf16), moved.astype(bf16)))
    taps_of = {0: ((1, 0),), 1: ((0, 1), (2, 0))}
    blocks = []
    for rp in range(2):
        for cp_ in range(2):
            total = None
            for a, rs in taps_of[rp]:
                for b, cs in taps_of[cp_]:
                    term = nt(shifted[rs][cs], wd[(3 * a + b) * C : (3 * a + b + 1) * C, :])
                    total = term if total is None else total + term
            blocks.append(total)
    gf = jnp.concatenate(blocks, axis=0).astype(bf16)
    perm_gf = one_at(j256 == h8 * 128 + w8 * 64 + f8 * 32 + k8)
    i512, j512 = iota2(512, C)
    u16 = i512 & 15
    f16, q16 = u16 >> 2, u16 & 3
    perm_cot = one_at((u16 < 8) & (j512 == q16 * 64 + f16 * 32 + (i512 >> 4)))
    cot_rows = jnp.concatenate([cot_own[:, 128 * q : 128 * q + 128] for q in range(4)], axis=0)
    cot_tiles = nn(perm_cot, cot_rows).reshape(FR, 16, 128)
    a2s[...] = jnp.concatenate([pack(nn(perm_gf, gf)), cot_tiles], axis=1).astype(bf16)
    a2a_start(a2s, a2r, 1)

    ip, jp = iota2(C, 128)
    wpos = 2 * (ip >> 3) - 1 + (ip & 3)
    perm_patch = one_at((wpos >= 0) & (wpos < 64) & (jp == ((ip >> 2) & 1) * 64 + wpos))
    rows_ext = (first[:128], first[128:])
    a3s[...] = jnp.concatenate([pack(nn(perm_patch, v)) for v in rows_ext], axis=1).astype(bf16)
    a2a_start(a3s, a3r, 2)

    for i in range(4, 7):
        loads[i].wait()
    a2a_wait(a1r, 0)
    sp = unpack(a1r[...].astype(f32))
    second = act(sp).astype(bf16)
    wtk = [wt[k * C : (k + 1) * C, :] for k in range(3)]
    temporal = sp + nn(second, wtk[2])
    temporal = temporal + row_shift(nn(second, wtk[1]), 4)
    temporal = temporal + row_shift(nn(second, wtk[0]), 8)
    temporal = temporal.astype(bf16).astype(f32)
    inv_t = inv_rms(temporal)
    norm_t = temporal * inv_t
    norm_b = norm_t.astype(bf16)

    proj = nn(norm_b, wq[...]).astype(bf16)
    query, key, value = proj[:, :C], proj[:, C : 2 * C], proj[:, 2 * C :]
    scale = 1.0 / math.sqrt(C)
    logits = nt(query, key) * scale
    allowed = ((i256 & 3) == (j256 & 3)) & (i256 >= j256)
    logits = jnp.where(allowed, logits, -1e30)
    exponent = jnp.exp(logits - jnp.max(logits, axis=-1, keepdims=True))
    weights = exponent / jnp.sum(exponent, axis=-1, keepdims=True)
    weights_b = weights.astype(bf16)
    mixed = nn(weights_b, value).astype(bf16)
    attended = nn(mixed, wo[...]).astype(bf16).astype(f32)
    residual = (temporal + attended).astype(bf16).astype(f32)
    fourth = act(residual)

    put(tmp, fourth)
    for cell in range(4):
        fc[cell] = every_fourth(tmp, cell).astype(bf16)
    fcl[0] = fc[1]
    fcl[1] = fc[3]
    fhalo = [
        remote(fc.at[pl.ds(2, 2)], halo_f.at[pl.ds(0, 2)], hs.at[3], hr.at[3], (fr, down)),
        remote(fcl, halo_f.at[pl.ds(2, 2)], hs.at[4], hr.at[4], (right, r)),
        remote(fc.at[3], halo_f.at[4], hs.at[5], hr.at[5], (right, down)),
    ]

    a2a_wait(a2r, 1)
    got = a2r[...].astype(f32)
    grad_res = act_grad(residual, unpack(got))
    grad_res_b = grad_res.astype(bf16)
    cotc[...] = got[:, 16:24, :].reshape(C, 128)
    cot_cell = jnp.concatenate(
        [cotc[pl.ds(q, 64, stride=4), :] for q in range(4)], axis=1
    ).astype(bf16)
    gp_[...] = tn(mixed, grad_res_b)
    grad_mixed = nt(grad_res_b, wo[...]).astype(bf16)

    a2a_wait(a3r, 2)
    phalo = [
        remote(a3r.at[:, pl.ds(16, 16)], hp.at[0], hs.at[6], hr.at[6], (fr, down)),
        remote(a3r.at[:, pl.ds(0, 16)], hp.at[1], hs.at[7], hr.at[7], (fr, up)),
    ]

    for h in fhalo:
        h.wait_recv()
    not_top, not_left = r > 0, fr > 0

    def masked(v, keep):
        return jnp.where(keep, v.astype(f32), 0.0).astype(bf16)

    taps_in = [
        masked(halo_f[4], not_top & not_left), masked(halo_f[0], not_top), masked(halo_f[1], not_top),
        masked(halo_f[2], not_left), fc[0], fc[1],
        masked(halo_f[3], not_left), fc[2], fc[3],
    ]
    for t in range(9):
        gd[t * C : (t + 1) * C, :] = tn(taps_in[t], cot_cell)

    def pack_rows(read, cbuf, rows):
        def step(p, carry):
            xd, zp = p >> 2, p & 3
            for cc in range(2):
                both = jnp.concatenate(
                    [read(8 * zp + xd, cc), read(8 * zp + 4 + xd, cc)], axis=0
                )
                at = pl.multiple_of((zp & 1) * (2 * rows), 16)
                cbuf[cc, zp >> 1, xd, pl.ds(at, 2 * rows), :] = both.astype(bf16)
            return carry

        lax.fori_loop(0, 16, step, 0)

    def read_d(block, cc):
        at = pl.multiple_of(block * 72, 8)
        return jnp.concatenate(
            [gd[pl.ds(at, 72), cc * 256 + q * 128 : cc * 256 + q * 128 + 128] for q in range(2)], axis=0
        )

    def read_1(block, cc):
        a24, a8 = pl.multiple_of(block * 24, 8), pl.multiple_of(block * 8, 8)
        pieces = [gt[pl.ds(a24, 24), cc * 128 : cc * 128 + 128]]
        pieces += [gq_[pl.ds(a8, 8), cc * 384 + m * 128 : cc * 384 + m * 128 + 128] for m in range(3)]
        pieces += [gp_[pl.ds(a8, 8), cc * 128 : cc * 128 + 128]]
        return jnp.concatenate(pieces, axis=0)

    def read_2(block, cc):
        at = pl.multiple_of(block * 72, 8)
        return gs_[pl.ds(at, 72), cc * 128 : cc * 128 + 128]

    def core_start(cbuf, rc, i):
        remote(cbuf.at[1 - c], rc, cs_s.at[i], cs_r.at[i], (fr, r ^ 1))

    places = (y, x)

    def along(axis, j):
        return (fr, 2 * j + c) if axis == 0 else (z * 4 + j, r)

    def first_start(cbuf, rc, ybuf, ry, i, rows):
        wait_for(rc, cs_r.at[i])
        for s in (1, 2, 3, 0):
            for h in range(2):
                j = (places[h] + s) & 3
                for p in range(2):
                    here = slice(2 * rows * p, 2 * rows * (p + 1))
                    total = cbuf[c, h, j, here, :].astype(f32) + rc[h, j, here, :].astype(f32)
                    ybuf[h, j, here, :] = total.astype(bf16)
                if s:
                    remote(
                        ybuf.at[h, j], ry.at[h, s - 1], ys_s.at[i], ys_r.at[6 * i + 3 * h + s - 1], along(h, j)
                    )

    def first_total(ybuf, ry, h, p, rows):
        here = slice(2 * rows * p, 2 * rows * (p + 1))
        total = ybuf[h, places[h], here, :].astype(f32)
        for s in range(3):
            total = total + ry[h, s, here, :].astype(f32)
        return total

    def first_wait(ry, i, h):
        for s in range(3):
            wait_for(ry.at[h, s], ys_r.at[6 * i + 3 * h + s])

    def second_start(zbuf, rz, i, h):
        for s in (1, 2, 3):
            j = (places[1 - h] + s) & 3
            remote(zbuf.at[h, j], rz.at[h, s - 1], zs_s.at[i], zs_r.at[6 * i + 3 * h + s - 1], along(1 - h, j))

    def second_total(zbuf, rz, i, h):
        total = zbuf[h, places[1 - h]].astype(f32)
        for s in range(3):
            wait_for(rz.at[h, s], zs_r.at[6 * i + 3 * h + s])
            total = total + rz[h, s].astype(f32)
        return total

    mine = 2 * z + c

    def last_start(fin_s, fin_r, i, h):
        for s in range(RS):
            dest = (r + s) & 7

            def send(dest=dest):
                remote(fin_s.at[h, dest], fin_r.at[mine], fs_s.at[i], fs_r.at[16 * i + mine], (last[h], dest))

            if s:
                send()
            else:
                pl.when(jnp.logical_not(own[h]))(send)

                @pl.when(own[h])
                def _():
                    fin_r[mine] = fin_s[h, r]

    def last_wait(fin_r, i):
        for slot in range(16):

            @pl.when(jnp.logical_not((own[0] | own[1]) & (mine == slot)))
            def _(slot=slot):
                wait_for(fin_r.at[slot], fs_r.at[16 * i + slot])

    pack_rows(read_d, cD, 144)
    core_start(cD, rcD, 0)

    grad_w = nt(grad_mixed, value)
    grad_s = (
        weights * (grad_w - jnp.sum(grad_w * weights, axis=-1, keepdims=True)) * scale
    ).astype(bf16)
    grad_v = tn(weights_b, grad_mixed).astype(bf16)
    grad_q = nn(grad_s, key).astype(bf16)
    grad_k = tn(grad_s, query).astype(bf16)
    grad_proj = jnp.concatenate([grad_q, grad_k, grad_v], axis=1)
    grad_n = nt(grad_proj, wq[...]).astype(bf16).astype(f32)
    gq_[...] = tn(norm_b, grad_proj)
    grad_t = grad_res + rms_grad(norm_t, inv_t, grad_n)
    grad_tb = grad_t.astype(bf16)
    grad_tb32 = grad_tb.astype(f32)

    first_start(cD, rcD, yD, ryD, 0, 144)

    grad_second = nt(grad_tb, wtk[2])
    grad_second = grad_second + row_shift(nt(grad_tb, wtk[1]), -4)
    grad_second = grad_second + row_shift(nt(grad_tb, wtk[0]), -8)
    gt[0:C, :] = tn(second, row_shift(grad_tb32, -8).astype(bf16))
    gt[C : 2 * C, :] = tn(second, row_shift(grad_tb32, -4).astype(bf16))
    gt[2 * C :, :] = tn(second, grad_tb)
    pack_rows(read_1, c1, 56)
    core_start(c1, rc1, 1)
    put(tmp, grad_t + act_grad(sp, grad_second))

    for h in phalo:
        h.wait_recv()
    rows_in = (
        masked(hp[0], not_top), a3r[:, 0:16, :], a3r[:, 16:32, :], masked(hp[1], r < RS - 1)
    )
    for hh in range(4):
        put(tmp2, unpack(rows_in[hh].astype(f32)))
        cells = [every_fourth(tmp2, ww) for ww in range(4)]
        for b in range(3):
            pair = jnp.concatenate([cells[b], cells[b + 1]], axis=0)
            at_[b, :, 128 * hh : 128 * hh + 128] = pair.T.astype(bf16)
    grad_sb = jnp.concatenate([every_fourth(tmp, cell) for cell in range(4)], axis=0).astype(bf16)
    for a in range(3):
        for b in range(3):
            gs_[(3 * a + b) * C : (3 * a + b + 1) * C, :] = nn(at_[b, :, 128 * a : 128 * a + 256], grad_sb)
    pack_rows(read_2, c2, 72)
    core_start(c2, rc2, 2)
    first_start(c1, rc1, y1, ry1, 1, 56)

    latent = None
    for t in range(9):
        term = nn(taps_in[t], wd[t * C : (t + 1) * C, :])
        latent = term if latent is None else latent + term
    latent = latent.astype(bf16)
    lat_rows = jnp.concatenate([latent[:, 128 * q : 128 * q + 128] for q in range(4)], axis=0)
    perm_lat = one_at((u16 < 8) & (j512 == q16 * 64 + 2 * (i512 >> 4) + f16))
    a4s[...] = nn(perm_lat, lat_rows).reshape(FR, 16, 128).astype(bf16)
    a2a_start(a4s, a4r, 3)

    first_start(c2, rc2, y2, ry2, 2, 72)
    for h in range(2):
        first_wait(ryD, 0, h)
        for p in range(2):
            total = first_total(yD, ryD, h, p, 144).astype(bf16)
            zD[h, 2 * p] = total[:144]
            zD[h, 2 * p + 1] = total[144:]
        second_start(zD, rzD, 0, h)

    a2a_wait(a4r, 3)
    cotc[...] = a4r[...].astype(f32)[:, :8, :].reshape(C, 128)
    for f in range(2):
        for q in range(4):
            lat_out[f, 0, :, 128 * q : 128 * q + 128] = cotc[pl.ds(4 * f + q, 32, stride=8), :].astype(bf16)

    d32, u32 = i256 >> 5, i256 & 31
    q32 = jnp.where(u32 >= 9, 1, 0)
    perm_d = one_at((u32 < 18) & (j256 == q32 * 72 + d32 * 9 + u32 - 9 * q32))
    ie, je = iota2(128, 128)
    de, ue = ie >> 4, ie & 15
    source = jnp.where(
        ue < 9, de * 9 + ue,
        jnp.where(ue < 12, 72 + de * 3 + ue - 9, jnp.where(ue < 15, 96 + (ue - 12) * 8 + de, 120 + de)),
    )
    perm_e = one_at(je == source)
    for h in range(2):
        total = second_total(zD, rzD, 0, h).astype(bf16)
        total = jnp.concatenate([total, jnp.zeros((112, 128), bf16)], axis=0)
        finD_s[h] = nn(perm_d, total).reshape(RS, 32, 128).astype(bf16)
        last_start(finD_s, finD_r, 0, h)

    for h in range(2):
        first_wait(ry1, 1, h)
        first_wait(ry2, 2, h)
        for p in range(2):
            t1 = first_total(y1, ry1, h, p, 56)
            t2 = first_total(y2, ry2, h, p, 72)
            zE[h, 2 * p] = jnp.concatenate([t2[:72], t1[:56]], axis=0).astype(bf16)
            zE[h, 2 * p + 1] = jnp.concatenate([t2[72:], t1[56:]], axis=0).astype(bf16)
        second_start(zE, rzE, 1, h)
    for h in range(2):
        total = second_total(zE, rzE, 1, h).astype(bf16)
        finE_s[h] = nn(perm_e, total).reshape(RS, 16, 128).astype(bf16)
        last_start(finE_s, finE_r, 1, h)

    def summed(fin_r, cc):
        total = fin_r[cc].astype(f32)
        for zs in range(1, ZS):
            total = total + fin_r[2 * zs + cc].astype(f32)
        return total

    last_wait(finD_r, 0)
    for cc in range(2):
        total = summed(finD_r, cc)
        for q in range(2):
            g_out[pl.ds(32 + 2 * cc + q, 9, stride=4), :] = total[9 * q : 9 + 9 * q]
    last_wait(finE_r, 1)
    for cc in range(2):
        total = summed(finE_r, cc)
        g_out[pl.ds(cc, 9, stride=2), :] = total[0:9]
        g_out[pl.ds(18 + cc, 3, stride=2), :] = total[9:12]
        g_out[24 + 3 * cc : 27 + 3 * cc, :] = total[12:15]
        g_out[30 + cc : 31 + cc, :] = total[15:16]

    for h in halo + fhalo + phalo:
        h.wait_send()
    for i, send in enumerate((a1s, a2s, a3s, a4s)):
        wait_for(send.at[pl.ds(0, FR - 1)], as_.at[i])
    for i, (rc, ry) in enumerate(((rcD, ryD), (rc1, ry1), (rc2, ry2))):
        wait_for(rc, cs_s.at[i])
        wait_for(ry, ys_s.at[i])
    wait_for(rzD, zs_s.at[0])
    wait_for(rzE, zs_s.at[1])
    for i, fin_s in enumerate((finD_s, finE_s)):
        for h in range(2):
            wait_for(fin_s.at[h, pl.ds(0, 7)], fs_s.at[i])
            pl.when(jnp.logical_not(own[h]))(lambda fin_s=fin_s, i=i, h=h: wait_for(fin_s.at[h, 0], fs_s.at[i]))


def outputs(lat, g, lat_out, *outs):
    lat_out[...] = lat[...]
    at = 0
    for out in outs:
        rows = out.shape[0]
        out[...] = g[at : at + rows, :]
        at += rows


def per_device(frames_in, w_space, w_time, w_qkv, w_out, w_down, cotangent):
    def vb(*shape):
        return pltpu.VMEM(shape, bf16)

    def vf(*shape):
        return pltpu.VMEM(shape, f32)

    dma = pltpu.SemaphoreType.DMA
    scratch = [
        vb(2, 2, 64, C), vb(9 * C, C), vb(3 * C, C), vb(C, 3 * C), vb(C, C), vb(9 * C, 512), vb(2, 1, 32, 512),
        vb(2, 2, 64, C), vb(2, 1, 32, 512),
        vb(FR, 16, 128), vb(FR, 16, 128), vb(FR, 32, 128), vb(FR, 32, 128),
        vb(FR, 32, 128), vb(FR, 32, 128), vb(FR, 16, 128), vb(FR, 16, 128), vb(2, FR, 16, 128),
        vf(2, C, 128), vf(2, C, 128), vb(4, 64, C), vb(2, 64, C), vb(5, 64, C), vf(C, 128), vb(3, C, 512),
        vf(9 * C, 512), vf(3 * C, C), vf(C, 3 * C), vf(C, C), vf(9 * C, C),
    ]
    for rows in (144, 56, 72):
        n = 4 * rows
        scratch += [vb(2, 2, 4, n, 128), vb(2, 4, n, 128), vb(2, 4, n, 128), vb(2, 3, n, 128)]
        if rows == 144:
            scratch += [vb(2, 4, 144, 128), vb(2, 3, 144, 128)]
    scratch += [vb(2, 4, 128, 128), vb(2, 3, 128, 128)]
    scratch += [vb(2, 8, 32, 128), vb(16, 32, 128), vb(2, 8, 16, 128), vb(16, 16, 128)]
    scratch += [
        dma((7,)), dma((8,)), dma((8,)), dma((4,)), dma((4,)), dma((3,)), dma((3,)),
        dma((3,)), dma((18,)), dma((2,)), dma((12,)), dma((2,)), dma((32,)),
    ]
    anywhere = pl.BlockSpec(memory_space=pl.ANY)
    inside = pl.BlockSpec(memory_space=pltpu.VMEM)
    latent, grads = pl.pallas_call(
        kernel,
        out_shape=(jax.ShapeDtypeStruct((2, 1, 32, 512), bf16), jax.ShapeDtypeStruct((68, 128), f32)),
        in_specs=[anywhere] * 7,
        out_specs=(inside, inside),
        scratch_shapes=scratch,
        compiler_params=pltpu.CompilerParams(has_side_effects=True, collective_id=0, vmem_limit_bytes=56 * 1024 * 1024),
        cost_estimate=pl.CostEstimate(flops=3 * 10**9, bytes_accessed=10**7, transcendentals=10**6),
    )(frames_in, w_space, w_time, w_qkv, w_out, w_down, cotangent)
    rows = (18, 6, 6, 2, 36)
    shapes = [latent.shape] + [(n, 128) for n in rows]
    results = pl.pallas_call(
        outputs,
        out_shape=[jax.ShapeDtypeStruct(v, f32 if i else bf16) for i, v in enumerate(shapes)],
        in_specs=[inside] * 2,
        out_specs=[inside] * 6,
    )(latent, grads)
    return (results[0],) + tuple(v.reshape(-1) for v in results[1:])


def solution(mesh):
    held = P("frame", "row", None, None)
    flat = P(("frame", "row"))
    return jax.shard_map(
        per_device,
        mesh=mesh,
        in_specs=(held, P(), P(), P(), P(), P(), held),
        out_specs=(held, flat, flat, flat, flat, flat),
        check_vma=False,
    )
```

```python
import math

import jax
import jax.numpy as jnp
from jax import lax
from jax.experimental import pallas as pl
from jax.experimental.pallas import tpu as pltpu
from jax.sharding import PartitionSpec as P

epsilon = 1e-06
f32 = jnp.float32
bf16 = jnp.bfloat16
MESH = pl.DeviceIdType.MESH
C = 256
FR, XS, ZS, YS, RS = 32, 4, 8, 4, 8


def nn(a, b):
    return jnp.dot(a, b, preferred_element_type=f32)


def nt(a, b):
    return lax.dot_general(a, b, (((1,), (1,)), ((), ())), preferred_element_type=f32)


def tn(a, b):
    return lax.dot_general(a, b, (((0,), (0,)), ((), ())), preferred_element_type=f32)


def inv_rms(v):
    return lax.rsqrt(jnp.mean(v * v, axis=-1, keepdims=True) + epsilon)


def sigmoid(n):
    return 1.0 / (1.0 + jnp.exp(-n))


def act(v):
    n = v * inv_rms(v)
    return n * sigmoid(n)


def rms_grad(normal, inv, upstream):
    return inv * (upstream - normal * jnp.mean(upstream * normal, axis=-1, keepdims=True))


def act_grad(v, upstream):
    inv = inv_rms(v)
    n = v * inv
    s = sigmoid(n)
    return rms_grad(n, inv, upstream * (s * (1.0 + n * (1.0 - s))))


def iota2(rows, cols):
    return (
        lax.broadcasted_iota(jnp.int32, (rows, cols), 0),
        lax.broadcasted_iota(jnp.int32, (rows, cols), 1),
    )


def one_at(hit):
    return jnp.where(hit, 1.0, 0.0).astype(bf16)


def frame_shift(v, by):
    frame = lax.broadcasted_iota(jnp.int32, v.shape, 0) & 63
    moved = pltpu.roll(v, by % v.shape[0], axis=0)
    keep = frame >= by if by > 0 else frame < 64 + by
    return jnp.where(keep, moved, 0.0)


def pack(m):
    m = m.reshape(FR, 8, C)
    return jnp.concatenate([m[:, :, :128], m[:, :, 128:]], axis=1)


def unpack(t):
    low = t[:, :8, :].reshape(C, 128)
    high = t[:, 8:16, :].reshape(C, 128)
    return jnp.concatenate([low, high], axis=1)


def put(ref, m):
    ref[0] = m[:, :128]
    ref[1] = m[:, 128:]


def every_fourth(ref, start):
    return jnp.concatenate([ref[u, pl.ds(start, 64, stride=4), :] for u in range(2)], axis=1)


def kernel(
    x_hbm, wsp_hbm, wt_hbm, wq_hbm, wo_hbm, wd_hbm, cot_hbm,
    lat_out, g_out,
    xv, wsp, wt, wq, wo, wd, cotv,
    halo_x,
    a1s, a1r, a2s, a2r, a3s, a3r, a4s, a4r,
    tmp, fc, fcl, halo_f, rows8, cc_, halo_c, patch, at_,
    gd, gt, gq_, gp_, gs_,
    cD, rcD, yD, ryD, zD, rzD,
    c1, rc1, y1, ry1,
    c2, rc2, y2, ry2,
    zE, rzE,
    finD_s, finD_r, finE_s, finE_r,
    lsem, hs, hr, as_, ar, cs_s, cs_r, ys_s, ys_r, zs_s, zs_r, fs_s, fs_r,
):
    fr = lax.axis_index("frame")
    r = lax.axis_index("row")
    z, x = fr >> 2, fr & 3
    y, c = r >> 1, r & 1

    def remote(src, dst, ssem, rsem, dev):
        cp = pltpu.make_async_remote_copy(
            src_ref=src, dst_ref=dst, send_sem=ssem, recv_sem=rsem, device_id=dev, device_id_type=MESH
        )
        cp.start()
        return cp

    def wait_for(ref, sem):
        pltpu.make_async_copy(ref, ref, sem).wait()

    up, down = (r + RS - 1) & 7, (r + 1) & 7
    left, right = (fr + FR - 1) & (FR - 1), (fr + 1) & (FR - 1)
    held = ((x - z) & 3, (y - z) & 3)
    last = (held[0] * 4 + y, (4 + held[1]) * 4 + x)
    own = (last[0] == fr, last[1] == fr)

    places = (y, x)

    barrier = pltpu.get_barrier_semaphore()

    def tell(dev):
        pl.semaphore_signal(barrier, inc=1, device_id=dev, device_id_type=MESH)

    for dest in (up, down):
        tell((fr, dest))
    for s in range(2, RS - 1):
        tell((fr, (r + s) & 7))
    lax.fori_loop(1, FR, lambda s, carry: (tell(((fr + s) & (FR - 1), r)), carry)[1], 0)
    for side in (left, right):
        for dest in (up, down):
            tell((side, dest))
    low = z < 4
    for s in range(ZS):
        zs = (z + s) & 7
        turn = (z + zs) & 3
        src_x = jnp.where(low, turn, x)
        src_y = jnp.where(low, x, turn)
        for cc in range(2):
            source = (zs * 4 + src_x, 2 * src_y + (c ^ cc))
            if s or cc:
                tell(source)
            else:
                pl.when(jnp.logical_not(own[0] | own[1]))(lambda source=source: tell(source))
    loads = []
    for i, (src, dst) in enumerate(
        ((cot_hbm, cotv), (x_hbm, xv), (wsp_hbm, wsp), (wd_hbm, wd), (wt_hbm, wt), (wq_hbm, wq), (wo_hbm, wo))
    ):
        cp = pltpu.make_async_copy(src, dst, lsem.at[i])
        cp.start()
        loads.append(cp)

    def a2a_start(send, recv, i):
        def step(s, carry):
            k = (fr + s) & (FR - 1)
            remote(send.at[k], recv.at[fr], as_.at[i], ar.at[i], (k, r))
            return carry

        lax.fori_loop(1, FR, step, 0)
        recv[fr] = send[fr]

    def a2a_wait(recv, i):
        wait_for(recv.at[pl.ds(0, FR - 1)], ar.at[i])

    i256, j256 = iota2(C, C)
    k8, f8, h8, w8 = i256 >> 3, (i256 >> 2) & 1, (i256 >> 1) & 1, i256 & 1
    perm_cells = one_at(j256 == h8 * 128 + f8 * 64 + 2 * k8 + w8)
    i512, j512 = iota2(512, C)
    u16 = i512 & 15
    f16, q16 = u16 >> 2, u16 & 3
    jcol = (i512 >> 4) + (u16 >> 3)
    perm_cot = one_at((jcol < 32) & (j512 == q16 * 64 + (f16 & 1) * 32 + jcol))
    loads[0].wait()
    cot_rows = jnp.concatenate(
        [cotv[f, 0, :, 128 * q : 128 * q + 128] for q in range(4) for f in range(2)], axis=0
    )
    a2s[...] = nn(perm_cot, cot_rows).reshape(FR, 16, 128).astype(bf16)

    loads[1].wait()
    xf = jnp.concatenate([xv[0, 0], xv[1, 0], xv[0, 1], xv[1, 1]], axis=0).astype(f32)
    first = act(xf).astype(bf16)
    a3s[...] = pack(nn(perm_cells, first)).astype(bf16)
    loads[2].wait()

    def tap(a, b):
        return wsp[(3 * a + b) * C : (3 * a + b + 1) * C, :]

    parts = []
    for b in range(3):
        mid = nn(first, tap(1, b))
        other = jnp.concatenate([nn(first[128:], tap(2, b)), nn(first[:128], tap(0, b))], axis=0)
        parts.append(mid + other)
    pl.semaphore_wait(
        barrier, (FR - 1) + (RS - 1) + 4 + 2 * RS - jnp.where(own[0], 1, 0) - jnp.where(own[1], 1, 0)
    )
    halo = [
        remote(x_hbm.at[:, 1], halo_x.at[0], hs.at[0], hr.at[0], (fr, down)),
        remote(x_hbm.at[:, 0], halo_x.at[1], hs.at[1], hr.at[1], (fr, up)),
    ]
    a2a_start(a2s, a2r, 1)
    halo[0].wait_recv()
    halo[1].wait_recv()
    top = act(jnp.concatenate([halo_x[0, 0], halo_x[0, 1]], axis=0).astype(f32))
    top = jnp.where(r > 0, top, 0.0).astype(bf16)
    bottom = act(jnp.concatenate([halo_x[1, 0], halo_x[1, 1]], axis=0).astype(f32))
    bottom = jnp.where(r < RS - 1, bottom, 0.0).astype(bf16)
    for b in range(3):
        parts[b] = parts[b] + jnp.concatenate([nn(top, tap(0, b)), nn(bottom, tap(2, b))], axis=0)
    col = i256 & 63
    spatial = xf + parts[1]
    spatial = spatial + jnp.where(col > 0, pltpu.roll(parts[0], 1, axis=0), 0.0)
    spatial = spatial + jnp.where(col < 63, pltpu.roll(parts[2], C - 1, axis=0), 0.0)
    a1s[...] = pack(nn(perm_cells, spatial.astype(bf16))).astype(bf16)
    a2a_start(a1s, a1r, 0)

    a2a_wait(a2r, 1)
    got = a2r[...].astype(f32)
    cots = []
    for u in range(2):
        rows8[...] = got[:, 8 * u : 8 * u + 8, :].reshape(C, 128)
        cots.append(
            jnp.concatenate([rows8[pl.ds(q, 64, stride=4), :] for q in range(4)], axis=1).astype(bf16)
        )
        cc_[u] = cots[u]
    cot_cell = cots[0]
    chalo = [remote(cc_, halo_c, hs.at[2], hr.at[2], (fr, up))]
    a2a_start(a3s, a3r, 2)
    not_top, not_left = r > 0, fr > 0
    not_bottom, not_right = r < RS - 1, fr < FR - 1

    def masked(v, keep):
        return jnp.where(keep, v.astype(f32), 0.0).astype(bf16)

    for i in range(3, 7):
        loads[i].wait()

    a2a_wait(a1r, 0)
    put(tmp, unpack(a1r[...].astype(f32)))
    sp = jnp.concatenate([every_fourth(tmp, cell) for cell in range(4)], axis=0)
    second = act(sp).astype(bf16)
    wtk = [wt[k * C : (k + 1) * C, :] for k in range(3)]
    temporal = sp + nn(second, wtk[2])
    temporal = temporal + frame_shift(nn(second, wtk[1]), 1)
    temporal = temporal + frame_shift(nn(second, wtk[0]), 2)
    temporal = temporal.astype(bf16).astype(f32)
    inv_t = inv_rms(temporal)
    norm_t = temporal * inv_t
    norm_b = norm_t.astype(bf16)

    proj = nn(norm_b, wq[...]).astype(bf16)
    query, key, value = proj[:, :C], proj[:, C : 2 * C], proj[:, 2 * C :]
    scale = 1.0 / math.sqrt(C)
    logits = nt(query, key) * scale
    allowed = ((i256 >> 6) == (j256 >> 6)) & (i256 >= j256)
    logits = jnp.where(allowed, logits, -1e30)
    exponent = jnp.exp(logits - jnp.max(logits, axis=-1, keepdims=True))
    weights = exponent / jnp.sum(exponent, axis=-1, keepdims=True)
    weights_b = weights.astype(bf16)
    mixed = nn(weights_b, value).astype(bf16)
    attended = nn(mixed, wo[...]).astype(bf16).astype(f32)
    residual = (temporal + attended).astype(bf16).astype(f32)
    fourth = act(residual)

    for cell in range(4):
        fc[cell] = fourth[64 * cell : 64 * cell + 64].astype(bf16)
    fcl[0] = fc[1]
    fcl[1] = fc[3]
    fhalo = [
        remote(fc.at[pl.ds(2, 2)], halo_f.at[pl.ds(0, 2)], hs.at[5], hr.at[5], (fr, down)),
        remote(fcl, halo_f.at[pl.ds(2, 2)], hs.at[6], hr.at[6], (right, r)),
        remote(fc.at[3], halo_f.at[4], hs.at[7], hr.at[7], (right, down)),
    ]

    for h in chalo:
        h.wait_recv()
    shifted = (
        tuple(cots),
        (masked(halo_c[0], not_bottom), masked(halo_c[1], not_bottom)),
    )
    taps_of = {0: ((1, 0),), 1: ((0, 1), (2, 0))}
    blocks = []
    for rp in range(2):
        for cp_ in range(2):
            total = None
            for a, rs in taps_of[rp]:
                for b, cs in taps_of[cp_]:
                    term = nt(shifted[rs][cs], wd[(3 * a + b) * C : (3 * a + b + 1) * C, :])
                    total = term if total is None else total + term
            blocks.append(total)
    grad_fourth = jnp.concatenate(blocks, axis=0)

    a2a_wait(a3r, 2)
    put(tmp, unpack(a3r[...].astype(f32)))
    for hh in range(2):
        for ww in range(2):
            patch[1 + hh, 1 + ww] = every_fourth(tmp, 2 * hh + ww).astype(bf16)
    two = pl.ds(1, 2)
    phalo = []
    for i, (src, dst, dev) in enumerate((
        ((2, two), (0, two), (fr, down)),
        ((1, two), (3, two), (fr, up)),
        ((two, 2), (two, 0), (right, r)),
        ((two, 1), (two, 3), (left, r)),
        ((2, 2), (0, 0), (right, down)),
        ((2, 1), (0, 3), (left, down)),
        ((1, 2), (3, 0), (right, up)),
        ((1, 1), (3, 3), (left, up)),
    )):
        phalo.append(remote(patch.at[src], patch.at[dst], hs.at[8 + i], hr.at[8 + i], dev))

    grad_res = act_grad(residual, grad_fourth)
    grad_res_b = grad_res.astype(bf16)
    gp_[...] = tn(mixed, grad_res_b)
    grad_mixed = nt(grad_res_b, wo[...]).astype(bf16)

    def pack_rows(read, cbuf, rows):
        def step(p, carry):
            xd, zp = p >> 2, p & 3
            for cc in range(2):
                both = jnp.concatenate(
                    [read(8 * zp + xd, cc), read(8 * zp + 4 + xd, cc)], axis=0
                )
                at = pl.multiple_of((zp & 1) * (2 * rows), 16)
                cbuf[cc, zp >> 1, xd, pl.ds(at, 2 * rows), :] = both.astype(bf16)
            return carry

        lax.fori_loop(0, 16, step, 0)

    def read_d(block, cc):
        at = pl.multiple_of(block * 72, 8)
        return jnp.concatenate(
            [gd[pl.ds(at, 72), cc * 256 + q * 128 : cc * 256 + q * 128 + 128] for q in range(2)], axis=0
        )

    def read_1(block, cc):
        a24, a8 = pl.multiple_of(block * 24, 8), pl.multiple_of(block * 8, 8)
        pieces = [gt[pl.ds(a24, 24), cc * 128 : cc * 128 + 128]]
        pieces += [gq_[pl.ds(a8, 8), cc * 384 + m * 128 : cc * 384 + m * 128 + 128] for m in range(3)]
        pieces += [gp_[pl.ds(a8, 8), cc * 128 : cc * 128 + 128]]
        return jnp.concatenate(pieces, axis=0)

    def read_2(block, cc):
        at = pl.multiple_of(block * 72, 8)
        return gs_[pl.ds(at, 72), cc * 128 : cc * 128 + 128]

    def core_start(cbuf, rc, i):
        for s in (1, 2, 3, 0):
            for h in range(2):
                j = (places[h] + s) & 3
                remote(cbuf.at[1 - c, h, j], rc.at[h, j], cs_s.at[i], cs_r.at[8 * i + 4 * h + s], (fr, r ^ 1))


    def along(axis, j):
        return (fr, 2 * j + c) if axis == 0 else (z * 4 + j, r)

    def first_start(cbuf, rc, ybuf, ry, i, rows):
        for s in (1, 2, 3, 0):
            for h in range(2):
                j = (places[h] + s) & 3
                wait_for(rc.at[h, j], cs_r.at[8 * i + 4 * h + s])
                for p in range(2):
                    here = slice(2 * rows * p, 2 * rows * (p + 1))
                    total = cbuf[c, h, j, here, :].astype(f32) + rc[h, j, here, :].astype(f32)
                    ybuf[h, j, here, :] = total.astype(bf16)
                if s:
                    remote(
                        ybuf.at[h, j], ry.at[h, s - 1], ys_s.at[i], ys_r.at[6 * i + 3 * h + s - 1], along(h, j)
                    )

    def first_total(ybuf, ry, h, p, rows):
        here = slice(2 * rows * p, 2 * rows * (p + 1))
        total = ybuf[h, places[h], here, :].astype(f32)
        for s in range(3):
            total = total + ry[h, s, here, :].astype(f32)
        return total

    def first_wait(ry, i, h):
        for s in range(3):
            wait_for(ry.at[h, s], ys_r.at[6 * i + 3 * h + s])

    def second_start(zbuf, rz, i, h):
        for s in (1, 2, 3):
            j = (places[1 - h] + s) & 3
            remote(zbuf.at[h, (j - z) & 3], rz.at[h, s - 1], zs_s.at[i], zs_r.at[6 * i + 3 * h + s - 1], along(1 - h, j))

    def second_total(zbuf, rz, i, h):
        total = zbuf[h, held[h]].astype(f32)
        for s in range(3):
            wait_for(rz.at[h, s], zs_r.at[6 * i + 3 * h + s])
            total = total + rz[h, s].astype(f32)
        return total

    mine = 2 * z + c

    def last_start(fin_s, fin_r, i, h):
        for s in range(RS):
            dest = (r + s) & 7

            def send(dest=dest):
                remote(fin_s.at[h, dest], fin_r.at[mine], fs_s.at[i], fs_r.at[16 * i + mine], (last[h], dest))

            if s:
                send()
            else:
                pl.when(jnp.logical_not(own[h]))(send)

                @pl.when(own[h])
                def _():
                    fin_r[mine] = fin_s[h, r]

    def last_wait(fin_r, i):
        for slot in range(16):

            @pl.when(jnp.logical_not((own[0] | own[1]) & (mine == slot)))
            def _(slot=slot):
                wait_for(fin_r.at[slot], fs_r.at[16 * i + slot])


    grad_w = nt(grad_mixed, value)
    grad_s = (
        weights * (grad_w - jnp.sum(grad_w * weights, axis=-1, keepdims=True)) * scale
    ).astype(bf16)
    grad_v = tn(weights_b, grad_mixed).astype(bf16)
    grad_q = nn(grad_s, key).astype(bf16)
    grad_k = tn(grad_s, query).astype(bf16)
    grad_proj = jnp.concatenate([grad_q, grad_k, grad_v], axis=1)
    grad_n = nt(grad_proj, wq[...]).astype(bf16).astype(f32)
    gq_[...] = tn(norm_b, grad_proj)
    grad_t = grad_res + rms_grad(norm_t, inv_t, grad_n)
    grad_tb = grad_t.astype(bf16)
    grad_tb32 = grad_tb.astype(f32)


    gt[0:C, :] = tn(second, frame_shift(grad_tb32, -2).astype(bf16))
    gt[C : 2 * C, :] = tn(second, frame_shift(grad_tb32, -1).astype(bf16))
    gt[2 * C :, :] = tn(second, grad_tb)
    pack_rows(read_1, c1, 56)
    core_start(c1, rc1, 1)

    for h in fhalo:
        h.wait_recv()
    taps_in = [
        masked(halo_f[4], not_top & not_left), masked(halo_f[0], not_top), masked(halo_f[1], not_top),
        masked(halo_f[2], not_left), fc[0], fc[1],
        masked(halo_f[3], not_left), fc[2], fc[3],
    ]
    for t in range(9):
        gd[t * C : (t + 1) * C, :] = tn(taps_in[t], cot_cell)

    pack_rows(read_d, cD, 144)
    core_start(cD, rcD, 0)
    first_start(c1, rc1, y1, ry1, 1, 56)

    grad_second = nt(grad_tb, wtk[2])
    grad_second = grad_second + frame_shift(nt(grad_tb, wtk[1]), -1)
    grad_second = grad_second + frame_shift(nt(grad_tb, wtk[0]), -2)
    grad_sb = (grad_t + act_grad(sp, grad_second)).astype(bf16)

    first_start(cD, rcD, yD, ryD, 0, 144)

    for h in phalo:
        h.wait_recv()
    keep_row = {0: not_top, 3: not_bottom}
    keep_col = {0: not_left, 3: not_right}
    for hh in range(4):
        cells = []
        for ww in range(4):
            v = patch[hh, ww].astype(f32)
            if hh in keep_row:
                v = jnp.where(keep_row[hh], v, 0.0)
            if ww in keep_col:
                v = jnp.where(keep_col[ww], v, 0.0)
            cells.append(v)
        for b in range(3):
            pair = jnp.concatenate([cells[b], cells[b + 1]], axis=0)
            at_[b, :, 128 * hh : 128 * hh + 128] = pair.T.astype(bf16)
    for a in range(3):
        for b in range(3):
            gs_[(3 * a + b) * C : (3 * a + b + 1) * C, :] = nn(at_[b, :, 128 * a : 128 * a + 256], grad_sb)
    pack_rows(read_2, c2, 72)
    core_start(c2, rc2, 2)

    latent = None
    for t in range(9):
        term = nn(taps_in[t], wd[t * C : (t + 1) * C, :])
        latent = term if latent is None else latent + term
    latent = latent.astype(bf16)
    lat_rows = jnp.concatenate([latent[:, 128 * q : 128 * q + 128] for q in range(4)], axis=0)
    perm_lat = one_at((u16 < 8) & (j512 == q16 * 64 + 2 * (i512 >> 4) + f16))
    a4s[...] = nn(perm_lat, lat_rows).reshape(FR, 16, 128).astype(bf16)
    a2a_start(a4s, a4r, 3)

    first_start(c2, rc2, y2, ry2, 2, 72)
    for h in range(2):
        first_wait(ryD, 0, h)
        for p in range(2):
            total = first_total(yD, ryD, h, p, 144).astype(bf16)
            zD[h, 2 * p] = total[:144]
            zD[h, 2 * p + 1] = total[144:]
        second_start(zD, rzD, 0, h)

    d32, u32 = i256 >> 5, i256 & 31
    q32 = jnp.where(u32 >= 9, 1, 0)
    perm_d = one_at((u32 < 18) & (j256 == q32 * 72 + d32 * 9 + u32 - 9 * q32))
    ie, je = iota2(128, 128)
    de, ue = ie >> 4, ie & 15
    source = jnp.where(
        ue < 9, de * 9 + ue,
        jnp.where(ue < 12, 72 + de * 3 + ue - 9, jnp.where(ue < 15, 96 + (ue - 12) * 8 + de, 120 + de)),
    )
    perm_e = one_at(je == source)
    for h in range(2):
        total = second_total(zD, rzD, 0, h).astype(bf16)
        total = jnp.concatenate([total, jnp.zeros((112, 128), bf16)], axis=0)
        finD_s[h] = nn(perm_d, total).reshape(RS, 32, 128).astype(bf16)
        last_start(finD_s, finD_r, 0, h)

    for h in range(2):
        first_wait(ry1, 1, h)
        first_wait(ry2, 2, h)
        for p in range(2):
            t1 = first_total(y1, ry1, h, p, 56)
            t2 = first_total(y2, ry2, h, p, 72)
            zE[h, 2 * p] = jnp.concatenate([t2[:72], t1[:56]], axis=0).astype(bf16)
            zE[h, 2 * p + 1] = jnp.concatenate([t2[72:], t1[56:]], axis=0).astype(bf16)
        second_start(zE, rzE, 1, h)
    for h in range(2):
        total = second_total(zE, rzE, 1, h).astype(bf16)
        finE_s[h] = nn(perm_e, total).reshape(RS, 16, 128).astype(bf16)
        last_start(finE_s, finE_r, 1, h)

    def summed(fin_r, cc):
        total = fin_r[cc].astype(f32)
        for zs in range(1, ZS):
            total = total + fin_r[2 * zs + cc].astype(f32)
        return total

    a2a_wait(a4r, 3)
    rows8[...] = a4r[...].astype(f32)[:, :8, :].reshape(C, 128)
    for f in range(2):
        for q in range(4):
            lat_out[f, 0, :, 128 * q : 128 * q + 128] = rows8[pl.ds(4 * f + q, 32, stride=8), :].astype(bf16)

    last_wait(finD_r, 0)
    for cc in range(2):
        total = summed(finD_r, cc)
        for q in range(2):
            g_out[pl.ds(32 + 2 * cc + q, 9, stride=4), :] = total[9 * q : 9 + 9 * q]
    last_wait(finE_r, 1)
    for cc in range(2):
        total = summed(finE_r, cc)
        g_out[pl.ds(cc, 9, stride=2), :] = total[0:9]
        g_out[pl.ds(18 + cc, 3, stride=2), :] = total[9:12]
        g_out[24 + 3 * cc : 27 + 3 * cc, :] = total[12:15]
        g_out[30 + cc : 31 + cc, :] = total[15:16]

    for h in halo + chalo + fhalo + phalo:
        h.wait_send()
    for i, send in enumerate((a1s, a2s, a3s, a4s)):
        wait_for(send.at[pl.ds(0, FR - 1)], as_.at[i])
    for i, (rc, ry) in enumerate(((rcD, ryD), (rc1, ry1), (rc2, ry2))):
        wait_for(rc, cs_s.at[i])
        wait_for(ry, ys_s.at[i])
    wait_for(rzD, zs_s.at[0])
    wait_for(rzE, zs_s.at[1])
    for i, fin_s in enumerate((finD_s, finE_s)):
        for h in range(2):
            wait_for(fin_s.at[h, pl.ds(0, 7)], fs_s.at[i])
            pl.when(jnp.logical_not(own[h]))(lambda fin_s=fin_s, i=i, h=h: wait_for(fin_s.at[h, 0], fs_s.at[i]))


def outputs(lat, g, lat_out, *outs):
    lat_out[...] = lat[...]
    at = 0
    for out in outs:
        rows = out.shape[0]
        out[...] = g[at : at + rows, :]
        at += rows


def per_device(frames_in, w_space, w_time, w_qkv, w_out, w_down, cotangent):
    def vb(*shape):
        return pltpu.VMEM(shape, bf16)

    def vf(*shape):
        return pltpu.VMEM(shape, f32)

    dma = pltpu.SemaphoreType.DMA
    scratch = [
        vb(2, 2, 64, C), vb(9 * C, C), vb(3 * C, C), vb(C, 3 * C), vb(C, C), vb(9 * C, 512), vb(2, 1, 32, 512),
        vb(2, 2, 64, C),
        vb(FR, 16, 128), vb(FR, 16, 128), vb(FR, 16, 128), vb(FR, 16, 128),
        vb(FR, 16, 128), vb(FR, 16, 128), vb(FR, 16, 128), vb(FR, 16, 128),
        vf(2, C, 128), vb(4, 64, C), vb(2, 64, C), vb(5, 64, C), vf(C, 128),
        vb(2, 64, 512), vb(2, 64, 512), vb(4, 4, 64, C), vb(3, C, 512),
        vf(9 * C, 512), vf(3 * C, C), vf(C, 3 * C), vf(C, C), vf(9 * C, C),
    ]
    for rows in (144, 56, 72):
        n = 4 * rows
        scratch += [vb(2, 2, 4, n, 128), vb(2, 4, n, 128), vb(2, 4, n, 128), vb(2, 3, n, 128)]
        if rows == 144:
            scratch += [vb(2, 4, 144, 128), vb(2, 3, 144, 128)]
    scratch += [vb(2, 4, 128, 128), vb(2, 3, 128, 128)]
    scratch += [vb(2, 8, 32, 128), vb(16, 32, 128), vb(2, 8, 16, 128), vb(16, 16, 128)]
    scratch += [
        dma((7,)), dma((16,)), dma((16,)), dma((4,)), dma((4,)), dma((3,)), dma((24,)),
        dma((3,)), dma((18,)), dma((2,)), dma((12,)), dma((2,)), dma((32,)),
    ]
    anywhere = pl.BlockSpec(memory_space=pl.ANY)
    inside = pl.BlockSpec(memory_space=pltpu.VMEM)
    latent, grads = pl.pallas_call(
        kernel,
        out_shape=(jax.ShapeDtypeStruct((2, 1, 32, 512), bf16), jax.ShapeDtypeStruct((68, 128), f32)),
        in_specs=[anywhere] * 7,
        out_specs=(inside, inside),
        scratch_shapes=scratch,
        compiler_params=pltpu.CompilerParams(has_side_effects=True, collective_id=0, vmem_limit_bytes=56 * 1024 * 1024),
        cost_estimate=pl.CostEstimate(flops=3 * 10**9, bytes_accessed=10**7, transcendentals=10**6),
    )(frames_in, w_space, w_time, w_qkv, w_out, w_down, cotangent)
    rows = (18, 6, 6, 2, 36)
    shapes = [latent.shape] + [(n, 128) for n in rows]
    results = pl.pallas_call(
        outputs,
        out_shape=[jax.ShapeDtypeStruct(v, f32 if i else bf16) for i, v in enumerate(shapes)],
        in_specs=[inside] * 2,
        out_specs=[inside] * 6,
    )(latent, grads)
    return (results[0],) + tuple(v.reshape(-1) for v in results[1:])


def solution(mesh):
    held = P("frame", "row", None, None)
    flat = P(("frame", "row"))
    return jax.shard_map(
        per_device,
        mesh=mesh,
        in_specs=(held, P(), P(), P(), P(), P(), held),
        out_specs=(held, flat, flat, flat, flat, flat),
        check_vma=False,
    )
```

```python
import math

import jax
import jax.numpy as jnp
from jax import lax
from jax.experimental import pallas as pl
from jax.experimental.pallas import tpu as pltpu
from jax.sharding import PartitionSpec as P

epsilon = 1e-06
f32 = jnp.float32
bf16 = jnp.bfloat16
MESH = pl.DeviceIdType.MESH
C = 256
FR, XS, ZS, YS, RS = 32, 4, 8, 4, 8


def nn(a, b):
    return jnp.dot(a, b, preferred_element_type=f32)


def nt(a, b):
    return lax.dot_general(a, b, (((1,), (1,)), ((), ())), preferred_element_type=f32)


def tn(a, b):
    return lax.dot_general(a, b, (((0,), (0,)), ((), ())), preferred_element_type=f32)


def inv_rms(v):
    return lax.rsqrt(jnp.mean(v * v, axis=-1, keepdims=True) + epsilon)


def sigmoid(n):
    return 1.0 / (1.0 + jnp.exp(-n))


def act(v):
    n = v * inv_rms(v)
    return n * sigmoid(n)


def rms_grad(normal, inv, upstream):
    return inv * (upstream - normal * jnp.mean(upstream * normal, axis=-1, keepdims=True))


def act_grad(v, upstream):
    inv = inv_rms(v)
    n = v * inv
    s = sigmoid(n)
    return rms_grad(n, inv, upstream * (s * (1.0 + n * (1.0 - s))))


def iota2(rows, cols):
    return (
        lax.broadcasted_iota(jnp.int32, (rows, cols), 0),
        lax.broadcasted_iota(jnp.int32, (rows, cols), 1),
    )


def one_at(hit):
    return jnp.where(hit, 1.0, 0.0).astype(bf16)


def frame_shift(v, by):
    frame = lax.broadcasted_iota(jnp.int32, v.shape, 0) & 63
    moved = pltpu.roll(v, by % v.shape[0], axis=0)
    keep = frame >= by if by > 0 else frame < 64 + by
    return jnp.where(keep, moved, 0.0)


def pack(m):
    m = m.reshape(FR, 8, C)
    return jnp.concatenate([m[:, :, :128], m[:, :, 128:]], axis=1)


def unpack(t):
    low = t[:, :8, :].reshape(C, 128)
    high = t[:, 8:16, :].reshape(C, 128)
    return jnp.concatenate([low, high], axis=1)


def put(ref, m):
    ref[0] = m[:, :128]
    ref[1] = m[:, 128:]


def every_fourth(ref, start):
    return jnp.concatenate([ref[u, pl.ds(start, 64, stride=4), :] for u in range(2)], axis=1)


def kernel(
    x_hbm, wsp_hbm, wt_hbm, wq_hbm, wo_hbm, wd_hbm, cot_hbm,
    lat_hbm, g_hbm,
    lat_out, g_out,
    xv, wsp, wt, wq, wo, wd, cotv,
    halo_x,
    a1s, a1r, a2s, a2r, a3s, a3r, a4s, a4r,
    tmp, fc, lrow_s, lrow_r, rows8, cc_, halo_c, hp, at_,
    gd, gt, gq_, gp_, gs_,
    cD, rcD, yD, rlD, ryD, zD, rzD,
    cT, rcT, zT, rzT, xT, rxT, finT_s, finT_r,
    c2, rc2, y2, ry2,
    zE, rzE,
    finD_s, finD_r, finE_s, finE_r,
    lsem, hs, hr, as_, ar, cs_s, cs_r, ys_s, ys_r, rl_r, zs_s, zs_r, fs_s, fs_r, t_s, t_r,
):
    fr = lax.axis_index("frame")
    r = lax.axis_index("row")
    z, x = fr >> 2, fr & 3
    y, c = r >> 1, r & 1

    def remote(src, dst, ssem, rsem, dev):
        cp = pltpu.make_async_remote_copy(
            src_ref=src, dst_ref=dst, send_sem=ssem, recv_sem=rsem, device_id=dev, device_id_type=MESH
        )
        cp.start()
        return cp

    def wait_for(ref, sem):
        pltpu.make_async_copy(ref, ref, sem).wait()

    up, down = (r + RS - 1) & 7, (r + 1) & 7
    turned = (y - z) & 3
    last = (turned * 4 + x, (4 + turned) * 4 + x)
    own = (last[0] == fr, last[1] == fr)

    places = (y, x)

    barrier = pltpu.get_barrier_semaphore()

    def tell(dev):
        pl.semaphore_signal(barrier, inc=1, device_id=dev, device_id_type=MESH)

    def far_first(n):
        t = n >> 2
        dz = 4 + (1 - 2 * (t & 1)) * ((t + 1) >> 1)
        return ((z + dz) & 7) * 4 + ((x + n + 1) & 3)

    lax.fori_loop(0, FR - 1, lambda n, carry: (tell((far_first(n), r)), carry)[1], 0)
    for dest in (up, down):
        tell((fr, dest))
    for s in range(2, RS - 1):
        tell((fr, (r + s) & 7))
    for s in range(ZS):
        zs = (z + s) & 7
        for cc in range(2):
            source = (zs * 4 + x, 2 * ((z + zs) & 3) + (c ^ cc))
            if s or cc:
                tell(source)
            else:
                pl.when(jnp.logical_not(own[0] | own[1]))(lambda source=source: tell(source))
    loads = []
    for i, (src, dst) in enumerate(
        ((cot_hbm, cotv), (x_hbm, xv), (wsp_hbm, wsp), (wd_hbm, wd), (wt_hbm, wt), (wq_hbm, wq), (wo_hbm, wo))
    ):
        cp = pltpu.make_async_copy(src, dst, lsem.at[i])
        cp.start()
        loads.append(cp)

    def a2a_start(send, recv, i):
        def step(n, carry):
            k = far_first(n)
            remote(send.at[k], recv.at[fr], as_.at[i], ar.at[i], (k, r))
            return carry

        lax.fori_loop(0, FR - 1, step, 0)
        recv[fr] = send[fr]

    def a2a_wait(recv, i):
        wait_for(recv.at[pl.ds(0, FR - 1)], ar.at[i])

    i256, j256 = iota2(C, C)
    k8, f8, h8, w8 = i256 >> 3, (i256 >> 2) & 1, (i256 >> 1) & 1, i256 & 1
    perm_cells = one_at(j256 == h8 * 128 + f8 * 64 + 2 * k8 + w8)
    i512, j512 = iota2(512, C)
    u16 = i512 & 15
    f16, q16 = u16 >> 2, u16 & 3
    jcol = (i512 >> 4) + (u16 >> 3)
    perm_cot = one_at((jcol < 32) & (j512 == q16 * 64 + (f16 & 1) * 32 + jcol))
    loads[0].wait()
    cot_rows = jnp.concatenate(
        [cotv[f, 0, :, 128 * q : 128 * q + 128] for q in range(4) for f in range(2)], axis=0
    )
    a2s[...] = nn(perm_cot, cot_rows).reshape(FR, 16, 128).astype(bf16)

    loads[1].wait()
    xf = jnp.concatenate([xv[0, 0], xv[1, 0], xv[0, 1], xv[1, 1]], axis=0).astype(f32)
    first = act(xf).astype(bf16)
    ip, jp = iota2(C, 128)
    wpos = 2 * (ip >> 3) - 1 + (ip & 3)
    perm_patch = one_at((wpos >= 0) & (wpos < 64) & (jp == ((ip >> 2) & 1) * 64 + wpos))
    a3s[0] = pack(nn(perm_patch, first[:128])).astype(bf16)
    a3s[1] = pack(nn(perm_patch, first[128:])).astype(bf16)
    loads[2].wait()

    def tap(a, b):
        return wsp[(3 * a + b) * C : (3 * a + b + 1) * C, :]

    parts = []
    for b in range(3):
        mid = nn(first, tap(1, b))
        other = jnp.concatenate([nn(first[128:], tap(2, b)), nn(first[:128], tap(0, b))], axis=0)
        parts.append(mid + other)
    pl.semaphore_wait(
        barrier, (FR - 1) + (RS - 1) + 2 * RS - jnp.where(own[0], 1, 0) - jnp.where(own[1], 1, 0)
    )
    halo = [
        remote(x_hbm.at[:, 1], halo_x.at[0], hs.at[0], hr.at[0], (fr, down)),
        remote(x_hbm.at[:, 0], halo_x.at[1], hs.at[1], hr.at[1], (fr, up)),
    ]
    a2a_start(a2s, a2r, 1)
    halo[0].wait_recv()
    halo[1].wait_recv()
    top = act(jnp.concatenate([halo_x[0, 0], halo_x[0, 1]], axis=0).astype(f32))
    top = jnp.where(r > 0, top, 0.0).astype(bf16)
    bottom = act(jnp.concatenate([halo_x[1, 0], halo_x[1, 1]], axis=0).astype(f32))
    bottom = jnp.where(r < RS - 1, bottom, 0.0).astype(bf16)
    for b in range(3):
        parts[b] = parts[b] + jnp.concatenate([nn(top, tap(0, b)), nn(bottom, tap(2, b))], axis=0)
    col = i256 & 63
    spatial = xf + parts[1]
    spatial = spatial + jnp.where(col > 0, pltpu.roll(parts[0], 1, axis=0), 0.0)
    spatial = spatial + jnp.where(col < 63, pltpu.roll(parts[2], C - 1, axis=0), 0.0)
    a1s[...] = pack(nn(perm_cells, spatial.astype(bf16))).astype(bf16)
    a2a_start(a1s, a1r, 0)
    a2a_start(a3s.at[0], a3r.at[0], 2)

    a2a_wait(a2r, 1)
    got = a2r[...].astype(f32)
    cots = []
    for u in range(2):
        rows8[...] = got[:, 8 * u : 8 * u + 8, :].reshape(C, 128)
        cots.append(
            jnp.concatenate([rows8[pl.ds(q, 64, stride=4), :] for q in range(4)], axis=1).astype(bf16)
        )
        cc_[u] = cots[u]
    cot_cell = cots[0]
    chalo = [remote(cc_, halo_c, hs.at[2], hr.at[2], (fr, up))]
    a2a_start(a3s.at[1], a3r.at[1], 4)
    not_top, not_left = r > 0, fr > 0
    not_bottom, not_right = r < RS - 1, fr < FR - 1

    def masked(v, keep):
        return jnp.where(keep, v.astype(f32), 0.0).astype(bf16)

    for i in range(3, 7):
        loads[i].wait()

    a2a_wait(a1r, 0)
    put(tmp, unpack(a1r[...].astype(f32)))
    sp = jnp.concatenate([every_fourth(tmp, cell) for cell in range(4)], axis=0)
    second = act(sp).astype(bf16)
    wtk = [wt[k * C : (k + 1) * C, :] for k in range(3)]
    temporal = sp + nn(second, wtk[2])
    temporal = temporal + frame_shift(nn(second, wtk[1]), 1)
    temporal = temporal + frame_shift(nn(second, wtk[0]), 2)
    temporal = temporal.astype(bf16).astype(f32)
    inv_t = inv_rms(temporal)
    norm_t = temporal * inv_t
    norm_b = norm_t.astype(bf16)

    proj = nn(norm_b, wq[...]).astype(bf16)
    query, key, value = proj[:, :C], proj[:, C : 2 * C], proj[:, 2 * C :]
    scale = 1.0 / math.sqrt(C)
    logits = nt(query, key) * scale
    allowed = ((i256 >> 6) == (j256 >> 6)) & (i256 >= j256)
    logits = jnp.where(allowed, logits, -1e30)
    exponent = jnp.exp(logits - jnp.max(logits, axis=-1, keepdims=True))
    weights = exponent / jnp.sum(exponent, axis=-1, keepdims=True)
    weights_b = weights.astype(bf16)
    mixed = nn(weights_b, value).astype(bf16)
    attended = nn(mixed, wo[...]).astype(bf16).astype(f32)
    residual = (temporal + attended).astype(bf16).astype(f32)
    fourth = act(residual)

    fourth_b = fourth.astype(bf16)
    for cell in range(4):
        fc[cell] = fourth_b[64 * cell : 64 * cell + 64]

    def pack_rows(read, cbuf, rows):
        def step(p, carry):
            s1, pair = p >> 1, p & 1
            at = pl.multiple_of(pair * (2 * rows), 16)
            pairs = ((s1 * 4 + 2 * pair, s1 * 4 + 2 * pair + 1), (16 + 8 * pair + s1, 20 + 8 * pair + s1))
            for h, (one, two) in enumerate(pairs):
                for cc in range(2):
                    both = jnp.concatenate([read(one, cc), read(two, cc)], axis=0)
                    cbuf[cc, h, s1, pl.ds(at, 2 * rows), :] = both.astype(bf16)
            return carry

        lax.fori_loop(0, 8, step, 0)

    def read_d(block, cc):
        at = pl.multiple_of(block * 72, 8)
        return jnp.concatenate(
            [gd[pl.ds(at, 72), cc * 256 + q * 128 : cc * 256 + q * 128 + 128] for q in range(2)], axis=0
        )

    def read_1(block, cc):
        a24, a8 = pl.multiple_of(block * 24, 8), pl.multiple_of(block * 8, 8)
        pieces = [gt[pl.ds(a24, 24), cc * 128 : cc * 128 + 128]]
        pieces += [gq_[pl.ds(a8, 8), cc * 384 + m * 128 : cc * 384 + m * 128 + 128] for m in range(3)]
        pieces += [gp_[pl.ds(a8, 8), cc * 128 : cc * 128 + 128]]
        return jnp.concatenate(pieces, axis=0)

    def read_2(block, cc):
        at = pl.multiple_of(block * 72, 8)
        return gs_[pl.ds(at, 72), cc * 128 : cc * 128 + 128]

    def part(axis, place):
        return (place - z) & 3 if axis == 0 else place

    def core_start(cbuf, rc, i):
        for s in (2, 1, 3, 0):
            for h in range(2):
                j = part(h, (places[h] + s) & 3)
                remote(cbuf.at[1 - c, h, j], rc.at[h, j], cs_s.at[i], cs_r.at[8 * i + 4 * h + s], (fr, r ^ 1))


    def along(axis, j):
        return (fr, 2 * j + c) if axis == 0 else (z * 4 + j, r)

    def pair_sum(cbuf, rc, h, s, p, rows):
        j = part(h, (places[h] + s) & 3)
        here = slice(2 * rows * p, 2 * rows * (p + 1))
        return cbuf[c, h, j, here, :].astype(f32) + rc[h, j, here, :].astype(f32)

    def core_wait(rc, i, s, h):
        j = part(h, (places[h] + s) & 3)
        wait_for(rc.at[h, j], cs_r.at[8 * i + 4 * h + s])

    def send_half(yb, ry, i, h, way, p, rows):
        half = pl.ds(2 * rows * p, 2 * rows)
        place = (places[h] + (1, 3)[way]) & 3
        remote(
            yb.at[h, way, half], ry.at[h, way, half], ys_s.at[i], ys_r.at[8 * i + 4 * h + 2 * way + p], along(h, place)
        )

    def first_start(cbuf, rc, yb, rl, i, rows, hs):
        for h in hs:
            core_wait(rc, i, 2, h)
            for p in range(2):
                half = slice(2 * rows * p, 2 * rows * (p + 1))
                yb[h, 2, half, :] = pair_sum(cbuf, rc, h, 2, p, rows).astype(bf16)
                place = (places[h] + (1, 3)[p]) & 3
                remote(
                    yb.at[h, 2, pl.ds(2 * rows * p, 2 * rows)], rl.at[h, p],
                    ys_s.at[i], rl_r.at[4 * i + 2 * h + p], along(h, place),
                )

    def first_halves(cbuf, rc, yb, ry, i, rows, hs):
        for way in range(2):
            for h in hs:
                p = 1 - way
                core_wait(rc, i, (1, 3)[way], h)
                half = slice(2 * rows * p, 2 * rows * (p + 1))
                yb[h, way, half, :] = pair_sum(cbuf, rc, h, (1, 3)[way], p, rows).astype(bf16)
                send_half(yb, ry, i, h, way, p, rows)

    def direct_start(cbuf, rc, yb, ry, i, rows):
        for s, slot in ((2, 2), (1, 0), (3, 1)):
            for h in range(2):
                core_wait(rc, i, s, h)
                for p in range(2):
                    half = slice(2 * rows * p, 2 * rows * (p + 1))
                    yb[h, slot, half, :] = pair_sum(cbuf, rc, h, s, p, rows).astype(bf16)
                place = (places[h] + s) & 3
                remote(yb.at[h, slot], ry.at[h, slot], ys_s.at[i], ys_r.at[8 * i + 4 * h + slot], along(h, place))

    def direct_wait(rc, ry, i, h):
        core_wait(rc, i, 0, h)
        for slot in range(3):
            wait_for(ry.at[h, slot], ys_r.at[8 * i + 4 * h + slot])

    def first_relay(cbuf, rc, yb, rl, ry, i, rows):
        for h in range(2):
            for way in range(2):
                wait_for(rl.at[h, way], rl_r.at[4 * i + 2 * h + way])
                half = slice(2 * rows * way, 2 * rows * (way + 1))
                total = pair_sum(cbuf, rc, h, (1, 3)[way], way, rows) + rl[h, way].astype(f32)
                yb[h, way, half, :] = total.astype(bf16)
                send_half(yb, ry, i, h, way, way, rows)

    def first_total(cbuf, rc, ry, h, p, rows):
        half = slice(2 * rows * p, 2 * rows * (p + 1))
        total = pair_sum(cbuf, rc, h, 0, p, rows)
        for way in range(ry.shape[1]):
            total = total + ry[h, way, half, :].astype(f32)
        return total

    def first_wait(rc, ry, i, h, rows):
        core_wait(rc, i, 0, h)
        for way in range(2):
            for p in range(2):
                half = pl.ds(2 * rows * p, 2 * rows)
                wait_for(ry.at[h, way, half], ys_r.at[8 * i + 4 * h + 2 * way + p])

    def second_start(zbuf, rz, i, h):
        for s in (1, 2, 3):
            j = (places[1 - h] + s) & 3
            remote(zbuf.at[h, part(1 - h, j)], rz.at[h, s - 1], zs_s.at[i], zs_r.at[6 * i + 3 * h + s - 1], along(1 - h, j))

    def second_total(zbuf, rz, i, h):
        total = zbuf[h, part(1 - h, places[1 - h])].astype(f32)
        for s in range(3):
            wait_for(rz.at[h, s], zs_r.at[6 * i + 3 * h + s])
            total = total + rz[h, s].astype(f32)
        return total

    mine = 2 * z + c

    def last_start(fin_s, fin_r, i, h):
        for s in range(RS):
            dest = (r + s) & 7

            def send(dest=dest):
                remote(fin_s.at[h, dest], fin_r.at[mine], fs_s.at[i], fs_r.at[i], (last[h], dest))

            if s:
                send()
            else:
                pl.when(jnp.logical_not(own[h]))(send)

                @pl.when(own[h])
                def _():
                    fin_r[mine] = fin_s[h, r]

    def last_wait(fin_r, i):
        @pl.when(own[0] | own[1])
        def _():
            wait_for(fin_r.at[pl.ds(0, 15)], fs_r.at[i])

        @pl.when(jnp.logical_not(own[0] | own[1]))
        def _():
            wait_for(fin_r, fs_r.at[i])

    def last_total(fin_r, cc):
        total = fin_r[cc].astype(f32)
        for zs in range(1, ZS):
            total = total + fin_r[2 * zs + cc].astype(f32)
        return total

    def t_pack():
        def step(p, carry):
            zd, pair = p >> 1, p & 1
            at = pl.multiple_of(pair * 112, 16)
            block = zd * 4 + 2 * pair
            for cc in range(2):
                both = jnp.concatenate([read_1(block, cc), read_1(block + 1, cc)], axis=0)
                cT[cc, zd, pl.ds(at, 112), :] = both.astype(bf16)
            return carry

        lax.fori_loop(0, 16, step, 0)
        for s in (4, 3, 5, 2, 6, 1, 7, 0):
            zd = (z + s) & 7
            remote(cT.at[1 - c, zd], rcT.at[zd], t_s.at[0], t_r.at[s], (fr, r ^ 1))

    def t_start():
        for s in (4, 3, 5, 2, 6, 1, 7):
            zd = (z + s) & 7
            wait_for(rcT.at[zd], t_r.at[s])
            zT[zd] = (cT[c, zd].astype(f32) + rcT[zd].astype(f32)).astype(bf16)
            remote(zT.at[zd], rzT.at[s - 1], t_s.at[1], t_r.at[7 + s], (zd * 4 + x, r))

    def t_second():
        wait_for(rcT.at[z], t_r.at[0])
        total = cT[c, z].astype(f32) + rcT[z].astype(f32)
        for s in range(1, ZS):
            wait_for(rzT.at[s - 1], t_r.at[7 + s])
            total = total + rzT[s - 1].astype(f32)
        gap = jnp.zeros((8, 128), f32)
        for j in range(XS):
            xT[j] = jnp.concatenate([total[56 * j : 56 * j + 56], gap], axis=0).astype(bf16)
        for s in (1, 2, 3):
            j = (x + s) & 3
            remote(xT.at[j], rxT.at[s - 1], t_s.at[2], t_r.at[14 + s], (z * 4 + j, r))

    def t_last():
        total = xT[x].astype(f32)
        for s in (1, 2, 3):
            wait_for(rxT.at[s - 1], t_r.at[14 + s])
            total = total + rxT[s - 1].astype(f32)
        total = jnp.concatenate([total.astype(bf16), jnp.zeros((64, 128), bf16)], axis=0)
        it, jt = iota2(128, 128)
        dt, ut = it >> 4, it & 15
        source = jnp.where(ut < 3, dt * 3 + ut, jnp.where(ut < 6, 24 + (ut - 3) * 8 + dt, 48 + dt))
        perm_t = one_at((ut < 7) & (jt == source))
        finT_s[...] = nn(perm_t, total).reshape(RS, 16, 128).astype(bf16)
        for s in range(1, RS):
            dest = (r + s) & 7
            remote(finT_s.at[dest], finT_r.at[r], t_s.at[3], t_r.at[17 + s], (fr, dest))
        finT_r[r] = finT_s[r]

    def t_finish():
        for s in range(1, RS):
            wait_for(finT_r.at[(r + RS - s) & 7], t_r.at[17 + s])
        for cc in range(2):
            total = finT_r[cc].astype(f32)
            for ys in range(1, YS):
                total = total + finT_r[2 * ys + cc].astype(f32)
            g_out[pl.ds(24 + cc, 3, stride=2), :] = total[0:3]
            g_out[32 + 3 * cc : 35 + 3 * cc, :] = total[3:6]
            g_out[40 + cc : 41 + cc, :] = total[6:7]

    for h in chalo:
        h.wait_recv()
    shifted = (
        tuple(cots),
        (masked(halo_c[0], not_bottom), masked(halo_c[1], not_bottom)),
    )
    cots_of = (
        (3, 1, 1), (2, 1, 0), (3, 1, 0),
        (1, 0, 1), (0, 0, 0), (1, 0, 0),
        (3, 0, 1), (2, 0, 0), (3, 0, 0),
    )
    for t, (cell, rs, cs) in enumerate(cots_of):
        gd[t * C : (t + 1) * C, :] = tn(fc[cell], shifted[rs][cs])

    pack_rows(read_d, cD, 144)
    core_start(cD, rcD, 0)

    perm_frames = one_at(j256 == (i256 & 3) * 64 + 2 * k8 + f8)
    a4s[...] = pack(nn(perm_frames, fourth_b)).astype(bf16)
    a2a_start(a4s, a4r, 3)

    taps_of = {0: ((1, 0),), 1: ((0, 1), (2, 0))}
    blocks = []
    for rp in range(2):
        for cp_ in range(2):
            total = None
            for a, rs in taps_of[rp]:
                for b, cs in taps_of[cp_]:
                    term = nt(shifted[rs][cs], wd[(3 * a + b) * C : (3 * a + b + 1) * C, :])
                    total = term if total is None else total + term
            blocks.append(total)
    grad_fourth = jnp.concatenate(blocks, axis=0)

    grad_res = act_grad(residual, grad_fourth)
    grad_res_b = grad_res.astype(bf16)
    gp_[...] = tn(mixed, grad_res_b)
    grad_mixed = nt(grad_res_b, wo[...]).astype(bf16)

    grad_w = nt(grad_mixed, value)
    grad_s = (
        weights * (grad_w - jnp.sum(grad_w * weights, axis=-1, keepdims=True)) * scale
    ).astype(bf16)
    grad_v = tn(weights_b, grad_mixed).astype(bf16)
    grad_q = nn(grad_s, key).astype(bf16)
    grad_k = tn(grad_s, query).astype(bf16)
    grad_proj = jnp.concatenate([grad_q, grad_k, grad_v], axis=1)
    grad_n = nt(grad_proj, wq[...]).astype(bf16).astype(f32)
    gq_[...] = tn(norm_b, grad_proj)
    grad_t = grad_res + rms_grad(norm_t, inv_t, grad_n)
    grad_tb = grad_t.astype(bf16)
    grad_tb32 = grad_tb.astype(f32)


    a2a_wait(a3r.at[0], 2)
    a2a_wait(a3r.at[1], 4)
    phalo = [
        remote(a3r.at[1], hp.at[0], hs.at[4], hr.at[4], (fr, down)),
        remote(a3r.at[0], hp.at[1], hs.at[5], hr.at[5], (fr, up)),
    ]
    first_start(cD, rcD, yD, rlD, 0, 144, (1,))

    gt[0:C, :] = tn(second, frame_shift(grad_tb32, -2).astype(bf16))
    gt[C : 2 * C, :] = tn(second, frame_shift(grad_tb32, -1).astype(bf16))
    gt[2 * C :, :] = tn(second, grad_tb)
    t_pack()

    grad_second = nt(grad_tb, wtk[2])
    grad_second = grad_second + frame_shift(nt(grad_tb, wtk[1]), -1)
    grad_second = grad_second + frame_shift(nt(grad_tb, wtk[0]), -2)
    grad_sb = (grad_t + act_grad(sp, grad_second)).astype(bf16)

    first_start(cD, rcD, yD, rlD, 0, 144, (0,))
    first_halves(cD, rcD, yD, ryD, 0, 144, (1,))
    t_start()
    first_halves(cD, rcD, yD, ryD, 0, 144, (0,))

    for h in phalo:
        h.wait_recv()
    rows_in = (masked(hp[0], not_top), a3r[0], a3r[1], masked(hp[1], not_bottom))
    for hh in range(4):
        put(tmp, unpack(rows_in[hh].astype(f32)))
        cells = [every_fourth(tmp, ww) for ww in range(4)]
        for b in range(3):
            pair = jnp.concatenate([cells[b], cells[b + 1]], axis=0)
            at_[b, :, 128 * hh : 128 * hh + 128] = pair.T.astype(bf16)
    for a in range(3):
        for b in range(3):
            gs_[(3 * a + b) * C : (3 * a + b + 1) * C, :] = nn(at_[b, :, 128 * a : 128 * a + 256], grad_sb)
    pack_rows(read_2, c2, 72)
    core_start(c2, rc2, 1)

    first_relay(cD, rcD, yD, rlD, ryD, 0, 144)
    direct_start(c2, rc2, y2, ry2, 1, 72)

    a2a_wait(a4r, 3)
    put(tmp, unpack(a4r[...].astype(f32)))
    first_col = lax.broadcasted_iota(jnp.int32, (32, C), 0) == 0
    cells_of = [
        [
            [
                jnp.concatenate(
                    [tmp[u, pl.ds(4 * f + 2 * hh + wp, 32, stride=8), :] for u in range(2)], axis=1
                ).astype(bf16)
                for wp in range(2)
            ]
            for hh in range(2)
        ]
        for f in range(2)
    ]
    for f in range(2):
        for wp in range(2):
            lrow_s[f, wp] = cells_of[f][1][wp]
    lhalo = remote(lrow_s, lrow_r, hs.at[3], hr.at[3], (fr, down))
    for h in range(2):
        first_wait(rcD, ryD, 0, h, 144)
        for p in range(2):
            total = first_total(cD, rcD, ryD, h, p, 144).astype(bf16)
            zD[h, 2 * p] = total[:144]
            zD[h, 2 * p + 1] = total[144:]
        second_start(zD, rzD, 0, h)
    lhalo.wait_recv()
    taps_in = []
    for a in range(3):
        here = [
            [masked(lrow_r[f, wp], not_top) if a == 0 else cells_of[f][a - 1][wp] for wp in range(2)]
            for f in range(2)
        ]
        for b in range(3):
            picked = [here[f][1 if b != 1 else 0].astype(f32) for f in range(2)]
            if b == 0:
                picked = [jnp.where(first_col, 0.0, pltpu.roll(v, 1, axis=0)) for v in picked]
            taps_in.append(jnp.concatenate(picked, axis=0).astype(bf16))
    latent = None
    for t in range(9):
        term = nn(taps_in[t], wd[t * C : (t + 1) * C, :])
        latent = term if latent is None else latent + term
    for f in range(2):
        lat_out[f, 0] = latent[32 * f : 32 * f + 32].astype(bf16)
    lat_copy = pltpu.make_async_copy(lat_out, lat_hbm, lsem.at[0])
    lat_copy.start()

    gap = jnp.zeros((8, 128), f32)
    for h in range(2):
        direct_wait(rc2, ry2, 1, h)
        for p in range(2):
            total = first_total(c2, rc2, ry2, h, p, 72)
            zE[h, 2 * p] = jnp.concatenate([total[:72], gap], axis=0).astype(bf16)
            zE[h, 2 * p + 1] = jnp.concatenate([total[72:], gap], axis=0).astype(bf16)
        second_start(zE, rzE, 1, h)
    t_second()

    it, jt = iota2(128, C)
    dt, ut = it >> 4, it & 15
    perm_d = one_at(jt == jnp.where(ut < 9, 0, 63) + dt * 9 + ut)
    perm_e = one_at((ut < 9) & (jt == dt * 9 + ut))
    perm_r = one_at((ut >= 9) & (ut < 11) & (jt == 70 + dt * 9 + ut))

    def widened(total, rows):
        return jnp.concatenate([total.astype(bf16), jnp.zeros((C - rows, 128), bf16)], axis=0)

    rest = []
    for h in range(2):
        total = widened(second_total(zD, rzD, 0, h), 144)
        finD_s[h] = nn(perm_d, total).reshape(RS, 16, 128).astype(bf16)
        last_start(finD_s, finD_r, 0, h)
        rest.append(nn(perm_r, total))
    for h in range(2):
        total = widened(second_total(zE, rzE, 1, h), 80)
        finE_s[h] = (nn(perm_e, total) + rest[h]).reshape(RS, 16, 128).astype(bf16)
        last_start(finE_s, finE_r, 1, h)
    t_last()

    last_wait(finD_r, 0)
    for cc in range(2):
        total = last_total(finD_r, cc)
        g_out[pl.ds(48 + 2 * cc, 9, stride=4), :] = total[0:9]
        g_out[pl.ds(49 + 2 * cc, 7, stride=4), :] = total[9:16]
    last_wait(finE_r, 1)
    for cc in range(2):
        total = last_total(finE_r, cc)
        g_out[pl.ds(cc, 9, stride=2), :] = total[0:9]
        g_out[pl.ds(77 + 2 * cc, 2, stride=4), :] = total[9:11]
    t_finish()
    g_copy = pltpu.make_async_copy(g_out, g_hbm, lsem.at[1])
    g_copy.start()

    for h in halo + chalo + phalo + [lhalo]:
        h.wait_send()
    for i, send in enumerate((a1s, a2s, a3s.at[0], a4s, a3s.at[1])):
        wait_for(send.at[pl.ds(0, FR - 1)], as_.at[i])
    for i, (rc, ry) in enumerate(((rcD, ryD), (rc2, ry2))):
        wait_for(rc, cs_s.at[i])
        wait_for(ry, ys_s.at[i])
    wait_for(rlD, ys_s.at[0])
    wait_for(rzD, zs_s.at[0])
    wait_for(rzE, zs_s.at[1])
    for i, fin_s in enumerate((finD_s, finE_s)):
        for h in range(2):
            wait_for(fin_s.at[h, pl.ds(0, 7)], fs_s.at[i])
            pl.when(jnp.logical_not(own[h]))(lambda fin_s=fin_s, i=i, h=h: wait_for(fin_s.at[h, 0], fs_s.at[i]))
    for i, ref in enumerate((rcT, rzT, rxT, finT_s.at[pl.ds(0, 7)])):
        wait_for(ref, t_s.at[i])
    lat_copy.wait()
    g_copy.wait()


starts = (0, 24, 32, 40, 48)


def outputs(lat, g, lat_out, *outs):
    lat_out[...] = lat[...]
    for at, out in zip(starts, outs):
        out[...] = g[at : at + out.shape[0], :]


def per_device(frames_in, w_space, w_time, w_qkv, w_out, w_down, cotangent):
    def vb(*shape):
        return pltpu.VMEM(shape, bf16)

    def vf(*shape):
        return pltpu.VMEM(shape, f32)

    dma = pltpu.SemaphoreType.DMA
    scratch = [
        vb(2, 1, 32, 512), vf(88, 128),
        vb(2, 2, 64, C), vb(9 * C, C), vb(3 * C, C), vb(C, 3 * C), vb(C, C), vb(9 * C, 512), vb(2, 1, 32, 512),
        vb(2, 2, 64, C),
        vb(FR, 16, 128), vb(FR, 16, 128), vb(FR, 16, 128), vb(FR, 16, 128),
        vb(2, FR, 16, 128), vb(2, FR, 16, 128), vb(FR, 16, 128), vb(FR, 16, 128),
        vf(2, C, 128), vb(4, 64, C), vb(2, 2, 32, C), vb(2, 2, 32, C), vf(C, 128),
        vb(2, 64, 512), vb(2, 64, 512), vb(2, FR, 16, 128), vb(3, C, 512),
        vf(9 * C, 512), vf(3 * C, C), vf(C, 3 * C), vf(C, C), vf(9 * C, C),
    ]
    for rows in (144, 72):
        n = 4 * rows
        scratch += [vb(2, 2, 4, n, 128), vb(2, 4, n, 128), vb(2, 3, n, 128)]
        if rows == 144:
            scratch += [vb(2, 2, n // 2, 128), vb(2, 2, n, 128), vb(2, 4, 144, 128), vb(2, 3, 144, 128)]
            scratch += [vb(2, 8, 224, 128), vb(8, 224, 128), vb(8, 224, 128), vb(7, 224, 128)]
            scratch += [vb(4, 64, 128), vb(3, 64, 128), vb(8, 16, 128), vb(8, 16, 128)]
        else:
            scratch += [vb(2, 3, n, 128)]
    scratch += [vb(2, 4, 80, 128), vb(2, 3, 80, 128)]
    scratch += [vb(2, 8, 16, 128), vb(16, 16, 128), vb(2, 8, 16, 128), vb(16, 16, 128)]
    scratch += [
        dma((7,)), dma((6,)), dma((6,)), dma((5,)), dma((5,)), dma((2,)), dma((16,)),
        dma((2,)), dma((16,)), dma((4,)), dma((2,)), dma((12,)), dma((2,)), dma((2,)),
        dma((4,)), dma((25,)),
    ]
    anywhere = pl.BlockSpec(memory_space=pl.ANY)
    inside = pl.BlockSpec(memory_space=pltpu.VMEM)
    latent, grads = pl.pallas_call(
        kernel,
        out_shape=(jax.ShapeDtypeStruct((2, 1, 32, 512), bf16), jax.ShapeDtypeStruct((88, 128), f32)),
        in_specs=[anywhere] * 7,
        out_specs=(anywhere, anywhere),
        scratch_shapes=scratch,
        compiler_params=pltpu.CompilerParams(has_side_effects=True, collective_id=0, vmem_limit_bytes=56 * 1024 * 1024),
        cost_estimate=pl.CostEstimate(flops=3 * 10**9, bytes_accessed=10**7, transcendentals=10**6),
    )(frames_in, w_space, w_time, w_qkv, w_out, w_down, cotangent)
    rows = (18, 6, 6, 2, 36)
    shapes = [latent.shape] + [(n, 128) for n in rows]
    results = pl.pallas_call(
        outputs,
        out_shape=[jax.ShapeDtypeStruct(v, f32 if i else bf16) for i, v in enumerate(shapes)],
        in_specs=[inside] * 2,
        out_specs=[inside] * 6,
    )(latent, grads)
    return (results[0],) + tuple(v.reshape(-1) for v in results[1:])


def solution(mesh):
    held = P("frame", "row", None, None)
    flat = P(("frame", "row"))
    return jax.shard_map(
        per_device,
        mesh=mesh,
        in_specs=(held, P(), P(), P(), P(), P(), held),
        out_specs=(held, flat, flat, flat, flat, flat),
        check_vma=False,
    )
```

```python
import math

import jax
import jax.numpy as jnp
from jax import lax
from jax.experimental import pallas as pl
from jax.experimental.pallas import tpu as pltpu
from jax.sharding import PartitionSpec as P

epsilon = 1e-06
f32 = jnp.float32
bf16 = jnp.bfloat16
MESH = pl.DeviceIdType.MESH
C = 256
FR, XS, ZS, YS, RS = 32, 4, 8, 4, 8


def nn(a, b):
    return jnp.dot(a, b, preferred_element_type=f32)


def nt(a, b):
    return lax.dot_general(a, b, (((1,), (1,)), ((), ())), preferred_element_type=f32)


def tn(a, b):
    return lax.dot_general(a, b, (((0,), (0,)), ((), ())), preferred_element_type=f32)


def inv_rms(v):
    return lax.rsqrt(jnp.mean(v * v, axis=-1, keepdims=True) + epsilon)


def sigmoid(n):
    return 1.0 / (1.0 + jnp.exp(-n))


def act(v):
    n = v * inv_rms(v)
    return n * sigmoid(n)


def rms_grad(normal, inv, upstream):
    return inv * (upstream - normal * jnp.mean(upstream * normal, axis=-1, keepdims=True))


def act_grad(v, upstream):
    inv = inv_rms(v)
    n = v * inv
    s = sigmoid(n)
    return rms_grad(n, inv, upstream * (s * (1.0 + n * (1.0 - s))))


def iota2(rows, cols):
    return (
        lax.broadcasted_iota(jnp.int32, (rows, cols), 0),
        lax.broadcasted_iota(jnp.int32, (rows, cols), 1),
    )


def one_at(hit):
    return jnp.where(hit, 1.0, 0.0).astype(bf16)


def frame_shift(v, by):
    frame = lax.broadcasted_iota(jnp.int32, v.shape, 0) & 63
    moved = pltpu.roll(v, by % v.shape[0], axis=0)
    keep = frame >= by if by > 0 else frame < 64 + by
    return jnp.where(keep, moved, 0.0)


def pack(m):
    m = m.reshape(FR, 8, C)
    return jnp.concatenate([m[:, :, :128], m[:, :, 128:]], axis=1)


def unpack(t):
    low = t[:, :8, :].reshape(C, 128)
    high = t[:, 8:16, :].reshape(C, 128)
    return jnp.concatenate([low, high], axis=1)


def put(ref, m):
    ref[0] = m[:, :128]
    ref[1] = m[:, 128:]


def every_fourth(ref, start):
    return jnp.concatenate([ref[u, pl.ds(start, 64, stride=4), :] for u in range(2)], axis=1)


def kernel(
    x_hbm, wsp_hbm, wt_hbm, wq_hbm, wo_hbm, wd_hbm, cot_hbm,
    lat_out, g_out,
    xv, wsp, wt, wq, wo, wd, cotv,
    halo_x,
    a1s, a1r, a2s, a2r, a3s, a3r, a4s, a4r,
    tmp, fc, lrow_s, lrow_r, rows8, cc_, halo_c, hp, at_,
    gd, gt, gq_, gp_, gs_,
    cD, rcD, yD, rlD, ryD, zD, rzD,
    cT, rcT, zT, rzT, xT, rxT, finT_s, finT_r,
    c2, rc2, y2, ry2,
    zE, rzE,
    finD_s, finD_r, finE_s, finE_r,
    lsem, sent, hr, ar, cs_r, ys_r, rl_r, zs_r, fs_r, t_r,
):
    fr = lax.axis_index("frame")
    r = lax.axis_index("row")
    z, x = fr >> 2, fr & 3
    y, c = r >> 1, r & 1

    def remote(src, dst, ssem, rsem, dev):
        cp = pltpu.make_async_remote_copy(
            src_ref=src, dst_ref=dst, send_sem=ssem, recv_sem=rsem, device_id=dev, device_id_type=MESH
        )
        cp.start()
        return cp

    def wait_for(ref, sem):
        pltpu.make_async_copy(ref, ref, sem).wait()

    up, down = (r + RS - 1) & 7, (r + 1) & 7
    turned = (y - z) & 3
    last = (turned * 4 + x, (4 + turned) * 4 + x)
    own = (last[0] == fr, last[1] == fr)

    places = (y, x)

    barrier = pltpu.get_barrier_semaphore()

    def tell(dev):
        pl.semaphore_signal(barrier, inc=1, device_id=dev, device_id_type=MESH)

    def far_first(n):
        t = n >> 2
        dz = 4 + (1 - 2 * (t & 1)) * ((t + 1) >> 1)
        return ((z + dz) & 7) * 4 + ((x + n + 1) & 3)

    lax.fori_loop(0, FR - 1, lambda n, carry: (tell((far_first(n), r)), carry)[1], 0)
    for dest in (up, down):
        tell((fr, dest))
    for s in range(2, RS - 1):
        tell((fr, (r + s) & 7))
    for s in range(ZS):
        zs = (z + s) & 7
        for cc in range(2):
            source = (zs * 4 + x, 2 * ((z + zs) & 3) + (c ^ cc))
            if s or cc:
                tell(source)
            else:
                pl.when(jnp.logical_not(own[0] | own[1]))(lambda source=source: tell(source))
    loads = []
    for i, (src, dst) in enumerate(
        ((cot_hbm, cotv), (x_hbm, xv), (wsp_hbm, wsp), (wd_hbm, wd), (wt_hbm, wt), (wq_hbm, wq), (wo_hbm, wo))
    ):
        cp = pltpu.make_async_copy(src, dst, lsem.at[i])
        cp.start()
        loads.append(cp)

    def a2a_start(send, recv, i):
        def step(n, carry):
            k = far_first(n)
            remote(send.at[k], recv.at[fr], sent, ar.at[i], (k, r))
            return carry

        lax.fori_loop(0, FR - 1, step, 0)
        recv[fr] = send[fr]

    def a2a_wait(recv, i):
        wait_for(recv.at[pl.ds(0, FR - 1)], ar.at[i])

    i256, j256 = iota2(C, C)
    k8, f8, h8, w8 = i256 >> 3, (i256 >> 2) & 1, (i256 >> 1) & 1, i256 & 1
    perm_cells = one_at(j256 == h8 * 128 + f8 * 64 + 2 * k8 + w8)
    i512, j512 = iota2(512, C)
    u16 = i512 & 15
    f16, q16 = u16 >> 2, u16 & 3
    jcol = (i512 >> 4) + (u16 >> 3)
    perm_cot = one_at((jcol < 32) & (j512 == q16 * 64 + (f16 & 1) * 32 + jcol))
    loads[0].wait()
    cot_rows = jnp.concatenate(
        [cotv[f, 0, :, 128 * q : 128 * q + 128] for q in range(4) for f in range(2)], axis=0
    )
    a2s[...] = nn(perm_cot, cot_rows).reshape(FR, 16, 128).astype(bf16)

    loads[1].wait()
    xf = jnp.concatenate([xv[0, 0], xv[1, 0], xv[0, 1], xv[1, 1]], axis=0).astype(f32)
    first = act(xf).astype(bf16)
    ip, jp = iota2(C, 128)
    wpos = 2 * (ip >> 3) - 1 + (ip & 3)
    perm_patch = one_at((wpos >= 0) & (wpos < 64) & (jp == ((ip >> 2) & 1) * 64 + wpos))
    a3s[0] = pack(nn(perm_patch, first[:128])).astype(bf16)
    a3s[1] = pack(nn(perm_patch, first[128:])).astype(bf16)
    loads[2].wait()

    def tap(a, b):
        return wsp[(3 * a + b) * C : (3 * a + b + 1) * C, :]

    parts = []
    for b in range(3):
        mid = nn(first, tap(1, b))
        other = jnp.concatenate([nn(first[128:], tap(2, b)), nn(first[:128], tap(0, b))], axis=0)
        parts.append(mid + other)
    pl.semaphore_wait(
        barrier, (FR - 1) + (RS - 1) + 2 * RS - jnp.where(own[0], 1, 0) - jnp.where(own[1], 1, 0)
    )
    halo = [
        remote(x_hbm.at[:, 1], halo_x.at[0], sent, hr.at[0], (fr, down)),
        remote(x_hbm.at[:, 0], halo_x.at[1], sent, hr.at[1], (fr, up)),
    ]
    a2a_start(a2s, a2r, 1)
    halo[0].wait_recv()
    halo[1].wait_recv()
    top = act(jnp.concatenate([halo_x[0, 0], halo_x[0, 1]], axis=0).astype(f32))
    top = jnp.where(r > 0, top, 0.0).astype(bf16)
    bottom = act(jnp.concatenate([halo_x[1, 0], halo_x[1, 1]], axis=0).astype(f32))
    bottom = jnp.where(r < RS - 1, bottom, 0.0).astype(bf16)
    for b in range(3):
        parts[b] = parts[b] + jnp.concatenate([nn(top, tap(0, b)), nn(bottom, tap(2, b))], axis=0)
    col = i256 & 63
    spatial = xf + parts[1]
    spatial = spatial + jnp.where(col > 0, pltpu.roll(parts[0], 1, axis=0), 0.0)
    spatial = spatial + jnp.where(col < 63, pltpu.roll(parts[2], C - 1, axis=0), 0.0)
    a1s[...] = pack(nn(perm_cells, spatial.astype(bf16))).astype(bf16)
    a2a_start(a1s, a1r, 0)
    a2a_start(a3s.at[0], a3r.at[0], 2)

    a2a_wait(a2r, 1)
    got = a2r[...].astype(f32)
    cots = []
    for u in range(2):
        rows8[...] = got[:, 8 * u : 8 * u + 8, :].reshape(C, 128)
        cots.append(
            jnp.concatenate([rows8[pl.ds(q, 64, stride=4), :] for q in range(4)], axis=1).astype(bf16)
        )
        cc_[u] = cots[u]
    cot_cell = cots[0]
    chalo = [remote(cc_, halo_c, sent, hr.at[2], (fr, up))]
    a2a_start(a3s.at[1], a3r.at[1], 4)
    not_top, not_left = r > 0, fr > 0
    not_bottom, not_right = r < RS - 1, fr < FR - 1

    def masked(v, keep):
        return jnp.where(keep, v.astype(f32), 0.0).astype(bf16)

    for i in range(3, 7):
        loads[i].wait()

    a2a_wait(a1r, 0)
    put(tmp, unpack(a1r[...].astype(f32)))
    sp = jnp.concatenate([every_fourth(tmp, cell) for cell in range(4)], axis=0)
    second = act(sp).astype(bf16)
    wtk = [wt[k * C : (k + 1) * C, :] for k in range(3)]
    temporal = sp + nn(second, wtk[2])
    temporal = temporal + frame_shift(nn(second, wtk[1]), 1)
    temporal = temporal + frame_shift(nn(second, wtk[0]), 2)
    temporal = temporal.astype(bf16).astype(f32)
    inv_t = inv_rms(temporal)
    norm_t = temporal * inv_t
    norm_b = norm_t.astype(bf16)

    proj = nn(norm_b, wq[...]).astype(bf16)
    query, key, value = proj[:, :C], proj[:, C : 2 * C], proj[:, 2 * C :]
    scale = 1.0 / math.sqrt(C)
    logits = nt(query, key) * scale
    allowed = ((i256 >> 6) == (j256 >> 6)) & (i256 >= j256)
    logits = jnp.where(allowed, logits, -1e30)
    exponent = jnp.exp(logits - jnp.max(logits, axis=-1, keepdims=True))
    weights = exponent / jnp.sum(exponent, axis=-1, keepdims=True)
    weights_b = weights.astype(bf16)
    mixed = nn(weights_b, value).astype(bf16)
    attended = nn(mixed, wo[...]).astype(bf16).astype(f32)
    residual = (temporal + attended).astype(bf16).astype(f32)
    fourth = act(residual)

    fourth_b = fourth.astype(bf16)
    for cell in range(4):
        fc[cell] = fourth_b[64 * cell : 64 * cell + 64]

    def pack_rows(read, cbuf, rows):
        def step(p, carry):
            s1, pair = p >> 1, p & 1
            at = pl.multiple_of(pair * (2 * rows), 16)
            pairs = ((s1 * 4 + 2 * pair, s1 * 4 + 2 * pair + 1), (16 + 8 * pair + s1, 20 + 8 * pair + s1))
            for h, (one, two) in enumerate(pairs):
                for cc in range(2):
                    both = jnp.concatenate([read(one, cc), read(two, cc)], axis=0)
                    cbuf[cc, h, s1, pl.ds(at, 2 * rows), :] = both.astype(bf16)
            return carry

        lax.fori_loop(0, 8, step, 0)

    def read_d(block, cc):
        at = pl.multiple_of(block * 72, 8)
        return jnp.concatenate(
            [gd[pl.ds(at, 72), cc * 256 + q * 128 : cc * 256 + q * 128 + 128] for q in range(2)], axis=0
        )

    def read_1(block, cc):
        a24, a8 = pl.multiple_of(block * 24, 8), pl.multiple_of(block * 8, 8)
        pieces = [gt[pl.ds(a24, 24), cc * 128 : cc * 128 + 128]]
        pieces += [gq_[pl.ds(a8, 8), cc * 384 + m * 128 : cc * 384 + m * 128 + 128] for m in range(3)]
        pieces += [gp_[pl.ds(a8, 8), cc * 128 : cc * 128 + 128]]
        return jnp.concatenate(pieces, axis=0)

    def read_2(block, cc):
        at = pl.multiple_of(block * 72, 8)
        return gs_[pl.ds(at, 72), cc * 128 : cc * 128 + 128]

    def part(axis, place):
        return (place - z) & 3 if axis == 0 else place

    def core_start(cbuf, rc, i):
        for s in (2, 1, 3, 0):
            for h in range(2):
                j = part(h, (places[h] + s) & 3)
                remote(cbuf.at[1 - c, h, j], rc.at[h, j], sent, cs_r.at[8 * i + 4 * h + s], (fr, r ^ 1))


    def along(axis, j):
        return (fr, 2 * j + c) if axis == 0 else (z * 4 + j, r)

    def pair_sum(cbuf, rc, h, s, p, rows):
        j = part(h, (places[h] + s) & 3)
        here = slice(2 * rows * p, 2 * rows * (p + 1))
        return cbuf[c, h, j, here, :].astype(f32) + rc[h, j, here, :].astype(f32)

    def core_wait(rc, i, s, h):
        j = part(h, (places[h] + s) & 3)
        wait_for(rc.at[h, j], cs_r.at[8 * i + 4 * h + s])

    def send_half(yb, ry, i, h, way, p, rows):
        half = pl.ds(2 * rows * p, 2 * rows)
        place = (places[h] + (1, 3)[way]) & 3
        remote(
            yb.at[h, way, half], ry.at[h, way, half], sent, ys_r.at[2 * i + h], along(h, place)
        )

    def first_start(cbuf, rc, yb, rl, i, rows, hs):
        for h in hs:
            core_wait(rc, i, 2, h)
            for p in range(2):
                half = slice(2 * rows * p, 2 * rows * (p + 1))
                yb[h, 2, half, :] = pair_sum(cbuf, rc, h, 2, p, rows).astype(bf16)
                place = (places[h] + (1, 3)[p]) & 3
                remote(
                    yb.at[h, 2, pl.ds(2 * rows * p, 2 * rows)], rl.at[h, p],
                    sent, rl_r.at[4 * i + 2 * h + p], along(h, place),
                )

    def first_halves(cbuf, rc, yb, ry, i, rows, hs):
        for way in range(2):
            for h in hs:
                p = 1 - way
                core_wait(rc, i, (1, 3)[way], h)
                half = slice(2 * rows * p, 2 * rows * (p + 1))
                yb[h, way, half, :] = pair_sum(cbuf, rc, h, (1, 3)[way], p, rows).astype(bf16)
                send_half(yb, ry, i, h, way, p, rows)

    def direct_start(cbuf, rc, yb, ry, i, rows):
        for s, slot in ((2, 2), (1, 0), (3, 1)):
            for h in range(2):
                core_wait(rc, i, s, h)
                for p in range(2):
                    half = slice(2 * rows * p, 2 * rows * (p + 1))
                    yb[h, slot, half, :] = pair_sum(cbuf, rc, h, s, p, rows).astype(bf16)
                place = (places[h] + s) & 3
                remote(yb.at[h, slot], ry.at[h, slot], sent, ys_r.at[2 * i + h], along(h, place))

    def direct_wait(rc, ry, i, h):
        core_wait(rc, i, 0, h)
        wait_for(ry.at[h], ys_r.at[2 * i + h])

    def first_relay(cbuf, rc, yb, rl, ry, i, rows):
        for h in range(2):
            for way in range(2):
                wait_for(rl.at[h, way], rl_r.at[4 * i + 2 * h + way])
                half = slice(2 * rows * way, 2 * rows * (way + 1))
                total = pair_sum(cbuf, rc, h, (1, 3)[way], way, rows) + rl[h, way].astype(f32)
                yb[h, way, half, :] = total.astype(bf16)
                send_half(yb, ry, i, h, way, way, rows)

    def first_total(cbuf, rc, ry, h, p, rows):
        half = slice(2 * rows * p, 2 * rows * (p + 1))
        total = pair_sum(cbuf, rc, h, 0, p, rows)
        for way in range(ry.shape[1]):
            total = total + ry[h, way, half, :].astype(f32)
        return total

    def first_wait(rc, ry, i, h, rows):
        core_wait(rc, i, 0, h)
        wait_for(ry.at[h], ys_r.at[2 * i + h])

    def second_start(zbuf, rz, i, h):
        for s in (1, 2, 3):
            j = (places[1 - h] + s) & 3
            remote(zbuf.at[h, part(1 - h, j)], rz.at[h, s - 1], sent, zs_r.at[2 * i + h], along(1 - h, j))

    def second_total(zbuf, rz, i, h):
        total = zbuf[h, part(1 - h, places[1 - h])].astype(f32)
        wait_for(rz.at[h], zs_r.at[2 * i + h])
        for s in range(3):
            total = total + rz[h, s].astype(f32)
        return total

    mine = 2 * z + c

    def last_start(fin_s, fin_r, i, h):
        for s in range(RS):
            dest = (r + s) & 7

            def send(dest=dest):
                remote(fin_s.at[h, dest], fin_r.at[mine], sent, fs_r.at[i], (last[h], dest))

            if s:
                send()
            else:
                pl.when(jnp.logical_not(own[h]))(send)

                @pl.when(own[h])
                def _():
                    fin_r[mine] = fin_s[h, r]

    def last_wait(fin_r, i):
        @pl.when(own[0] | own[1])
        def _():
            wait_for(fin_r.at[pl.ds(0, 15)], fs_r.at[i])

        @pl.when(jnp.logical_not(own[0] | own[1]))
        def _():
            wait_for(fin_r, fs_r.at[i])

    def last_total(fin_r, cc):
        total = fin_r[cc].astype(f32)
        for zs in range(1, ZS):
            total = total + fin_r[2 * zs + cc].astype(f32)
        return total

    def t_pack():
        def step(p, carry):
            zd, pair = p >> 1, p & 1
            at = pl.multiple_of(pair * 112, 16)
            block = zd * 4 + 2 * pair
            for cc in range(2):
                both = jnp.concatenate([read_1(block, cc), read_1(block + 1, cc)], axis=0)
                cT[cc, zd, pl.ds(at, 112), :] = both.astype(bf16)
            return carry

        lax.fori_loop(0, 16, step, 0)
        for s in (4, 3, 5, 2, 6, 1, 7, 0):
            zd = (z + s) & 7
            remote(cT.at[1 - c, zd], rcT.at[zd], sent, t_r.at[s], (fr, r ^ 1))

    def t_start():
        for s in (4, 3, 5, 2, 6, 1, 7):
            zd = (z + s) & 7
            wait_for(rcT.at[zd], t_r.at[s])
            zT[zd] = (cT[c, zd].astype(f32) + rcT[zd].astype(f32)).astype(bf16)
            remote(zT.at[zd], rzT.at[s - 1], sent, t_r.at[8], (zd * 4 + x, r))

    def t_second():
        wait_for(rcT.at[z], t_r.at[0])
        total = cT[c, z].astype(f32) + rcT[z].astype(f32)
        wait_for(rzT, t_r.at[8])
        for s in range(1, ZS):
            total = total + rzT[s - 1].astype(f32)
        gap = jnp.zeros((8, 128), f32)
        for j in range(XS):
            xT[j] = jnp.concatenate([total[56 * j : 56 * j + 56], gap], axis=0).astype(bf16)
        for s in (1, 2, 3):
            j = (x + s) & 3
            remote(xT.at[j], rxT.at[s - 1], sent, t_r.at[9], (z * 4 + j, r))

    def t_last():
        total = xT[x].astype(f32)
        wait_for(rxT, t_r.at[9])
        for s in (1, 2, 3):
            total = total + rxT[s - 1].astype(f32)
        total = jnp.concatenate([total.astype(bf16), jnp.zeros((64, 128), bf16)], axis=0)
        it, jt = iota2(128, 128)
        dt, ut = it >> 4, it & 15
        source = jnp.where(ut < 3, dt * 3 + ut, jnp.where(ut < 6, 24 + (ut - 3) * 8 + dt, 48 + dt))
        perm_t = one_at((ut < 7) & (jt == source))
        finT_s[...] = nn(perm_t, total).reshape(RS, 16, 128).astype(bf16)
        for s in range(1, RS):
            dest = (r + s) & 7
            remote(finT_s.at[dest], finT_r.at[r], sent, t_r.at[10], (fr, dest))
        finT_r[r] = finT_s[r]

    def t_finish():
        wait_for(finT_r.at[pl.ds(0, 7)], t_r.at[10])
        for cc in range(2):
            total = finT_r[cc].astype(f32)
            for ys in range(1, YS):
                total = total + finT_r[2 * ys + cc].astype(f32)
            g_out[pl.ds(24 + cc, 3, stride=2), :] = total[0:3]
            g_out[32 + 3 * cc : 35 + 3 * cc, :] = total[3:6]
            g_out[40 + cc : 41 + cc, :] = total[6:7]

    for h in chalo:
        h.wait_recv()
    shifted = (
        tuple(cots),
        (masked(halo_c[0], not_bottom), masked(halo_c[1], not_bottom)),
    )
    cots_of = (
        (3, 1, 1), (2, 1, 0), (3, 1, 0),
        (1, 0, 1), (0, 0, 0), (1, 0, 0),
        (3, 0, 1), (2, 0, 0), (3, 0, 0),
    )
    for t, (cell, rs, cs) in enumerate(cots_of):
        gd[t * C : (t + 1) * C, :] = tn(fc[cell], shifted[rs][cs])

    pack_rows(read_d, cD, 144)
    core_start(cD, rcD, 0)

    taps_of = {0: ((1, 0),), 1: ((0, 1), (2, 0))}
    blocks = []
    for rp in range(2):
        for cp_ in range(2):
            total = None
            for a, rs in taps_of[rp]:
                for b, cs in taps_of[cp_]:
                    term = nt(shifted[rs][cs], wd[(3 * a + b) * C : (3 * a + b + 1) * C, :])
                    total = term if total is None else total + term
            blocks.append(total)
    grad_fourth = jnp.concatenate(blocks, axis=0)

    grad_res = act_grad(residual, grad_fourth)
    grad_res_b = grad_res.astype(bf16)
    gp_[...] = tn(mixed, grad_res_b)
    grad_mixed = nt(grad_res_b, wo[...]).astype(bf16)

    perm_frames = one_at(j256 == (i256 & 3) * 64 + 2 * k8 + f8)
    a4s[...] = pack(nn(perm_frames, fourth_b)).astype(bf16)
    a2a_start(a4s, a4r, 3)

    a2a_wait(a3r.at[0], 2)
    a2a_wait(a3r.at[1], 4)
    phalo = [
        remote(a3r.at[1], hp.at[0], sent, hr.at[4], (fr, down)),
        remote(a3r.at[0], hp.at[1], sent, hr.at[5], (fr, up)),
    ]
    first_start(cD, rcD, yD, rlD, 0, 144, (1,))

    grad_w = nt(grad_mixed, value)
    grad_s = (
        weights * (grad_w - jnp.sum(grad_w * weights, axis=-1, keepdims=True)) * scale
    ).astype(bf16)
    grad_v = tn(weights_b, grad_mixed).astype(bf16)
    grad_q = nn(grad_s, key).astype(bf16)
    grad_k = tn(grad_s, query).astype(bf16)
    grad_proj = jnp.concatenate([grad_q, grad_k, grad_v], axis=1)
    grad_n = nt(grad_proj, wq[...]).astype(bf16).astype(f32)
    gq_[...] = tn(norm_b, grad_proj)
    grad_t = grad_res + rms_grad(norm_t, inv_t, grad_n)
    grad_tb = grad_t.astype(bf16)
    grad_tb32 = grad_tb.astype(f32)


    gt[0:C, :] = tn(second, frame_shift(grad_tb32, -2).astype(bf16))
    gt[C : 2 * C, :] = tn(second, frame_shift(grad_tb32, -1).astype(bf16))
    gt[2 * C :, :] = tn(second, grad_tb)
    t_pack()

    grad_second = nt(grad_tb, wtk[2])
    grad_second = grad_second + frame_shift(nt(grad_tb, wtk[1]), -1)
    grad_second = grad_second + frame_shift(nt(grad_tb, wtk[0]), -2)
    grad_sb = (grad_t + act_grad(sp, grad_second)).astype(bf16)

    first_start(cD, rcD, yD, rlD, 0, 144, (0,))
    first_halves(cD, rcD, yD, ryD, 0, 144, (1,))
    t_start()
    first_halves(cD, rcD, yD, ryD, 0, 144, (0,))

    for h in phalo:
        h.wait_recv()
    rows_in = (masked(hp[0], not_top), a3r[0], a3r[1], masked(hp[1], not_bottom))
    for hh in range(4):
        put(tmp, unpack(rows_in[hh].astype(f32)))
        cells = [every_fourth(tmp, ww) for ww in range(4)]
        for b in range(3):
            pair = jnp.concatenate([cells[b], cells[b + 1]], axis=0)
            at_[b, :, 128 * hh : 128 * hh + 128] = pair.T.astype(bf16)
    for a in range(3):
        for b in range(3):
            gs_[(3 * a + b) * C : (3 * a + b + 1) * C, :] = nn(at_[b, :, 128 * a : 128 * a + 256], grad_sb)
    pack_rows(read_2, c2, 72)
    core_start(c2, rc2, 1)

    first_relay(cD, rcD, yD, rlD, ryD, 0, 144)
    direct_start(c2, rc2, y2, ry2, 1, 72)

    for h in range(2):
        first_wait(rcD, ryD, 0, h, 144)
        for p in range(2):
            total = first_total(cD, rcD, ryD, h, p, 144).astype(bf16)
            zD[h, 2 * p] = total[:144]
            zD[h, 2 * p + 1] = total[144:]
        second_start(zD, rzD, 0, h)
    a2a_wait(a4r, 3)
    put(tmp, unpack(a4r[...].astype(f32)))
    first_col = lax.broadcasted_iota(jnp.int32, (32, C), 0) == 0
    cells_of = [
        [
            [
                jnp.concatenate(
                    [tmp[u, pl.ds(4 * f + 2 * hh + wp, 32, stride=8), :] for u in range(2)], axis=1
                ).astype(bf16)
                for wp in range(2)
            ]
            for hh in range(2)
        ]
        for f in range(2)
    ]
    for f in range(2):
        for wp in range(2):
            lrow_s[f, wp] = cells_of[f][1][wp]
    lhalo = remote(lrow_s, lrow_r, sent, hr.at[3], (fr, down))
    gap = jnp.zeros((8, 128), f32)
    for h in range(2):
        direct_wait(rc2, ry2, 1, h)
        for p in range(2):
            total = first_total(c2, rc2, ry2, h, p, 72)
            zE[h, 2 * p] = jnp.concatenate([total[:72], gap], axis=0).astype(bf16)
            zE[h, 2 * p + 1] = jnp.concatenate([total[72:], gap], axis=0).astype(bf16)
        second_start(zE, rzE, 1, h)

    it, jt = iota2(128, C)
    dt, ut = it >> 4, it & 15
    perm_d = one_at(jt == jnp.where(ut < 9, 0, 63) + dt * 9 + ut)
    perm_e = one_at((ut < 9) & (jt == dt * 9 + ut))
    perm_r = one_at((ut >= 9) & (ut < 11) & (jt == 70 + dt * 9 + ut))

    def widened(total, rows):
        return jnp.concatenate([total.astype(bf16), jnp.zeros((C - rows, 128), bf16)], axis=0)

    rest = []
    for h in range(2):
        total = widened(second_total(zD, rzD, 0, h), 144)
        finD_s[h] = nn(perm_d, total).reshape(RS, 16, 128).astype(bf16)
        last_start(finD_s, finD_r, 0, h)
        rest.append(nn(perm_r, total))
    t_second()
    for h in range(2):
        total = widened(second_total(zE, rzE, 1, h), 80)
        finE_s[h] = (nn(perm_e, total) + rest[h]).reshape(RS, 16, 128).astype(bf16)
        last_start(finE_s, finE_r, 1, h)

    lhalo.wait_recv()
    taps_in = []
    for a in range(3):
        here = [
            [masked(lrow_r[f, wp], not_top) if a == 0 else cells_of[f][a - 1][wp] for wp in range(2)]
            for f in range(2)
        ]
        for b in range(3):
            picked = [here[f][1 if b != 1 else 0].astype(f32) for f in range(2)]
            if b == 0:
                picked = [jnp.where(first_col, 0.0, pltpu.roll(v, 1, axis=0)) for v in picked]
            taps_in.append(jnp.concatenate(picked, axis=0).astype(bf16))
    latent = None
    for t in range(9):
        term = nn(taps_in[t], wd[t * C : (t + 1) * C, :])
        latent = term if latent is None else latent + term
    for f in range(2):
        lat_out[f, 0] = latent[32 * f : 32 * f + 32].astype(bf16)
    t_last()

    last_wait(finD_r, 0)
    for cc in range(2):
        total = last_total(finD_r, cc)
        g_out[pl.ds(48 + 2 * cc, 9, stride=4), :] = total[0:9]
        g_out[pl.ds(49 + 2 * cc, 7, stride=4), :] = total[9:16]
    last_wait(finE_r, 1)
    for cc in range(2):
        total = last_total(finE_r, cc)
        g_out[pl.ds(cc, 9, stride=2), :] = total[0:9]
        g_out[pl.ds(77 + 2 * cc, 2, stride=4), :] = total[9:11]
    t_finish()
    for h in halo + chalo + phalo + [lhalo]:
        h.wait_send()
    for send in (a1s, a2s, a3s.at[0], a3s.at[1], a4s):
        wait_for(send.at[pl.ds(0, FR - 1)], sent)
    for ref in (rcD, rlD, ryD, rzD, rc2, ry2, rzE, rcT, rzT, rxT, finT_s.at[pl.ds(0, 7)]):
        wait_for(ref, sent)
    for fin_s in (finD_s, finE_s):
        for h in range(2):
            wait_for(fin_s.at[h, pl.ds(0, 7)], sent)
            pl.when(jnp.logical_not(own[h]))(lambda fin_s=fin_s, h=h: wait_for(fin_s.at[h, 0], sent))


starts = (0, 24, 32, 40, 48)


def outputs(lat, g, lat_out, *outs):
    lat_out[...] = lat[...]
    for at, out in zip(starts, outs):
        out[...] = g[at : at + out.shape[0], :]


def per_device(frames_in, w_space, w_time, w_qkv, w_out, w_down, cotangent):
    def vb(*shape):
        return pltpu.VMEM(shape, bf16)

    def vf(*shape):
        return pltpu.VMEM(shape, f32)

    dma = pltpu.SemaphoreType.DMA
    scratch = [
        vb(2, 2, 64, C), vb(9 * C, C), vb(3 * C, C), vb(C, 3 * C), vb(C, C), vb(9 * C, 512), vb(2, 1, 32, 512),
        vb(2, 2, 64, C),
        vb(FR, 16, 128), vb(FR, 16, 128), vb(FR, 16, 128), vb(FR, 16, 128),
        vb(2, FR, 16, 128), vb(2, FR, 16, 128), vb(FR, 16, 128), vb(FR, 16, 128),
        vf(2, C, 128), vb(4, 64, C), vb(2, 2, 32, C), vb(2, 2, 32, C), vf(C, 128),
        vb(2, 64, 512), vb(2, 64, 512), vb(2, FR, 16, 128), vb(3, C, 512),
        vf(9 * C, 512), vf(3 * C, C), vf(C, 3 * C), vf(C, C), vf(9 * C, C),
    ]
    for rows in (144, 72):
        n = 4 * rows
        scratch += [vb(2, 2, 4, n, 128), vb(2, 4, n, 128), vb(2, 3, n, 128)]
        if rows == 144:
            scratch += [vb(2, 2, n // 2, 128), vb(2, 2, n, 128), vb(2, 4, 144, 128), vb(2, 3, 144, 128)]
            scratch += [vb(2, 8, 224, 128), vb(8, 224, 128), vb(8, 224, 128), vb(7, 224, 128)]
            scratch += [vb(4, 64, 128), vb(3, 64, 128), vb(8, 16, 128), vb(8, 16, 128)]
        else:
            scratch += [vb(2, 3, n, 128)]
    scratch += [vb(2, 4, 80, 128), vb(2, 3, 80, 128)]
    scratch += [vb(2, 8, 16, 128), vb(16, 16, 128), vb(2, 8, 16, 128), vb(16, 16, 128)]
    scratch += [
        dma((7,)), dma, dma((6,)), dma((5,)), dma((16,)), dma((4,)), dma((4,)), dma((4,)), dma((2,)), dma((11,)),
    ]
    anywhere = pl.BlockSpec(memory_space=pl.ANY)
    inside = pl.BlockSpec(memory_space=pltpu.VMEM)
    latent, grads = pl.pallas_call(
        kernel,
        out_shape=(vb(2, 1, 32, 512), vf(88, 128)),
        in_specs=[anywhere] * 7,
        out_specs=(inside, inside),
        scratch_shapes=scratch,
        compiler_params=pltpu.CompilerParams(has_side_effects=True, collective_id=0, vmem_limit_bytes=56 * 1024 * 1024),
        cost_estimate=pl.CostEstimate(flops=3 * 10**9, bytes_accessed=10**7, transcendentals=10**6),
    )(frames_in, w_space, w_time, w_qkv, w_out, w_down, cotangent)
    latent = pltpu.with_memory_space_constraint(latent, pltpu.VMEM)
    grads = pltpu.with_memory_space_constraint(grads, pltpu.VMEM)
    rows = (18, 6, 6, 2, 36)
    shapes = [latent.shape] + [(n, 128) for n in rows]
    results = pl.pallas_call(
        outputs,
        out_shape=[jax.ShapeDtypeStruct(v, f32 if i else bf16) for i, v in enumerate(shapes)],
        in_specs=[inside] * 2,
        out_specs=[inside] * 6,
    )(latent, grads)
    return (results[0],) + tuple(v.reshape(-1) for v in results[1:])


def solution(mesh):
    held = P("frame", "row", None, None)
    flat = P(("frame", "row"))
    return jax.shard_map(
        per_device,
        mesh=mesh,
        in_specs=(held, P(), P(), P(), P(), P(), held),
        out_specs=(held, flat, flat, flat, flat, flat),
        check_vma=False,
    )
```

```python
import math

import jax
import jax.numpy as jnp
from jax import lax
from jax.experimental import pallas as pl
from jax.experimental.pallas import tpu as pltpu
from jax.sharding import PartitionSpec as P

epsilon = 1e-06
f32 = jnp.float32
bf16 = jnp.bfloat16
MESH = pl.DeviceIdType.MESH
C = 256
FR, XS, ZS, YS, RS = 32, 4, 8, 4, 8


def nn(a, b):
    return jnp.dot(a, b, preferred_element_type=f32)


def nt(a, b):
    return lax.dot_general(a, b, (((1,), (1,)), ((), ())), preferred_element_type=f32)


def tn(a, b):
    return lax.dot_general(a, b, (((0,), (0,)), ((), ())), preferred_element_type=f32)


def inv_rms(v):
    return lax.rsqrt(jnp.mean(v * v, axis=-1, keepdims=True) + epsilon)


def sigmoid(n):
    return 1.0 / (1.0 + jnp.exp(-n))


def act(v):
    n = v * inv_rms(v)
    return n * sigmoid(n)


def rms_grad(normal, inv, upstream):
    return inv * (upstream - normal * jnp.mean(upstream * normal, axis=-1, keepdims=True))


def act_grad(v, upstream):
    inv = inv_rms(v)
    n = v * inv
    s = sigmoid(n)
    return rms_grad(n, inv, upstream * (s * (1.0 + n * (1.0 - s))))


def iota2(rows, cols):
    return (
        lax.broadcasted_iota(jnp.int32, (rows, cols), 0),
        lax.broadcasted_iota(jnp.int32, (rows, cols), 1),
    )


def one_at(hit):
    return jnp.where(hit, 1.0, 0.0).astype(bf16)


def frame_shift(v, by):
    frame = lax.broadcasted_iota(jnp.int32, v.shape, 0) & 63
    moved = pltpu.roll(v, by % v.shape[0], axis=0)
    keep = frame >= by if by > 0 else frame < 64 + by
    return jnp.where(keep, moved, 0.0)


def pack(m):
    m = m.reshape(FR, 8, C)
    return jnp.concatenate([m[:, :, :128], m[:, :, 128:]], axis=1)


def unpack(t):
    low = t[:, :8, :].reshape(C, 128)
    high = t[:, 8:16, :].reshape(C, 128)
    return jnp.concatenate([low, high], axis=1)


def put(ref, m):
    ref[0] = m[:, :128]
    ref[1] = m[:, 128:]


def every_fourth(ref, start):
    return jnp.concatenate([ref[u, pl.ds(start, 64, stride=4), :] for u in range(2)], axis=1)


def kernel(
    x_hbm, wsp_hbm, wt_hbm, wq_hbm, wo_hbm, wd_hbm, cot_hbm,
    lat_out, g_out,
    xv, wsp, wt, wq, wo, wd, cotv,
    halo_x,
    a1s, a1r, a2s, a2r, a3s, a3r, a4s, a4r,
    tmp, lrow_s, lrow_r, rows8, cc_, halo_c, hp, at_,
    gd, gt, gq_, gp_, gs_,
    cD, rcD, yD, rlD, ryD, zD, rzD,
    cT, rcT, zT, rzT, finT_s, finT_r,
    c2, rc2, y2, ry2,
    zE, rzE,
    finD_s, finD_r, finE_s, finE_r,
    lsem, sent, hr, ar, cs_r, ys_r, rl_r, zs_r, fs_r, t_r,
):
    fr = lax.axis_index("frame")
    r = lax.axis_index("row")
    z, x = fr >> 2, fr & 3
    y, c = r >> 1, r & 1

    def remote(src, dst, ssem, rsem, dev):
        cp = pltpu.make_async_remote_copy(
            src_ref=src, dst_ref=dst, send_sem=ssem, recv_sem=rsem, device_id=dev, device_id_type=MESH
        )
        cp.start()
        return cp

    def wait_for(ref, sem):
        pltpu.make_async_copy(ref, ref, sem).wait()

    up, down = (r + RS - 1) & 7, (r + 1) & 7
    turned = (y - z) & 3
    last = (turned * 4 + x, (4 + turned) * 4 + x)
    own = (last[0] == fr, last[1] == fr)

    places = (y, x)

    barrier = pltpu.get_barrier_semaphore()

    def tell(dev):
        pl.semaphore_signal(barrier, inc=1, device_id=dev, device_id_type=MESH)

    def far_first(n):
        t = n >> 2
        dz = 4 + (1 - 2 * (t & 1)) * ((t + 1) >> 1)
        return ((z + dz) & 7) * 4 + ((x + n + 1) & 3)

    lax.fori_loop(0, FR - 1, lambda n, carry: (tell((far_first(n), r)), carry)[1], 0)
    for dest in (up, down):
        tell((fr, dest))
    for s in range(2, RS - 1):
        tell((fr, (r + s) & 7))
    for s in range(ZS):
        zs = (z + s) & 7
        for cc in range(2):
            source = (zs * 4 + x, 2 * ((z + zs) & 3) + (c ^ cc))
            if s or cc:
                tell(source)
            else:
                pl.when(jnp.logical_not(own[0] | own[1]))(lambda source=source: tell(source))
    for s in range(1, XS):
        for dr in range(1, RS):
            tell((z * 4 + ((x + s) & 3), (r + dr) & 7))

    loads = []
    for i, (src, dst) in enumerate(
        ((cot_hbm, cotv), (x_hbm, xv), (wsp_hbm, wsp), (wd_hbm, wd), (wt_hbm, wt), (wq_hbm, wq), (wo_hbm, wo))
    ):
        cp = pltpu.make_async_copy(src, dst, lsem.at[i])
        cp.start()
        loads.append(cp)

    def a2a_start(send, recv, i):
        def step(n, carry):
            k = far_first(n)
            remote(send.at[k], recv.at[fr], sent, ar.at[i], (k, r))
            return carry

        lax.fori_loop(0, FR - 1, step, 0)
        recv[fr] = send[fr]

    def a2a_wait(recv, i):
        wait_for(recv.at[pl.ds(0, FR - 1)], ar.at[i])

    i256, j256 = iota2(C, C)
    k8, f8, h8, w8 = i256 >> 3, (i256 >> 2) & 1, (i256 >> 1) & 1, i256 & 1
    perm_cells = one_at(j256 == h8 * 128 + f8 * 64 + 2 * k8 + w8)
    i512, j512 = iota2(512, C)
    u16 = i512 & 15
    f16, q16 = u16 >> 2, u16 & 3
    jcol = (i512 >> 4) + (u16 >> 3)
    perm_cot = one_at((jcol < 32) & (j512 == q16 * 64 + (f16 & 1) * 32 + jcol))
    loads[0].wait()
    cot_rows = jnp.concatenate(
        [cotv[f, 0, :, 128 * q : 128 * q + 128] for q in range(4) for f in range(2)], axis=0
    )
    a2s[...] = nn(perm_cot, cot_rows).reshape(FR, 16, 128).astype(bf16)

    loads[1].wait()
    xf = jnp.concatenate([xv[0, 0], xv[1, 0], xv[0, 1], xv[1, 1]], axis=0).astype(f32)
    first = act(xf).astype(bf16)
    ip, jp = iota2(C, 128)
    wpos = 2 * (ip >> 3) - 1 + (ip & 3)
    perm_patch = one_at((wpos >= 0) & (wpos < 64) & (jp == ((ip >> 2) & 1) * 64 + wpos))
    a3s[0] = pack(nn(perm_patch, first[:128])).astype(bf16)
    a3s[1] = pack(nn(perm_patch, first[128:])).astype(bf16)
    loads[2].wait()

    def tap(a, b):
        return wsp[(3 * a + b) * C : (3 * a + b + 1) * C, :]

    parts = []
    for b in range(3):
        mid = nn(first, tap(1, b))
        other = jnp.concatenate([nn(first[128:], tap(2, b)), nn(first[:128], tap(0, b))], axis=0)
        parts.append(mid + other)
    pl.semaphore_wait(
        barrier, (FR - 1) + (RS - 1) + 21 + 2 * RS - jnp.where(own[0], 1, 0) - jnp.where(own[1], 1, 0)
    )
    halo = [
        remote(x_hbm.at[:, 1], halo_x.at[0], sent, hr.at[0], (fr, down)),
        remote(x_hbm.at[:, 0], halo_x.at[1], sent, hr.at[1], (fr, up)),
    ]
    a2a_start(a2s, a2r, 1)
    halo[0].wait_recv()
    halo[1].wait_recv()
    top = act(jnp.concatenate([halo_x[0, 0], halo_x[0, 1]], axis=0).astype(f32))
    top = jnp.where(r > 0, top, 0.0).astype(bf16)
    bottom = act(jnp.concatenate([halo_x[1, 0], halo_x[1, 1]], axis=0).astype(f32))
    bottom = jnp.where(r < RS - 1, bottom, 0.0).astype(bf16)
    for b in range(3):
        parts[b] = parts[b] + jnp.concatenate([nn(top, tap(0, b)), nn(bottom, tap(2, b))], axis=0)
    col = i256 & 63
    spatial = xf + parts[1]
    spatial = spatial + jnp.where(col > 0, pltpu.roll(parts[0], 1, axis=0), 0.0)
    spatial = spatial + jnp.where(col < 63, pltpu.roll(parts[2], C - 1, axis=0), 0.0)
    a1s[...] = pack(nn(perm_cells, spatial.astype(bf16))).astype(bf16)
    a2a_start(a1s, a1r, 0)
    a2a_start(a3s.at[0], a3r.at[0], 2)

    a2a_wait(a2r, 1)
    got = a2r[...].astype(f32)
    cots = []
    for u in range(2):
        rows8[...] = got[:, 8 * u : 8 * u + 8, :].reshape(C, 128)
        cots.append(
            jnp.concatenate([rows8[pl.ds(q, 64, stride=4), :] for q in range(4)], axis=1).astype(bf16)
        )
        cc_[u] = cots[u]
    cot_cell = cots[0]
    chalo = [remote(cc_, halo_c, sent, hr.at[2], (fr, up))]
    a2a_start(a3s.at[1], a3r.at[1], 4)
    not_top, not_left = r > 0, fr > 0
    not_bottom, not_right = r < RS - 1, fr < FR - 1

    def masked(v, keep):
        return jnp.where(keep, v.astype(f32), 0.0).astype(bf16)

    for i in range(3, 7):
        loads[i].wait()

    def down_tap(a, b, v):
        return nt(v, wd[(3 * a + b) * C : (3 * a + b + 1) * C, :])

    grad_own = [
        [down_tap(a, 1, cots[0]), down_tap(a, 0, cots[1]) + down_tap(a, 2, cots[0])] for a in (1, 2)
    ]

    a2a_wait(a1r, 0)
    put(tmp, unpack(a1r[...].astype(f32)))
    sp = jnp.concatenate([every_fourth(tmp, cell) for cell in range(4)], axis=0)
    second = act(sp).astype(bf16)
    wtk = [wt[k * C : (k + 1) * C, :] for k in range(3)]
    temporal = sp + nn(second, wtk[2])
    temporal = temporal + frame_shift(nn(second, wtk[1]), 1)
    temporal = temporal + frame_shift(nn(second, wtk[0]), 2)
    temporal = temporal.astype(bf16).astype(f32)
    inv_t = inv_rms(temporal)
    norm_t = temporal * inv_t
    norm_b = norm_t.astype(bf16)

    proj = nn(norm_b, wq[...]).astype(bf16)
    query, key, value = proj[:, :C], proj[:, C : 2 * C], proj[:, 2 * C :]
    scale = 1.0 / math.sqrt(C)
    logits = nt(query, key) * scale
    allowed = ((i256 >> 6) == (j256 >> 6)) & (i256 >= j256)
    logits = jnp.where(allowed, logits, -1e30)
    exponent = jnp.exp(logits - jnp.max(logits, axis=-1, keepdims=True))
    weights = exponent / jnp.sum(exponent, axis=-1, keepdims=True)
    weights_b = weights.astype(bf16)
    mixed = nn(weights_b, value).astype(bf16)
    attended = nn(mixed, wo[...]).astype(bf16).astype(f32)
    residual = (temporal + attended).astype(bf16).astype(f32)
    fourth = act(residual)

    fourth_b = fourth.astype(bf16)

    def pack_rows(read, cbuf, rows):
        def step(p, carry):
            s1, pair = p >> 1, p & 1
            at = pl.multiple_of(pair * (2 * rows), 16)
            pairs = ((s1 * 4 + 2 * pair, s1 * 4 + 2 * pair + 1), (16 + 8 * pair + s1, 20 + 8 * pair + s1))
            for h, (one, two) in enumerate(pairs):
                for cc in range(2):
                    both = jnp.concatenate([read(one, cc), read(two, cc)], axis=0)
                    cbuf[cc, h, s1, pl.ds(at, 2 * rows), :] = both.astype(bf16)
            return carry

        lax.fori_loop(0, 8, step, 0)

    def read_d(block, cc):
        at = pl.multiple_of(block * 72, 8)
        return jnp.concatenate(
            [gd[pl.ds(at, 72), cc * 256 + q * 128 : cc * 256 + q * 128 + 128] for q in range(2)], axis=0
        )

    def read_1(block, cc):
        a24, a8 = pl.multiple_of(block * 24, 8), pl.multiple_of(block * 8, 8)
        pieces = [gt[pl.ds(a24, 24), cc * 128 : cc * 128 + 128]]
        pieces += [gq_[pl.ds(a8, 8), cc * 384 + m * 128 : cc * 384 + m * 128 + 128] for m in range(3)]
        pieces += [gp_[pl.ds(a8, 8), cc * 128 : cc * 128 + 128]]
        return jnp.concatenate(pieces, axis=0)

    def read_2(block, cc):
        at = pl.multiple_of(block * 72, 8)
        return gs_[pl.ds(at, 72), cc * 128 : cc * 128 + 128]

    def part(axis, place):
        return (place - z) & 3 if axis == 0 else place

    def core_start(cbuf, rc, i):
        for s in (2, 1, 3, 0):
            for h in range(2):
                j = part(h, (places[h] + s) & 3)
                remote(cbuf.at[1 - c, h, j], rc.at[h, j], sent, cs_r.at[8 * i + 4 * h + s], (fr, r ^ 1))


    def along(axis, j):
        return (fr, 2 * j + c) if axis == 0 else (z * 4 + j, r)

    def pair_sum(cbuf, rc, h, s, p, rows):
        j = part(h, (places[h] + s) & 3)
        here = slice(2 * rows * p, 2 * rows * (p + 1))
        return cbuf[c, h, j, here, :].astype(f32) + rc[h, j, here, :].astype(f32)

    def core_wait(rc, i, s, h):
        j = part(h, (places[h] + s) & 3)
        wait_for(rc.at[h, j], cs_r.at[8 * i + 4 * h + s])

    def send_half(yb, ry, i, h, way, p, rows):
        half = pl.ds(2 * rows * p, 2 * rows)
        place = (places[h] + (1, 3)[way]) & 3
        remote(
            yb.at[h, way, half], ry.at[h, way, half], sent, ys_r.at[2 * i + h], along(h, place)
        )

    def first_start(cbuf, rc, yb, rl, i, rows, hs):
        for h in hs:
            core_wait(rc, i, 2, h)
            for p in range(2):
                half = slice(2 * rows * p, 2 * rows * (p + 1))
                yb[h, 2, half, :] = pair_sum(cbuf, rc, h, 2, p, rows).astype(bf16)
                place = (places[h] + (1, 3)[p]) & 3
                remote(
                    yb.at[h, 2, pl.ds(2 * rows * p, 2 * rows)], rl.at[h, p],
                    sent, rl_r.at[4 * i + 2 * h + p], along(h, place),
                )

    def first_halves(cbuf, rc, yb, ry, i, rows, hs):
        for way in range(2):
            for h in hs:
                p = 1 - way
                core_wait(rc, i, (1, 3)[way], h)
                half = slice(2 * rows * p, 2 * rows * (p + 1))
                yb[h, way, half, :] = pair_sum(cbuf, rc, h, (1, 3)[way], p, rows).astype(bf16)
                send_half(yb, ry, i, h, way, p, rows)

    def direct_start(cbuf, rc, yb, ry, i, rows):
        for s, slot in ((2, 2), (1, 0), (3, 1)):
            for h in range(2):
                core_wait(rc, i, s, h)
                for p in range(2):
                    half = slice(2 * rows * p, 2 * rows * (p + 1))
                    yb[h, slot, half, :] = pair_sum(cbuf, rc, h, s, p, rows).astype(bf16)
                place = (places[h] + s) & 3
                remote(yb.at[h, slot], ry.at[h, slot], sent, ys_r.at[2 * i + h], along(h, place))

    def direct_wait(rc, ry, i, h):
        core_wait(rc, i, 0, h)
        wait_for(ry.at[h], ys_r.at[2 * i + h])

    def first_relay(cbuf, rc, yb, rl, ry, i, rows):
        for h in range(2):
            for way in range(2):
                wait_for(rl.at[h, way], rl_r.at[4 * i + 2 * h + way])
                half = slice(2 * rows * way, 2 * rows * (way + 1))
                total = pair_sum(cbuf, rc, h, (1, 3)[way], way, rows) + rl[h, way].astype(f32)
                yb[h, way, half, :] = total.astype(bf16)
                send_half(yb, ry, i, h, way, way, rows)

    def first_total(cbuf, rc, ry, h, p, rows):
        half = slice(2 * rows * p, 2 * rows * (p + 1))
        total = pair_sum(cbuf, rc, h, 0, p, rows)
        for way in range(ry.shape[1]):
            total = total + ry[h, way, half, :].astype(f32)
        return total

    def first_wait(rc, ry, i, h, rows):
        core_wait(rc, i, 0, h)
        wait_for(ry.at[h], ys_r.at[2 * i + h])

    def second_start(zbuf, rz, i, h):
        for s in (1, 2, 3):
            j = (places[1 - h] + s) & 3
            remote(zbuf.at[h, part(1 - h, j)], rz.at[h, s - 1], sent, zs_r.at[2 * i + h], along(1 - h, j))

    def second_total(zbuf, rz, i, h):
        total = zbuf[h, part(1 - h, places[1 - h])].astype(f32)
        wait_for(rz.at[h], zs_r.at[2 * i + h])
        for s in range(3):
            total = total + rz[h, s].astype(f32)
        return total

    mine = 2 * z + c

    def last_start(fin_s, fin_r, i, h):
        for s in range(RS):
            dest = (r + s) & 7

            def send(dest=dest):
                remote(fin_s.at[h, dest], fin_r.at[mine], sent, fs_r.at[i], (last[h], dest))

            if s:
                send()
            else:
                pl.when(jnp.logical_not(own[h]))(send)

                @pl.when(own[h])
                def _():
                    fin_r[mine] = fin_s[h, r]

    def last_wait(fin_r, i):
        @pl.when(own[0] | own[1])
        def _():
            wait_for(fin_r.at[pl.ds(0, 15)], fs_r.at[i])

        @pl.when(jnp.logical_not(own[0] | own[1]))
        def _():
            wait_for(fin_r, fs_r.at[i])

    def last_total(fin_r, cc):
        total = fin_r[cc].astype(f32)
        for zs in range(1, ZS):
            total = total + fin_r[2 * zs + cc].astype(f32)
        return total

    def t_pack():
        def step(p, carry):
            zd, pair = p >> 1, p & 1
            at = pl.multiple_of(pair * 112, 16)
            block = zd * 4 + 2 * pair
            for cc in range(2):
                both = jnp.concatenate([read_1(block, cc), read_1(block + 1, cc)], axis=0)
                cT[cc, zd, pl.ds(at, 112), :] = both.astype(bf16)
            return carry

        lax.fori_loop(0, 16, step, 0)
        for s in (4, 3, 5, 2, 6, 1, 7, 0):
            zd = (z + s) & 7
            remote(cT.at[1 - c, zd], rcT.at[zd], sent, t_r.at[s], (fr, r ^ 1))

    def t_start():
        for s in (4, 3, 5, 2, 6, 1, 7):
            zd = (z + s) & 7
            wait_for(rcT.at[zd], t_r.at[s])
            zT[zd] = (cT[c, zd].astype(f32) + rcT[zd].astype(f32)).astype(bf16)
            remote(zT.at[zd], rzT.at[s - 1], sent, t_r.at[8], (zd * 4 + x, r))

    plane = x * RS + r

    def t_last():
        wait_for(rcT.at[z], t_r.at[0])
        total = cT[c, z].astype(f32) + rcT[z].astype(f32)
        wait_for(rzT, t_r.at[8])
        for s in range(1, ZS):
            total = total + rzT[s - 1].astype(f32)
        total = jnp.concatenate([total.astype(bf16), jnp.zeros((32, 128), bf16)], axis=0)
        it, jt = iota2(512, C)
        xt, dt, ut = it >> 7, (it >> 4) & 7, it & 15
        source = jnp.where(ut < 3, dt * 3 + ut, jnp.where(ut < 6, 24 + (ut - 3) * 8 + dt, 48 + dt))
        perm_t = one_at((ut < 7) & (jt == xt * 56 + source))
        finT_s[...] = nn(perm_t, total).reshape(32, 16, 128).astype(bf16)

        def step(n, carry):
            dest = (plane + n) & 31
            remote(finT_s.at[dest], finT_r.at[plane], sent, t_r.at[9], (z * 4 + (dest >> 3), dest & 7))
            return carry

        lax.fori_loop(1, 32, step, 0)
        finT_r[plane] = finT_s[plane]

    def t_finish():
        wait_for(finT_r.at[pl.ds(0, 31)], t_r.at[9])
        for cc in range(2):
            total = finT_r[cc].astype(f32)
            for chip in range(1, XS * YS):
                total = total + finT_r[2 * chip + cc].astype(f32)
            g_out[pl.ds(24 + cc, 3, stride=2), :] = total[0:3]
            g_out[32 + 3 * cc : 35 + 3 * cc, :] = total[3:6]
            g_out[40 + cc : 41 + cc, :] = total[6:7]

    for h in chalo:
        h.wait_recv()
    shifted = (
        tuple(cots),
        (masked(halo_c[0], not_bottom), masked(halo_c[1], not_bottom)),
    )
    cots_of = (
        (3, 1, 1), (2, 1, 0), (3, 1, 0),
        (1, 0, 1), (0, 0, 0), (1, 0, 0),
        (3, 0, 1), (2, 0, 0), (3, 0, 0),
    )
    turned_cells = [fourth[64 * cell : 64 * cell + 64].T.astype(bf16) for cell in range(4)]
    for t, (cell, rs, cs) in enumerate(cots_of):
        gd[t * C : (t + 1) * C, :] = nn(turned_cells[cell], shifted[rs][cs])

    pack_rows(read_d, cD, 144)
    core_start(cD, rcD, 0)

    below = shifted[1]
    grad_fourth = jnp.concatenate(
        grad_own[0]
        + [
            grad_own[1][0] + down_tap(0, 1, below[0]),
            grad_own[1][1] + down_tap(0, 0, below[1]) + down_tap(0, 2, below[0]),
        ],
        axis=0,
    )

    a2a_wait(a3r.at[0], 2)
    phalo = [remote(a3r.at[0], hp.at[1], sent, hr.at[5], (fr, up))]

    grad_res = act_grad(residual, grad_fourth)
    grad_res_b = grad_res.astype(bf16)
    gp_[...] = tn(mixed, grad_res_b)
    grad_mixed = nt(grad_res_b, wo[...]).astype(bf16)

    first_start(cD, rcD, yD, rlD, 0, 144, (1,))

    perm_frames = one_at(j256 == (i256 & 3) * 64 + 2 * k8 + f8)
    a4s[...] = pack(nn(perm_frames, fourth_b)).astype(bf16)
    a2a_start(a4s, a4r, 3)

    a2a_wait(a3r.at[1], 4)
    phalo.append(remote(a3r.at[1], hp.at[0], sent, hr.at[4], (fr, down)))

    grad_w = nt(grad_mixed, value)
    grad_s = (
        weights * (grad_w - jnp.sum(grad_w * weights, axis=-1, keepdims=True)) * scale
    ).astype(bf16)
    grad_v = tn(weights_b, grad_mixed).astype(bf16)
    grad_q = nn(grad_s, key).astype(bf16)
    grad_k = tn(grad_s, query).astype(bf16)
    grad_proj = jnp.concatenate([grad_q, grad_k, grad_v], axis=1)
    grad_n = nt(grad_proj, wq[...]).astype(bf16).astype(f32)
    gq_[...] = tn(norm_b, grad_proj)
    grad_t = grad_res + rms_grad(norm_t, inv_t, grad_n)
    grad_tb = grad_t.astype(bf16)
    grad_tb32 = grad_tb.astype(f32)


    turned_second = second.astype(f32).T.astype(bf16)
    gt[0:C, :] = nn(turned_second, frame_shift(grad_tb32, -2).astype(bf16))
    gt[C : 2 * C, :] = nn(turned_second, frame_shift(grad_tb32, -1).astype(bf16))
    gt[2 * C :, :] = nn(turned_second, grad_tb)
    t_pack()

    grad_second = nt(grad_tb, wtk[2])
    grad_second = grad_second + frame_shift(nt(grad_tb, wtk[1]), -1)
    grad_second = grad_second + frame_shift(nt(grad_tb, wtk[0]), -2)
    grad_sb = (grad_t + act_grad(sp, grad_second)).astype(bf16)

    first_start(cD, rcD, yD, rlD, 0, 144, (0,))
    first_halves(cD, rcD, yD, ryD, 0, 144, (1,))
    t_start()
    first_halves(cD, rcD, yD, ryD, 0, 144, (0,))

    for h in phalo:
        h.wait_recv()
    rows_in = (masked(hp[0], not_top), a3r[0], a3r[1], masked(hp[1], not_bottom))
    for hh in range(4):
        put(tmp, unpack(rows_in[hh].astype(f32)))
        cells = [every_fourth(tmp, ww) for ww in range(4)]
        for b in range(3):
            pair = jnp.concatenate([cells[b], cells[b + 1]], axis=0)
            at_[b, :, 128 * hh : 128 * hh + 128] = pair.T.astype(bf16)
    for a in range(3):
        for b in range(3):
            gs_[(3 * a + b) * C : (3 * a + b + 1) * C, :] = nn(at_[b, :, 128 * a : 128 * a + 256], grad_sb)
    pack_rows(read_2, c2, 72)
    core_start(c2, rc2, 1)

    first_relay(cD, rcD, yD, rlD, ryD, 0, 144)
    direct_start(c2, rc2, y2, ry2, 1, 72)

    for h in range(2):
        first_wait(rcD, ryD, 0, h, 144)
        for p in range(2):
            total = first_total(cD, rcD, ryD, h, p, 144).astype(bf16)
            zD[h, 2 * p] = total[:144]
            zD[h, 2 * p + 1] = total[144:]
        second_start(zD, rzD, 0, h)
    a2a_wait(a4r, 3)
    put(tmp, unpack(a4r[...].astype(f32)))
    first_col = lax.broadcasted_iota(jnp.int32, (32, C), 0) == 0
    cells_of = [
        [
            [
                jnp.concatenate(
                    [tmp[u, pl.ds(4 * f + 2 * hh + wp, 32, stride=8), :] for u in range(2)], axis=1
                ).astype(bf16)
                for wp in range(2)
            ]
            for hh in range(2)
        ]
        for f in range(2)
    ]
    for f in range(2):
        for wp in range(2):
            lrow_s[f, wp] = cells_of[f][1][wp]
    lhalo = remote(lrow_s, lrow_r, sent, hr.at[3], (fr, down))
    gap = jnp.zeros((8, 128), f32)
    for h in range(2):
        direct_wait(rc2, ry2, 1, h)
        for p in range(2):
            total = first_total(c2, rc2, ry2, h, p, 72)
            zE[h, 2 * p] = jnp.concatenate([total[:72], gap], axis=0).astype(bf16)
            zE[h, 2 * p + 1] = jnp.concatenate([total[72:], gap], axis=0).astype(bf16)
        second_start(zE, rzE, 1, h)

    it, jt = iota2(128, C)
    dt, ut = it >> 4, it & 15
    perm_d = one_at(jt == jnp.where(ut < 9, 0, 63) + dt * 9 + ut)
    perm_e = one_at((ut < 9) & (jt == dt * 9 + ut))
    perm_r = one_at((ut >= 9) & (ut < 11) & (jt == 70 + dt * 9 + ut))

    def widened(total, rows):
        return jnp.concatenate([total.astype(bf16), jnp.zeros((C - rows, 128), bf16)], axis=0)

    for h in range(2):
        total_d = widened(second_total(zD, rzD, 0, h), 144)
        finD_s[h] = nn(perm_d, total_d).reshape(RS, 16, 128).astype(bf16)
        last_start(finD_s, finD_r, 0, h)
        total = widened(second_total(zE, rzE, 1, h), 80)
        finE_s[h] = (nn(perm_e, total) + nn(perm_r, total_d)).reshape(RS, 16, 128).astype(bf16)
        last_start(finE_s, finE_r, 1, h)
        if h == 0:
            t_last()

    lhalo.wait_recv()
    taps_in = []
    for a in range(3):
        here = [
            [masked(lrow_r[f, wp], not_top) if a == 0 else cells_of[f][a - 1][wp] for wp in range(2)]
            for f in range(2)
        ]
        for b in range(3):
            picked = [here[f][1 if b != 1 else 0].astype(f32) for f in range(2)]
            if b == 0:
                picked = [jnp.where(first_col, 0.0, pltpu.roll(v, 1, axis=0)) for v in picked]
            taps_in.append(jnp.concatenate(picked, axis=0).astype(bf16))
    latent = None
    for t in range(9):
        term = nn(taps_in[t], wd[t * C : (t + 1) * C, :])
        latent = term if latent is None else latent + term
    for f in range(2):
        lat_out[f, 0] = latent[32 * f : 32 * f + 32].astype(bf16)

    last_wait(finD_r, 0)
    for cc in range(2):
        total = last_total(finD_r, cc)
        g_out[pl.ds(48 + 2 * cc, 9, stride=4), :] = total[0:9]
        g_out[pl.ds(49 + 2 * cc, 7, stride=4), :] = total[9:16]
    t_finish()
    last_wait(finE_r, 1)
    for cc in range(2):
        total = last_total(finE_r, cc)
        g_out[pl.ds(cc, 9, stride=2), :] = total[0:9]
        g_out[pl.ds(77 + 2 * cc, 2, stride=4), :] = total[9:11]
    for h in halo + chalo + phalo + [lhalo]:
        h.wait_send()
    for send in (a1s, a2s, a3s.at[0], a3s.at[1], a4s):
        wait_for(send.at[pl.ds(0, FR - 1)], sent)
    for ref in (rcD, rlD, ryD, rzD, rc2, ry2, rzE, rcT, rzT, finT_s.at[pl.ds(0, 31)]):
        wait_for(ref, sent)
    for fin_s in (finD_s, finE_s):
        for h in range(2):
            wait_for(fin_s.at[h, pl.ds(0, 7)], sent)
            pl.when(jnp.logical_not(own[h]))(lambda fin_s=fin_s, h=h: wait_for(fin_s.at[h, 0], sent))


starts = (0, 24, 32, 40, 48)


def outputs(lat, g, lat_out, *outs):
    lat_out[...] = lat[...]
    for at, out in zip(starts, outs):
        out[...] = g[at : at + out.shape[0], :]


def per_device(frames_in, w_space, w_time, w_qkv, w_out, w_down, cotangent):
    def vb(*shape):
        return pltpu.VMEM(shape, bf16)

    def vf(*shape):
        return pltpu.VMEM(shape, f32)

    dma = pltpu.SemaphoreType.DMA
    scratch = [
        vb(2, 2, 64, C), vb(9 * C, C), vb(3 * C, C), vb(C, 3 * C), vb(C, C), vb(9 * C, 512), vb(2, 1, 32, 512),
        vb(2, 2, 64, C),
        vb(FR, 16, 128), vb(FR, 16, 128), vb(FR, 16, 128), vb(FR, 16, 128),
        vb(2, FR, 16, 128), vb(2, FR, 16, 128), vb(FR, 16, 128), vb(FR, 16, 128),
        vf(2, C, 128), vb(2, 2, 32, C), vb(2, 2, 32, C), vf(C, 128),
        vb(2, 64, 512), vb(2, 64, 512), vb(2, FR, 16, 128), vb(3, C, 512),
        vf(9 * C, 512), vf(3 * C, C), vf(C, 3 * C), vf(C, C), vf(9 * C, C),
    ]
    for rows in (144, 72):
        n = 4 * rows
        scratch += [vb(2, 2, 4, n, 128), vb(2, 4, n, 128), vb(2, 3, n, 128)]
        if rows == 144:
            scratch += [vb(2, 2, n // 2, 128), vb(2, 2, n, 128), vb(2, 4, 144, 128), vb(2, 3, 144, 128)]
            scratch += [vb(2, 8, 224, 128), vb(8, 224, 128), vb(8, 224, 128), vb(7, 224, 128)]
            scratch += [vb(32, 16, 128), vb(32, 16, 128)]
        else:
            scratch += [vb(2, 3, n, 128)]
    scratch += [vb(2, 4, 80, 128), vb(2, 3, 80, 128)]
    scratch += [vb(2, 8, 16, 128), vb(16, 16, 128), vb(2, 8, 16, 128), vb(16, 16, 128)]
    scratch += [
        dma((7,)), dma, dma((6,)), dma((5,)), dma((16,)), dma((4,)), dma((4,)), dma((4,)), dma((2,)), dma((10,)),
    ]
    anywhere = pl.BlockSpec(memory_space=pl.ANY)
    inside = pl.BlockSpec(memory_space=pltpu.VMEM)
    latent, grads = pl.pallas_call(
        kernel,
        out_shape=(vb(2, 1, 32, 512), vf(88, 128)),
        in_specs=[anywhere] * 7,
        out_specs=(inside, inside),
        scratch_shapes=scratch,
        compiler_params=pltpu.CompilerParams(has_side_effects=True, collective_id=0, vmem_limit_bytes=56 * 1024 * 1024),
        cost_estimate=pl.CostEstimate(flops=3 * 10**9, bytes_accessed=10**7, transcendentals=10**6),
    )(frames_in, w_space, w_time, w_qkv, w_out, w_down, cotangent)
    latent = pltpu.with_memory_space_constraint(latent, pltpu.VMEM)
    grads = pltpu.with_memory_space_constraint(grads, pltpu.VMEM)
    rows = (18, 6, 6, 2, 36)
    shapes = [latent.shape] + [(n, 128) for n in rows]
    results = pl.pallas_call(
        outputs,
        out_shape=[jax.ShapeDtypeStruct(v, f32 if i else bf16) for i, v in enumerate(shapes)],
        in_specs=[inside] * 2,
        out_specs=[inside] * 6,
    )(latent, grads)
    return (results[0],) + tuple(v.reshape(-1) for v in results[1:])


def solution(mesh):
    held = P("frame", "row", None, None)
    flat = P(("frame", "row"))
    return jax.shard_map(
        per_device,
        mesh=mesh,
        in_specs=(held, P(), P(), P(), P(), P(), held),
        out_specs=(held, flat, flat, flat, flat, flat),
        check_vma=False,
    )
```

```python
import math

import jax
import jax.numpy as jnp
from jax import lax
from jax.experimental import pallas as pl
from jax.experimental.pallas import tpu as pltpu
from jax.sharding import PartitionSpec as P

epsilon = 1e-06
f32 = jnp.float32
bf16 = jnp.bfloat16
MESH = pl.DeviceIdType.MESH
C = 256
FR, XS, ZS, YS, RS = 32, 4, 8, 4, 8


def nn(a, b):
    return jnp.dot(a, b, preferred_element_type=f32)


def nt(a, b):
    return lax.dot_general(a, b, (((1,), (1,)), ((), ())), preferred_element_type=f32)


def tn(a, b):
    return lax.dot_general(a, b, (((0,), (0,)), ((), ())), preferred_element_type=f32)


def inv_rms(v):
    return lax.rsqrt(jnp.mean(v * v, axis=-1, keepdims=True) + epsilon)


def sigmoid(n):
    return 1.0 / (1.0 + jnp.exp(-n))


def act(v):
    n = v * inv_rms(v)
    return n * sigmoid(n)


def rms_grad(normal, inv, upstream):
    return inv * (upstream - normal * jnp.mean(upstream * normal, axis=-1, keepdims=True))


def act_grad(v, upstream):
    inv = inv_rms(v)
    n = v * inv
    s = sigmoid(n)
    return rms_grad(n, inv, upstream * (s * (1.0 + n * (1.0 - s))))


def iota2(rows, cols):
    return (
        lax.broadcasted_iota(jnp.int32, (rows, cols), 0),
        lax.broadcasted_iota(jnp.int32, (rows, cols), 1),
    )


def one_at(hit):
    return jnp.where(hit, 1.0, 0.0).astype(bf16)


def frame_shift(v, by):
    frame = lax.broadcasted_iota(jnp.int32, v.shape, 0) & 63
    moved = pltpu.roll(v, by % v.shape[0], axis=0)
    keep = frame >= by if by > 0 else frame < 64 + by
    return jnp.where(keep, moved, 0.0)


def pack(m):
    m = m.reshape(FR, 8, C)
    return jnp.concatenate([m[:, :, :128], m[:, :, 128:]], axis=1)


def unpack(t):
    low = t[:, :8, :].reshape(C, 128)
    high = t[:, 8:16, :].reshape(C, 128)
    return jnp.concatenate([low, high], axis=1)


def put(ref, m):
    ref[0] = m[:, :128]
    ref[1] = m[:, 128:]


def every_fourth(ref, start):
    return jnp.concatenate([ref[u, pl.ds(start, 64, stride=4), :] for u in range(2)], axis=1)


def kernel(
    x_hbm, wsp_hbm, wt_hbm, wq_hbm, wo_hbm, wd_hbm, cot_hbm,
    lat_out, g_out,
    xv, wsp, wt, wq, wo, wd, cotv,
    halo_x,
    a1s, a1r, a2s, a2r, a3s, a3r, a4s, a4r,
    tmp, lrow_s, lrow_r, rows8, cc_, halo_c, hp, at_,
    gd, gt, gq_, gp_, gs_,
    cD, rcD, yD, rlD, ryD, zD, rzD,
    cT, rcT, zT, rzT, finT_s, finT_r,
    c2, rc2, y2, ry2,
    zE, rzE,
    finD_s, finD_r, finE_s, finE_r,
    lsem, sent, hr, ar, cs_r, ys_r, rl_r, zs_r, fs_r, t_r,
):
    fr = lax.axis_index("frame")
    r = lax.axis_index("row")
    z, x = fr >> 2, fr & 3
    y, c = r >> 1, r & 1

    def remote(src, dst, ssem, rsem, dev):
        cp = pltpu.make_async_remote_copy(
            src_ref=src, dst_ref=dst, send_sem=ssem, recv_sem=rsem, device_id=dev, device_id_type=MESH
        )
        cp.start()
        return cp

    def wait_for(ref, sem):
        pltpu.make_async_copy(ref, ref, sem).wait()

    up, down = (r + RS - 1) & 7, (r + 1) & 7
    turned = (y - z) & 3
    last = (turned * 4 + x, (4 + turned) * 4 + x)
    own = (last[0] == fr, last[1] == fr)

    places = (y, x)

    barrier = pltpu.get_barrier_semaphore()

    def tell(dev):
        pl.semaphore_signal(barrier, inc=1, device_id=dev, device_id_type=MESH)

    def far_first(n):
        t = n >> 2
        dz = 4 + (1 - 2 * (t & 1)) * ((t + 1) >> 1)
        return ((z + dz) & 7) * 4 + ((x + n + 1) & 3)

    lax.fori_loop(0, FR - 1, lambda n, carry: (tell((far_first(n), r)), carry)[1], 0)
    for dest in (up, down):
        tell((fr, dest))
    for s in range(2, RS - 1):
        tell((fr, (r + s) & 7))
    loads = []
    for i, (src, dst) in enumerate(
        ((cot_hbm, cotv), (x_hbm, xv), (wsp_hbm, wsp), (wd_hbm, wd), (wt_hbm, wt), (wq_hbm, wq), (wo_hbm, wo))
    ):
        cp = pltpu.make_async_copy(src, dst, lsem.at[i])
        cp.start()
        loads.append(cp)

    def a2a_start(send, recv, i):
        def step(n, carry):
            k = far_first(n)
            remote(send.at[k], recv.at[fr], sent, ar.at[i], (k, r))
            return carry

        lax.fori_loop(0, FR - 1, step, 0)
        recv[fr] = send[fr]

    def a2a_wait(recv, i):
        wait_for(recv.at[pl.ds(0, FR - 1)], ar.at[i])

    i256, j256 = iota2(C, C)
    k8, f8, h8, w8 = i256 >> 3, (i256 >> 2) & 1, (i256 >> 1) & 1, i256 & 1
    perm_cells = one_at(j256 == h8 * 128 + f8 * 64 + 2 * k8 + w8)
    i512, j512 = iota2(512, C)
    u16 = i512 & 15
    f16, q16 = u16 >> 2, u16 & 3
    jcol = (i512 >> 4) + (u16 >> 3)
    perm_cot = one_at((jcol < 32) & (j512 == q16 * 64 + (f16 & 1) * 32 + jcol))
    loads[0].wait()
    cot_rows = jnp.concatenate(
        [cotv[f, 0, :, 128 * q : 128 * q + 128] for q in range(4) for f in range(2)], axis=0
    )
    a2s[...] = nn(perm_cot, cot_rows).reshape(FR, 16, 128).astype(bf16)

    loads[1].wait()
    xf = jnp.concatenate([xv[0, 0], xv[1, 0], xv[0, 1], xv[1, 1]], axis=0).astype(f32)
    first = act(xf).astype(bf16)
    ip, jp = iota2(C, 128)
    wpos = 2 * (ip >> 3) - 1 + (ip & 3)
    perm_patch = one_at((wpos >= 0) & (wpos < 64) & (jp == ((ip >> 2) & 1) * 64 + wpos))
    a3s[0] = pack(nn(perm_patch, first[:128])).astype(bf16)
    a3s[1] = pack(nn(perm_patch, first[128:])).astype(bf16)
    loads[2].wait()

    def tap(a, b):
        return wsp[(3 * a + b) * C : (3 * a + b + 1) * C, :]

    parts = []
    for b in range(3):
        mid = nn(first, tap(1, b))
        other = jnp.concatenate([nn(first[128:], tap(2, b)), nn(first[:128], tap(0, b))], axis=0)
        parts.append(mid + other)
    pl.semaphore_wait(
        barrier, (FR - 1) + (RS - 1)
    )
    halo = [
        remote(x_hbm.at[:, 1], halo_x.at[0], sent, hr.at[0], (fr, down)),
        remote(x_hbm.at[:, 0], halo_x.at[1], sent, hr.at[1], (fr, up)),
    ]
    a2a_start(a2s, a2r, 1)
    halo[0].wait_recv()
    halo[1].wait_recv()
    top = act(jnp.concatenate([halo_x[0, 0], halo_x[0, 1]], axis=0).astype(f32))
    top = jnp.where(r > 0, top, 0.0).astype(bf16)
    bottom = act(jnp.concatenate([halo_x[1, 0], halo_x[1, 1]], axis=0).astype(f32))
    bottom = jnp.where(r < RS - 1, bottom, 0.0).astype(bf16)
    for b in range(3):
        parts[b] = parts[b] + jnp.concatenate([nn(top, tap(0, b)), nn(bottom, tap(2, b))], axis=0)
    col = i256 & 63
    spatial = xf + parts[1]
    spatial = spatial + jnp.where(col > 0, pltpu.roll(parts[0], 1, axis=0), 0.0)
    spatial = spatial + jnp.where(col < 63, pltpu.roll(parts[2], C - 1, axis=0), 0.0)
    a1s[...] = pack(nn(perm_cells, spatial.astype(bf16))).astype(bf16)
    a2a_start(a1s, a1r, 0)
    a2a_start(a3s.at[0], a3r.at[0], 2)

    a2a_wait(a2r, 1)
    got = a2r[...].astype(f32)
    cots = []
    for u in range(2):
        rows8[...] = got[:, 8 * u : 8 * u + 8, :].reshape(C, 128)
        cots.append(
            jnp.concatenate([rows8[pl.ds(q, 64, stride=4), :] for q in range(4)], axis=1).astype(bf16)
        )
        cc_[u] = cots[u]
    cot_cell = cots[0]
    chalo = [remote(cc_, halo_c, sent, hr.at[2], (fr, up))]
    a2a_start(a3s.at[1], a3r.at[1], 4)
    not_top, not_left = r > 0, fr > 0
    not_bottom, not_right = r < RS - 1, fr < FR - 1

    def masked(v, keep):
        return jnp.where(keep, v.astype(f32), 0.0).astype(bf16)

    for i in range(3, 7):
        loads[i].wait()

    def down_tap(a, b, v):
        return nt(v, wd[(3 * a + b) * C : (3 * a + b + 1) * C, :])

    grad_own = [
        [down_tap(a, 1, cots[0]), down_tap(a, 0, cots[1]) + down_tap(a, 2, cots[0])] for a in (1, 2)
    ]

    a2a_wait(a1r, 0)
    put(tmp, unpack(a1r[...].astype(f32)))
    sp = jnp.concatenate([every_fourth(tmp, cell) for cell in range(4)], axis=0)
    second = act(sp).astype(bf16)
    wtk = [wt[k * C : (k + 1) * C, :] for k in range(3)]
    temporal = sp + nn(second, wtk[2])
    temporal = temporal + frame_shift(nn(second, wtk[1]), 1)
    temporal = temporal + frame_shift(nn(second, wtk[0]), 2)
    temporal = temporal.astype(bf16).astype(f32)
    inv_t = inv_rms(temporal)
    norm_t = temporal * inv_t
    norm_b = norm_t.astype(bf16)

    proj = nn(norm_b, wq[...]).astype(bf16)
    query, key, value = proj[:, :C], proj[:, C : 2 * C], proj[:, 2 * C :]
    scale = 1.0 / math.sqrt(C)
    logits = nt(query, key) * scale
    allowed = ((i256 >> 6) == (j256 >> 6)) & (i256 >= j256)
    logits = jnp.where(allowed, logits, -1e30)
    exponent = jnp.exp(logits - jnp.max(logits, axis=-1, keepdims=True))
    weights = exponent / jnp.sum(exponent, axis=-1, keepdims=True)
    weights_b = weights.astype(bf16)
    mixed = nn(weights_b, value).astype(bf16)
    attended = nn(mixed, wo[...]).astype(bf16).astype(f32)
    residual = (temporal + attended).astype(bf16).astype(f32)
    fourth = act(residual)

    fourth_b = fourth.astype(bf16)

    def pack_rows(read, cbuf, rows):
        def step(p, carry):
            s1, pair = p >> 1, p & 1
            at = pl.multiple_of(pair * (2 * rows), 16)
            pairs = ((s1 * 4 + 2 * pair, s1 * 4 + 2 * pair + 1), (16 + 8 * pair + s1, 20 + 8 * pair + s1))
            for h, (one, two) in enumerate(pairs):
                for cc in range(2):
                    both = jnp.concatenate([read(one, cc), read(two, cc)], axis=0)
                    cbuf[cc, h, s1, pl.ds(at, 2 * rows), :] = both.astype(bf16)
            return carry

        lax.fori_loop(0, 8, step, 0)

    def read_d(block, cc):
        at = pl.multiple_of(block * 72, 8)
        return jnp.concatenate(
            [gd[pl.ds(at, 72), cc * 256 + q * 128 : cc * 256 + q * 128 + 128] for q in range(2)], axis=0
        )

    def read_1(block, cc):
        a24, a8 = pl.multiple_of(block * 24, 8), pl.multiple_of(block * 8, 8)
        pieces = [gt[pl.ds(a24, 24), cc * 128 : cc * 128 + 128]]
        pieces += [gq_[pl.ds(a8, 8), cc * 384 + m * 128 : cc * 384 + m * 128 + 128] for m in range(3)]
        pieces += [gp_[pl.ds(a8, 8), cc * 128 : cc * 128 + 128]]
        return jnp.concatenate(pieces, axis=0)

    def read_2(block, cc):
        at = pl.multiple_of(block * 72, 8)
        return gs_[pl.ds(at, 72), cc * 128 : cc * 128 + 128]

    def part(axis, place):
        return (place - z) & 3 if axis == 0 else place

    def core_start(cbuf, rc, i):
        for s in (2, 1, 3, 0):
            for h in range(2):
                j = part(h, (places[h] + s) & 3)
                remote(cbuf.at[1 - c, h, j], rc.at[h, j], sent, cs_r.at[8 * i + 4 * h + s], (fr, r ^ 1))


    def along(axis, j):
        return (fr, 2 * j + c) if axis == 0 else (z * 4 + j, r)

    def pair_sum(cbuf, rc, h, s, p, rows):
        j = part(h, (places[h] + s) & 3)
        here = slice(2 * rows * p, 2 * rows * (p + 1))
        return cbuf[c, h, j, here, :].astype(f32) + rc[h, j, here, :].astype(f32)

    def core_wait(rc, i, s, h):
        j = part(h, (places[h] + s) & 3)
        wait_for(rc.at[h, j], cs_r.at[8 * i + 4 * h + s])

    def send_half(yb, ry, i, h, way, p, rows):
        half = pl.ds(2 * rows * p, 2 * rows)
        place = (places[h] + (1, 3)[way]) & 3
        remote(
            yb.at[h, way, half], ry.at[h, way, half], sent, ys_r.at[2 * i + h], along(h, place)
        )

    def first_start(cbuf, rc, yb, rl, i, rows, hs):
        for h in hs:
            core_wait(rc, i, 2, h)
            for p in range(2):
                half = slice(2 * rows * p, 2 * rows * (p + 1))
                yb[h, 2, half, :] = pair_sum(cbuf, rc, h, 2, p, rows).astype(bf16)
                place = (places[h] + (1, 3)[p]) & 3
                remote(
                    yb.at[h, 2, pl.ds(2 * rows * p, 2 * rows)], rl.at[h, p],
                    sent, rl_r.at[4 * i + 2 * h + p], along(h, place),
                )

    def first_halves(cbuf, rc, yb, ry, i, rows, hs):
        for way in range(2):
            for h in hs:
                p = 1 - way
                core_wait(rc, i, (1, 3)[way], h)
                half = slice(2 * rows * p, 2 * rows * (p + 1))
                yb[h, way, half, :] = pair_sum(cbuf, rc, h, (1, 3)[way], p, rows).astype(bf16)
                send_half(yb, ry, i, h, way, p, rows)

    def direct_start(cbuf, rc, yb, ry, i, rows):
        for s, slot in ((2, 2), (1, 0), (3, 1)):
            for h in range(2):
                core_wait(rc, i, s, h)
                for p in range(2):
                    half = slice(2 * rows * p, 2 * rows * (p + 1))
                    yb[h, slot, half, :] = pair_sum(cbuf, rc, h, s, p, rows).astype(bf16)
                place = (places[h] + s) & 3
                remote(yb.at[h, slot], ry.at[h, slot], sent, ys_r.at[2 * i + h], along(h, place))

    def direct_wait(rc, ry, i, h):
        core_wait(rc, i, 0, h)
        wait_for(ry.at[h], ys_r.at[2 * i + h])

    def first_relay(cbuf, rc, yb, rl, ry, i, rows):
        for h in range(2):
            for way in range(2):
                wait_for(rl.at[h, way], rl_r.at[4 * i + 2 * h + way])
                half = slice(2 * rows * way, 2 * rows * (way + 1))
                total = pair_sum(cbuf, rc, h, (1, 3)[way], way, rows) + rl[h, way].astype(f32)
                yb[h, way, half, :] = total.astype(bf16)
                send_half(yb, ry, i, h, way, way, rows)

    def first_total(cbuf, rc, ry, h, p, rows):
        half = slice(2 * rows * p, 2 * rows * (p + 1))
        total = pair_sum(cbuf, rc, h, 0, p, rows)
        for way in range(ry.shape[1]):
            total = total + ry[h, way, half, :].astype(f32)
        return total

    def first_wait(rc, ry, i, h, rows):
        core_wait(rc, i, 0, h)
        wait_for(ry.at[h], ys_r.at[2 * i + h])

    def second_start(zbuf, rz, i, h):
        for s in (1, 2, 3):
            j = (places[1 - h] + s) & 3
            remote(zbuf.at[h, part(1 - h, j)], rz.at[h, s - 1], sent, zs_r.at[2 * i + h], along(1 - h, j))

    def second_total(zbuf, rz, i, h):
        total = zbuf[h, part(1 - h, places[1 - h])].astype(f32)
        wait_for(rz.at[h], zs_r.at[2 * i + h])
        for s in range(3):
            total = total + rz[h, s].astype(f32)
        return total

    mine = 2 * z + c

    def last_start(fin_s, fin_r, i, h):
        for s in range(RS):
            dest = (r + s) & 7

            def send(dest=dest):
                remote(fin_s.at[h, dest], fin_r.at[mine], sent, fs_r.at[i], (last[h], dest))

            if s:
                send()
            else:
                pl.when(jnp.logical_not(own[h]))(send)

                @pl.when(own[h])
                def _():
                    fin_r[mine] = fin_s[h, r]

    def last_wait(fin_r, i):
        @pl.when(own[0] | own[1])
        def _():
            wait_for(fin_r.at[pl.ds(0, 15)], fs_r.at[i])

        @pl.when(jnp.logical_not(own[0] | own[1]))
        def _():
            wait_for(fin_r, fs_r.at[i])

    def last_total(fin_r, cc):
        total = fin_r[cc].astype(f32)
        for zs in range(1, ZS):
            total = total + fin_r[2 * zs + cc].astype(f32)
        return total

    def t_pack():
        def step(p, carry):
            zd, pair = p >> 1, p & 1
            at = pl.multiple_of(pair * 112, 16)
            block = zd * 4 + 2 * pair
            for cc in range(2):
                both = jnp.concatenate([read_1(block, cc), read_1(block + 1, cc)], axis=0)
                cT[cc, zd, pl.ds(at, 112), :] = both.astype(bf16)
            return carry

        lax.fori_loop(0, 16, step, 0)
        for s in (4, 3, 5, 2, 6, 1, 7, 0):
            zd = (z + s) & 7
            remote(cT.at[1 - c, zd], rcT.at[zd], sent, t_r.at[s], (fr, r ^ 1))

    def t_start():
        for s in (4, 3, 5, 2, 6, 1, 7):
            zd = (z + s) & 7
            wait_for(rcT.at[zd], t_r.at[s])
            zT[zd] = (cT[c, zd].astype(f32) + rcT[zd].astype(f32)).astype(bf16)
            remote(zT.at[zd], rzT.at[s - 1], sent, t_r.at[8], (zd * 4 + x, r))

    plane = x * RS + r

    def t_last():
        wait_for(rcT.at[z], t_r.at[0])
        total = cT[c, z].astype(f32) + rcT[z].astype(f32)
        wait_for(rzT, t_r.at[8])
        for s in range(1, ZS):
            total = total + rzT[s - 1].astype(f32)
        total = jnp.concatenate([total.astype(bf16), jnp.zeros((32, 128), bf16)], axis=0)
        it, jt = iota2(512, C)
        xt, dt, ut = it >> 7, (it >> 4) & 7, it & 15
        source = jnp.where(ut < 3, dt * 3 + ut, jnp.where(ut < 6, 24 + (ut - 3) * 8 + dt, 48 + dt))
        perm_t = one_at((ut < 7) & (jt == xt * 56 + source))
        finT_s[...] = nn(perm_t, total).reshape(32, 16, 128).astype(bf16)

        def step(n, carry):
            dest = (plane + n) & 31
            remote(finT_s.at[dest], finT_r.at[plane], sent, t_r.at[9], (z * 4 + (dest >> 3), dest & 7))
            return carry

        lax.fori_loop(1, 32, step, 0)
        finT_r[plane] = finT_s[plane]

    def t_finish():
        wait_for(finT_r.at[pl.ds(0, 31)], t_r.at[9])
        for cc in range(2):
            total = finT_r[cc].astype(f32)
            for chip in range(1, XS * YS):
                total = total + finT_r[2 * chip + cc].astype(f32)
            g_out[pl.ds(24 + cc, 3, stride=2), :] = total[0:3]
            g_out[32 + 3 * cc : 35 + 3 * cc, :] = total[3:6]
            g_out[40 + cc : 41 + cc, :] = total[6:7]

    for h in chalo:
        h.wait_recv()
    shifted = (
        tuple(cots),
        (masked(halo_c[0], not_bottom), masked(halo_c[1], not_bottom)),
    )
    cots_of = (
        (3, 1, 1), (2, 1, 0), (3, 1, 0),
        (1, 0, 1), (0, 0, 0), (1, 0, 0),
        (3, 0, 1), (2, 0, 0), (3, 0, 0),
    )
    turned_cells = [fourth[64 * cell : 64 * cell + 64].T.astype(bf16) for cell in range(4)]
    for t, (cell, rs, cs) in enumerate(cots_of):
        gd[t * C : (t + 1) * C, :] = nn(turned_cells[cell], shifted[rs][cs])

    pack_rows(read_d, cD, 144)
    core_start(cD, rcD, 0)

    below = shifted[1]
    grad_fourth = jnp.concatenate(
        grad_own[0]
        + [
            grad_own[1][0] + down_tap(0, 1, below[0]),
            grad_own[1][1] + down_tap(0, 0, below[1]) + down_tap(0, 2, below[0]),
        ],
        axis=0,
    )

    a2a_wait(a3r.at[0], 2)
    phalo = [remote(a3r.at[0], hp.at[1], sent, hr.at[5], (fr, up))]

    grad_res = act_grad(residual, grad_fourth)
    grad_res_b = grad_res.astype(bf16)
    gp_[...] = tn(mixed, grad_res_b)
    grad_mixed = nt(grad_res_b, wo[...]).astype(bf16)

    first_start(cD, rcD, yD, rlD, 0, 144, (1,))

    perm_frames = one_at(j256 == (i256 & 3) * 64 + 2 * k8 + f8)
    a4s[...] = pack(nn(perm_frames, fourth_b)).astype(bf16)
    a2a_start(a4s, a4r, 3)

    a2a_wait(a3r.at[1], 4)
    phalo.append(remote(a3r.at[1], hp.at[0], sent, hr.at[4], (fr, down)))

    grad_w = nt(grad_mixed, value)
    grad_s = (
        weights * (grad_w - jnp.sum(grad_w * weights, axis=-1, keepdims=True)) * scale
    ).astype(bf16)
    grad_v = tn(weights_b, grad_mixed).astype(bf16)
    grad_q = nn(grad_s, key).astype(bf16)
    grad_k = tn(grad_s, query).astype(bf16)
    grad_proj = jnp.concatenate([grad_q, grad_k, grad_v], axis=1)
    grad_n = nt(grad_proj, wq[...]).astype(bf16).astype(f32)
    gq_[...] = tn(norm_b, grad_proj)
    grad_t = grad_res + rms_grad(norm_t, inv_t, grad_n)
    grad_tb = grad_t.astype(bf16)
    grad_tb32 = grad_tb.astype(f32)


    first_start(cD, rcD, yD, rlD, 0, 144, (0,))
    turned_second = second.astype(f32).T.astype(bf16)
    gt[0:C, :] = nn(turned_second, frame_shift(grad_tb32, -2).astype(bf16))
    gt[C : 2 * C, :] = nn(turned_second, frame_shift(grad_tb32, -1).astype(bf16))
    gt[2 * C :, :] = nn(turned_second, grad_tb)
    t_pack()

    grad_second = nt(grad_tb, wtk[2])
    grad_second = grad_second + frame_shift(nt(grad_tb, wtk[1]), -1)
    grad_second = grad_second + frame_shift(nt(grad_tb, wtk[0]), -2)
    grad_sb = (grad_t + act_grad(sp, grad_second)).astype(bf16)

    first_halves(cD, rcD, yD, ryD, 0, 144, (1,))
    def turn_rows(hh, rows):
        put(tmp, unpack(rows.astype(f32)))
        cells = [every_fourth(tmp, ww) for ww in range(4)]
        for b in range(3):
            pair = jnp.concatenate([cells[b], cells[b + 1]], axis=0)
            at_[b, :, 128 * hh : 128 * hh + 128] = pair.T.astype(bf16)

    def space_taps(a):
        for b in range(3):
            gs_[(3 * a + b) * C : (3 * a + b + 1) * C, :] = nn(at_[b, :, 128 * a : 128 * a + 256], grad_sb)

    turn_rows(1, a3r[0])
    turn_rows(2, a3r[1])
    space_taps(1)
    t_start()
    first_halves(cD, rcD, yD, ryD, 0, 144, (0,))

    for h in phalo:
        h.wait_recv()
    turn_rows(0, masked(hp[0], not_top))
    turn_rows(3, masked(hp[1], not_bottom))
    for a in (0, 2):
        space_taps(a)
    pack_rows(read_2, c2, 72)
    core_start(c2, rc2, 1)

    first_relay(cD, rcD, yD, rlD, ryD, 0, 144)
    direct_start(c2, rc2, y2, ry2, 1, 72)

    for h in range(2):
        first_wait(rcD, ryD, 0, h, 144)
        for p in range(2):
            total = first_total(cD, rcD, ryD, h, p, 144).astype(bf16)
            zD[h, 2 * p] = total[:144]
            zD[h, 2 * p + 1] = total[144:]
        second_start(zD, rzD, 0, h)
    a2a_wait(a4r, 3)
    put(tmp, unpack(a4r[...].astype(f32)))
    first_col = lax.broadcasted_iota(jnp.int32, (32, C), 0) == 0
    cells_of = [
        [
            [
                jnp.concatenate(
                    [tmp[u, pl.ds(4 * f + 2 * hh + wp, 32, stride=8), :] for u in range(2)], axis=1
                ).astype(bf16)
                for wp in range(2)
            ]
            for hh in range(2)
        ]
        for f in range(2)
    ]
    for f in range(2):
        for wp in range(2):
            lrow_s[f, wp] = cells_of[f][1][wp]
    lhalo = remote(lrow_s, lrow_r, sent, hr.at[3], (fr, down))
    gap = jnp.zeros((8, 128), f32)
    for h in range(2):
        direct_wait(rc2, ry2, 1, h)
        for p in range(2):
            total = first_total(c2, rc2, ry2, h, p, 72)
            zE[h, 2 * p] = jnp.concatenate([total[:72], gap], axis=0).astype(bf16)
            zE[h, 2 * p + 1] = jnp.concatenate([total[72:], gap], axis=0).astype(bf16)
        second_start(zE, rzE, 1, h)

    it, jt = iota2(128, C)
    dt, ut = it >> 4, it & 15
    perm_d = one_at(jt == jnp.where(ut < 9, 0, 63) + dt * 9 + ut)
    perm_e = one_at((ut < 9) & (jt == dt * 9 + ut))
    perm_r = one_at((ut >= 9) & (ut < 11) & (jt == 70 + dt * 9 + ut))

    def widened(total, rows):
        return jnp.concatenate([total.astype(bf16), jnp.zeros((C - rows, 128), bf16)], axis=0)

    for h in range(2):
        total_d = widened(second_total(zD, rzD, 0, h), 144)
        finD_s[h] = nn(perm_d, total_d).reshape(RS, 16, 128).astype(bf16)
        last_start(finD_s, finD_r, 0, h)
        total = widened(second_total(zE, rzE, 1, h), 80)
        finE_s[h] = (nn(perm_e, total) + nn(perm_r, total_d)).reshape(RS, 16, 128).astype(bf16)
        last_start(finE_s, finE_r, 1, h)
        if h == 0:
            t_last()

    lhalo.wait_recv()
    taps_in = []
    for a in range(3):
        here = [
            [masked(lrow_r[f, wp], not_top) if a == 0 else cells_of[f][a - 1][wp] for wp in range(2)]
            for f in range(2)
        ]
        for b in range(3):
            picked = [here[f][1 if b != 1 else 0].astype(f32) for f in range(2)]
            if b == 0:
                picked = [jnp.where(first_col, 0.0, pltpu.roll(v, 1, axis=0)) for v in picked]
            taps_in.append(jnp.concatenate(picked, axis=0).astype(bf16))
    latent = None
    for t in range(9):
        term = nn(taps_in[t], wd[t * C : (t + 1) * C, :])
        latent = term if latent is None else latent + term
    for f in range(2):
        lat_out[f, 0] = latent[32 * f : 32 * f + 32].astype(bf16)

    last_wait(finD_r, 0)
    for cc in range(2):
        total = last_total(finD_r, cc)
        g_out[pl.ds(48 + 2 * cc, 9, stride=4), :] = total[0:9]
        g_out[pl.ds(49 + 2 * cc, 7, stride=4), :] = total[9:16]
    t_finish()
    last_wait(finE_r, 1)
    for cc in range(2):
        total = last_total(finE_r, cc)
        g_out[pl.ds(cc, 9, stride=2), :] = total[0:9]
        g_out[pl.ds(77 + 2 * cc, 2, stride=4), :] = total[9:11]
    for h in halo + chalo + phalo + [lhalo]:
        h.wait_send()
    for send in (a1s, a2s, a3s.at[0], a3s.at[1], a4s):
        wait_for(send.at[pl.ds(0, FR - 1)], sent)
    for ref in (rcD, rlD, ryD, rzD, rc2, ry2, rzE, rcT, rzT, finT_s.at[pl.ds(0, 31)]):
        wait_for(ref, sent)
    for fin_s in (finD_s, finE_s):
        for h in range(2):
            wait_for(fin_s.at[h, pl.ds(0, 7)], sent)
            pl.when(jnp.logical_not(own[h]))(lambda fin_s=fin_s, h=h: wait_for(fin_s.at[h, 0], sent))


starts = (0, 24, 32, 40, 48)


def outputs(lat, g, lat_out, *outs):
    lat_out[...] = lat[...]
    for at, out in zip(starts, outs):
        out[...] = g[at : at + out.shape[0], :]


def per_device(frames_in, w_space, w_time, w_qkv, w_out, w_down, cotangent):
    def vb(*shape):
        return pltpu.VMEM(shape, bf16)

    def vf(*shape):
        return pltpu.VMEM(shape, f32)

    dma = pltpu.SemaphoreType.DMA
    scratch = [
        vb(2, 2, 64, C), vb(9 * C, C), vb(3 * C, C), vb(C, 3 * C), vb(C, C), vb(9 * C, 512), vb(2, 1, 32, 512),
        vb(2, 2, 64, C),
        vb(FR, 16, 128), vb(FR, 16, 128), vb(FR, 16, 128), vb(FR, 16, 128),
        vb(2, FR, 16, 128), vb(2, FR, 16, 128), vb(FR, 16, 128), vb(FR, 16, 128),
        vf(2, C, 128), vb(2, 2, 32, C), vb(2, 2, 32, C), vf(C, 128),
        vb(2, 64, 512), vb(2, 64, 512), vb(2, FR, 16, 128), vb(3, C, 512),
        vf(9 * C, 512), vf(3 * C, C), vf(C, 3 * C), vf(C, C), vf(9 * C, C),
    ]
    for rows in (144, 72):
        n = 4 * rows
        scratch += [vb(2, 2, 4, n, 128), vb(2, 4, n, 128), vb(2, 3, n, 128)]
        if rows == 144:
            scratch += [vb(2, 2, n // 2, 128), vb(2, 2, n, 128), vb(2, 4, 144, 128), vb(2, 3, 144, 128)]
            scratch += [vb(2, 8, 224, 128), vb(8, 224, 128), vb(8, 224, 128), vb(7, 224, 128)]
            scratch += [vb(32, 16, 128), vb(32, 16, 128)]
        else:
            scratch += [vb(2, 3, n, 128)]
    scratch += [vb(2, 4, 80, 128), vb(2, 3, 80, 128)]
    scratch += [vb(2, 8, 16, 128), vb(16, 16, 128), vb(2, 8, 16, 128), vb(16, 16, 128)]
    scratch += [
        dma((7,)), dma, dma((6,)), dma((5,)), dma((16,)), dma((4,)), dma((4,)), dma((4,)), dma((2,)), dma((10,)),
    ]
    anywhere = pl.BlockSpec(memory_space=pl.ANY)
    inside = pl.BlockSpec(memory_space=pltpu.VMEM)
    latent, grads = pl.pallas_call(
        kernel,
        out_shape=(vb(2, 1, 32, 512), vf(88, 128)),
        in_specs=[anywhere] * 7,
        out_specs=(inside, inside),
        scratch_shapes=scratch,
        compiler_params=pltpu.CompilerParams(has_side_effects=True, collective_id=0, vmem_limit_bytes=56 * 1024 * 1024),
        cost_estimate=pl.CostEstimate(flops=3 * 10**9, bytes_accessed=10**7, transcendentals=10**6),
    )(frames_in, w_space, w_time, w_qkv, w_out, w_down, cotangent)
    latent = pltpu.with_memory_space_constraint(latent, pltpu.VMEM)
    grads = pltpu.with_memory_space_constraint(grads, pltpu.VMEM)
    rows = (18, 6, 6, 2, 36)
    shapes = [latent.shape] + [(n, 128) for n in rows]
    results = pl.pallas_call(
        outputs,
        out_shape=[jax.ShapeDtypeStruct(v, f32 if i else bf16) for i, v in enumerate(shapes)],
        in_specs=[inside] * 2,
        out_specs=[inside] * 6,
    )(latent, grads)
    return (results[0],) + tuple(v.reshape(-1) for v in results[1:])


def solution(mesh):
    held = P("frame", "row", None, None)
    flat = P(("frame", "row"))
    return jax.shard_map(
        per_device,
        mesh=mesh,
        in_specs=(held, P(), P(), P(), P(), P(), held),
        out_specs=(held, flat, flat, flat, flat, flat),
        check_vma=False,
    )
```

```python
import math

import jax
import jax.numpy as jnp
from jax import lax
from jax.experimental import pallas as pl
from jax.experimental.pallas import tpu as pltpu
from jax.sharding import PartitionSpec as P

epsilon = 1e-06
f32 = jnp.float32
bf16 = jnp.bfloat16
MESH = pl.DeviceIdType.MESH
C = 256
FR, XS, ZS, YS, RS = 32, 4, 8, 4, 8


def nn(a, b):
    return jnp.dot(a, b, preferred_element_type=f32)


def nt(a, b):
    return lax.dot_general(a, b, (((1,), (1,)), ((), ())), preferred_element_type=f32)


def tn(a, b):
    return lax.dot_general(a, b, (((0,), (0,)), ((), ())), preferred_element_type=f32)


def inv_rms(v):
    return lax.rsqrt(jnp.mean(v * v, axis=-1, keepdims=True) + epsilon)


def sigmoid(n):
    return 1.0 / (1.0 + jnp.exp(-n))


def act(v):
    n = v * inv_rms(v)
    return n * sigmoid(n)


def rms_grad(normal, inv, upstream):
    return inv * (upstream - normal * jnp.mean(upstream * normal, axis=-1, keepdims=True))


def act_grad(v, upstream):
    inv = inv_rms(v)
    n = v * inv
    s = sigmoid(n)
    return rms_grad(n, inv, upstream * (s * (1.0 + n * (1.0 - s))))


def iota2(rows, cols):
    return (
        lax.broadcasted_iota(jnp.int32, (rows, cols), 0),
        lax.broadcasted_iota(jnp.int32, (rows, cols), 1),
    )


def one_at(hit):
    return jnp.where(hit, 1.0, 0.0).astype(bf16)


def frame_shift(v, by):
    frame = lax.broadcasted_iota(jnp.int32, v.shape, 0) & 63
    moved = pltpu.roll(v, by % v.shape[0], axis=0)
    keep = frame >= by if by > 0 else frame < 64 + by
    return jnp.where(keep, moved, 0.0)


def pack(m):
    m = m.reshape(FR, 8, C)
    return jnp.concatenate([m[:, :, :128], m[:, :, 128:]], axis=1)


def unpack(t):
    low = t[:, :8, :].reshape(C, 128)
    high = t[:, 8:16, :].reshape(C, 128)
    return jnp.concatenate([low, high], axis=1)


def put(ref, m):
    ref[0] = m[:, :128]
    ref[1] = m[:, 128:]


def every_fourth(ref, start):
    return jnp.concatenate([ref[u, pl.ds(start, 64, stride=4), :] for u in range(2)], axis=1)


def kernel(
    x_hbm, wsp_hbm, wt_hbm, wq_hbm, wo_hbm, wd_hbm, cot_hbm,
    lat_out, g_out,
    xv, wsp, wt, wq, wo, wd, cotv,
    halo_x,
    a1s, a1r, a2s, a2r, a3s, a3r, a4s, a4r,
    tmp, lrow_s, lrow_r, rows8, cc_, halo_c, hp, at_,
    gd, gt, gq_, gp_, gs_,
    cD, rcD, yD, rlD, ryD, zD, rzD,
    cT, rcT, zT, rzT, finT_s, finT_r,
    c2, rc2, y2, ry2,
    zE, rzE,
    finD_s, finD_r, finE_s, finE_r,
    lsem, sent, hr, ar, cs_r, ys_r, rl_r, zs_r, fs_r, t_r,
):
    fr = lax.axis_index("frame")
    r = lax.axis_index("row")
    z, x = fr >> 2, fr & 3
    y, c = r >> 1, r & 1

    def remote(src, dst, ssem, rsem, dev):
        cp = pltpu.make_async_remote_copy(
            src_ref=src, dst_ref=dst, send_sem=ssem, recv_sem=rsem, device_id=dev, device_id_type=MESH
        )
        cp.start()
        return cp

    def wait_for(ref, sem):
        pltpu.make_async_copy(ref, ref, sem).wait()

    up, down = (r + RS - 1) & 7, (r + 1) & 7
    turned = (y - z) & 3
    last = (turned * 4 + x, (4 + turned) * 4 + x)
    own = (last[0] == fr, last[1] == fr)

    places = (y, x)

    loads = []
    for i, (src, dst) in enumerate(
        ((cot_hbm, cotv), (x_hbm, xv), (wsp_hbm, wsp), (wd_hbm, wd), (wt_hbm, wt), (wq_hbm, wq), (wo_hbm, wo))
    ):
        cp = pltpu.make_async_copy(src, dst, lsem.at[i])
        cp.start()
        loads.append(cp)

    barrier = pltpu.get_barrier_semaphore()

    def tell(dev):
        pl.semaphore_signal(barrier, inc=1, device_id=dev, device_id_type=MESH)

    def far_first(n):
        t = n >> 2
        dz = 4 + (1 - 2 * (t & 1)) * ((t + 1) >> 1)
        return ((z + dz) & 7) * 4 + ((x + n + 1) & 3)

    lax.fori_loop(0, FR - 1, lambda n, carry: (tell((far_first(n), r)), carry)[1], 0)
    for dest in (up, down):
        tell((fr, dest))
    for s in range(2, RS - 1):
        tell((fr, (r + s) & 7))
    def a2a_start(send, recv, i):
        def step(n, carry):
            k = far_first(n)
            remote(send.at[k], recv.at[fr], sent, ar.at[i], (k, r))
            return carry

        lax.fori_loop(0, FR - 1, step, 0)
        recv[fr] = send[fr]

    def a2a_wait(recv, i):
        wait_for(recv.at[pl.ds(0, FR - 1)], ar.at[i])

    i256, j256 = iota2(C, C)
    k8, f8, h8, w8 = i256 >> 3, (i256 >> 2) & 1, (i256 >> 1) & 1, i256 & 1
    perm_cells = one_at(j256 == h8 * 128 + f8 * 64 + 2 * k8 + w8)
    i512, j512 = iota2(512, C)
    u16 = i512 & 15
    f16, q16 = u16 >> 2, u16 & 3
    jcol = (i512 >> 4) + (u16 >> 3)
    perm_cot = one_at((jcol < 32) & (j512 == q16 * 64 + (f16 & 1) * 32 + jcol))
    loads[0].wait()
    cot_rows = jnp.concatenate(
        [cotv[f, 0, :, 128 * q : 128 * q + 128] for q in range(4) for f in range(2)], axis=0
    )
    a2s[...] = nn(perm_cot, cot_rows).reshape(FR, 16, 128).astype(bf16)

    loads[1].wait()
    xf = jnp.concatenate([xv[0, 0], xv[1, 0], xv[0, 1], xv[1, 1]], axis=0).astype(f32)
    first = act(xf).astype(bf16)
    ip, jp = iota2(C, 128)
    wpos = 2 * (ip >> 3) - 1 + (ip & 3)
    perm_patch = one_at((wpos >= 0) & (wpos < 64) & (jp == ((ip >> 2) & 1) * 64 + wpos))
    a3s[0] = pack(nn(perm_patch, first[:128])).astype(bf16)
    a3s[1] = pack(nn(perm_patch, first[128:])).astype(bf16)
    loads[2].wait()

    def tap(a, b):
        return wsp[(3 * a + b) * C : (3 * a + b + 1) * C, :]

    parts = []
    for b in range(3):
        mid = nn(first, tap(1, b))
        other = jnp.concatenate([nn(first[128:], tap(2, b)), nn(first[:128], tap(0, b))], axis=0)
        parts.append(mid + other)
    pl.semaphore_wait(
        barrier, (FR - 1) + (RS - 1)
    )
    halo = [
        remote(x_hbm.at[:, 1], halo_x.at[0], sent, hr.at[0], (fr, down)),
        remote(x_hbm.at[:, 0], halo_x.at[1], sent, hr.at[1], (fr, up)),
    ]
    a2a_start(a2s, a2r, 1)
    halo[0].wait_recv()
    halo[1].wait_recv()
    top = act(jnp.concatenate([halo_x[0, 0], halo_x[0, 1]], axis=0).astype(f32))
    top = jnp.where(r > 0, top, 0.0).astype(bf16)
    bottom = act(jnp.concatenate([halo_x[1, 0], halo_x[1, 1]], axis=0).astype(f32))
    bottom = jnp.where(r < RS - 1, bottom, 0.0).astype(bf16)
    for b in range(3):
        parts[b] = parts[b] + jnp.concatenate([nn(top, tap(0, b)), nn(bottom, tap(2, b))], axis=0)
    col = i256 & 63
    spatial = xf + parts[1]
    spatial = spatial + jnp.where(col > 0, pltpu.roll(parts[0], 1, axis=0), 0.0)
    spatial = spatial + jnp.where(col < 63, pltpu.roll(parts[2], C - 1, axis=0), 0.0)
    a1s[...] = pack(nn(perm_cells, spatial.astype(bf16))).astype(bf16)
    a2a_start(a1s, a1r, 0)
    a2a_start(a3s.at[0], a3r.at[0], 2)

    a2a_wait(a2r, 1)
    got = a2r[...].astype(f32)
    cots = []
    for u in range(2):
        rows8[...] = got[:, 8 * u : 8 * u + 8, :].reshape(C, 128)
        cots.append(
            jnp.concatenate([rows8[pl.ds(q, 64, stride=4), :] for q in range(4)], axis=1).astype(bf16)
        )
        cc_[u] = cots[u]
    cot_cell = cots[0]
    chalo = [remote(cc_, halo_c, sent, hr.at[2], (fr, up))]
    a2a_start(a3s.at[1], a3r.at[1], 4)
    not_top, not_left = r > 0, fr > 0
    not_bottom, not_right = r < RS - 1, fr < FR - 1

    def masked(v, keep):
        return jnp.where(keep, v.astype(f32), 0.0).astype(bf16)

    for i in range(3, 7):
        loads[i].wait()

    def down_tap(a, b, v):
        return nt(v, wd[(3 * a + b) * C : (3 * a + b + 1) * C, :])

    grad_own = [
        [down_tap(a, 1, cots[0]), down_tap(a, 0, cots[1]) + down_tap(a, 2, cots[0])] for a in (1, 2)
    ]

    a2a_wait(a1r, 0)
    put(tmp, unpack(a1r[...].astype(f32)))
    sp = jnp.concatenate([every_fourth(tmp, cell) for cell in range(4)], axis=0)
    second = act(sp).astype(bf16)
    wtk = [wt[k * C : (k + 1) * C, :] for k in range(3)]
    temporal = sp + nn(second, wtk[2])
    temporal = temporal + frame_shift(nn(second, wtk[1]), 1)
    temporal = temporal + frame_shift(nn(second, wtk[0]), 2)
    temporal = temporal.astype(bf16).astype(f32)
    inv_t = inv_rms(temporal)
    norm_t = temporal * inv_t
    norm_b = norm_t.astype(bf16)

    proj = nn(norm_b, wq[...]).astype(bf16)
    query, key, value = proj[:, :C], proj[:, C : 2 * C], proj[:, 2 * C :]
    scale = 1.0 / math.sqrt(C)
    logits = nt(query, key) * scale
    allowed = ((i256 >> 6) == (j256 >> 6)) & (i256 >= j256)
    logits = jnp.where(allowed, logits, -1e30)
    exponent = jnp.exp(logits - jnp.max(logits, axis=-1, keepdims=True))
    weights = exponent / jnp.sum(exponent, axis=-1, keepdims=True)
    weights_b = weights.astype(bf16)
    mixed = nn(weights_b, value).astype(bf16)
    attended = nn(mixed, wo[...]).astype(bf16).astype(f32)
    residual = (temporal + attended).astype(bf16).astype(f32)
    fourth = act(residual)

    fourth_b = fourth.astype(bf16)

    def pack_rows(read, cbuf, rows):
        def step(p, carry):
            s1, pair = p >> 1, p & 1
            at = pl.multiple_of(pair * (2 * rows), 16)
            pairs = ((s1 * 4 + 2 * pair, s1 * 4 + 2 * pair + 1), (16 + 8 * pair + s1, 20 + 8 * pair + s1))
            for h, (one, two) in enumerate(pairs):
                for cc in range(2):
                    both = jnp.concatenate([read(one, cc), read(two, cc)], axis=0)
                    cbuf[cc, h, s1, pl.ds(at, 2 * rows), :] = both.astype(bf16)
            return carry

        lax.fori_loop(0, 8, step, 0)

    def read_d(block, cc):
        at = pl.multiple_of(block * 72, 8)
        return jnp.concatenate(
            [gd[pl.ds(at, 72), cc * 256 + q * 128 : cc * 256 + q * 128 + 128] for q in range(2)], axis=0
        )

    def read_1(block, cc):
        a24, a8 = pl.multiple_of(block * 24, 8), pl.multiple_of(block * 8, 8)
        pieces = [gt[pl.ds(a24, 24), cc * 128 : cc * 128 + 128]]
        pieces += [gq_[pl.ds(a8, 8), cc * 384 + m * 128 : cc * 384 + m * 128 + 128] for m in range(3)]
        pieces += [gp_[pl.ds(a8, 8), cc * 128 : cc * 128 + 128]]
        return jnp.concatenate(pieces, axis=0)

    def read_2(block, cc):
        at = pl.multiple_of(block * 72, 8)
        return gs_[pl.ds(at, 72), cc * 128 : cc * 128 + 128]

    def part(axis, place):
        return (place - z) & 3 if axis == 0 else place

    def core_start(cbuf, rc, i):
        for s in (2, 1, 3, 0):
            for h in range(2):
                j = part(h, (places[h] + s) & 3)
                remote(cbuf.at[1 - c, h, j], rc.at[h, j], sent, cs_r.at[8 * i + 4 * h + s], (fr, r ^ 1))


    def along(axis, j):
        return (fr, 2 * j + c) if axis == 0 else (z * 4 + j, r)

    def pair_sum(cbuf, rc, h, s, p, rows):
        j = part(h, (places[h] + s) & 3)
        here = slice(2 * rows * p, 2 * rows * (p + 1))
        return cbuf[c, h, j, here, :].astype(f32) + rc[h, j, here, :].astype(f32)

    def core_wait(rc, i, s, h):
        j = part(h, (places[h] + s) & 3)
        wait_for(rc.at[h, j], cs_r.at[8 * i + 4 * h + s])

    def send_half(yb, ry, i, h, way, p, rows):
        half = pl.ds(2 * rows * p, 2 * rows)
        place = (places[h] + (1, 3)[way]) & 3
        remote(
            yb.at[h, way, half], ry.at[h, way, half], sent, ys_r.at[2 * i + h], along(h, place)
        )

    def first_start(cbuf, rc, yb, rl, i, rows, hs):
        for h in hs:
            core_wait(rc, i, 2, h)
            for p in range(2):
                half = slice(2 * rows * p, 2 * rows * (p + 1))
                yb[h, 2, half, :] = pair_sum(cbuf, rc, h, 2, p, rows).astype(bf16)
                place = (places[h] + (1, 3)[p]) & 3
                remote(
                    yb.at[h, 2, pl.ds(2 * rows * p, 2 * rows)], rl.at[h, p],
                    sent, rl_r.at[4 * i + 2 * h + p], along(h, place),
                )

    def first_halves(cbuf, rc, yb, ry, i, rows, hs):
        for way in range(2):
            for h in hs:
                p = 1 - way
                core_wait(rc, i, (1, 3)[way], h)
                half = slice(2 * rows * p, 2 * rows * (p + 1))
                yb[h, way, half, :] = pair_sum(cbuf, rc, h, (1, 3)[way], p, rows).astype(bf16)
                send_half(yb, ry, i, h, way, p, rows)

    def direct_start(cbuf, rc, yb, ry, i, rows):
        for s, slot in ((2, 2), (1, 0), (3, 1)):
            for h in range(2):
                core_wait(rc, i, s, h)
                for p in range(2):
                    half = slice(2 * rows * p, 2 * rows * (p + 1))
                    yb[h, slot, half, :] = pair_sum(cbuf, rc, h, s, p, rows).astype(bf16)
                place = (places[h] + s) & 3
                remote(yb.at[h, slot], ry.at[h, slot], sent, ys_r.at[2 * i + h], along(h, place))

    def direct_wait(rc, ry, i, h):
        core_wait(rc, i, 0, h)
        wait_for(ry.at[h], ys_r.at[2 * i + h])

    def first_relay(cbuf, rc, yb, rl, ry, i, rows):
        for h in range(2):
            for way in range(2):
                wait_for(rl.at[h, way], rl_r.at[4 * i + 2 * h + way])
                half = slice(2 * rows * way, 2 * rows * (way + 1))
                total = pair_sum(cbuf, rc, h, (1, 3)[way], way, rows) + rl[h, way].astype(f32)
                yb[h, way, half, :] = total.astype(bf16)
                send_half(yb, ry, i, h, way, way, rows)

    def first_total(cbuf, rc, ry, h, p, rows):
        half = slice(2 * rows * p, 2 * rows * (p + 1))
        total = pair_sum(cbuf, rc, h, 0, p, rows)
        for way in range(ry.shape[1]):
            total = total + ry[h, way, half, :].astype(f32)
        return total

    def first_wait(rc, ry, i, h, rows):
        core_wait(rc, i, 0, h)
        wait_for(ry.at[h], ys_r.at[2 * i + h])

    def second_start(zbuf, rz, i, h):
        for s in (1, 2, 3):
            j = (places[1 - h] + s) & 3
            remote(zbuf.at[h, part(1 - h, j)], rz.at[h, s - 1], sent, zs_r.at[2 * i + h], along(1 - h, j))

    def second_total(zbuf, rz, i, h):
        total = zbuf[h, part(1 - h, places[1 - h])].astype(f32)
        wait_for(rz.at[h], zs_r.at[2 * i + h])
        for s in range(3):
            total = total + rz[h, s].astype(f32)
        return total

    mine = 2 * z + c

    def last_start(fin_s, fin_r, i, h):
        for s in range(RS):
            dest = (r + s) & 7

            def send(dest=dest):
                remote(fin_s.at[h, dest], fin_r.at[mine], sent, fs_r.at[i], (last[h], dest))

            if s:
                send()
            else:
                pl.when(jnp.logical_not(own[h]))(send)

                @pl.when(own[h])
                def _():
                    fin_r[mine] = fin_s[h, r]

    def last_wait(fin_r, i):
        @pl.when(own[0] | own[1])
        def _():
            wait_for(fin_r.at[pl.ds(0, 15)], fs_r.at[i])

        @pl.when(jnp.logical_not(own[0] | own[1]))
        def _():
            wait_for(fin_r, fs_r.at[i])

    def last_total(fin_r, cc):
        total = fin_r[cc].astype(f32)
        for zs in range(1, ZS):
            total = total + fin_r[2 * zs + cc].astype(f32)
        return total

    def t_pack():
        def step(p, carry):
            zd, pair = p >> 1, p & 1
            at = pl.multiple_of(pair * 112, 16)
            block = zd * 4 + 2 * pair
            for cc in range(2):
                both = jnp.concatenate([read_1(block, cc), read_1(block + 1, cc)], axis=0)
                cT[cc, zd, pl.ds(at, 112), :] = both.astype(bf16)
            return carry

        lax.fori_loop(0, 16, step, 0)
        for s in (4, 3, 5, 2, 6, 1, 7, 0):
            zd = (z + s) & 7
            remote(cT.at[1 - c, zd], rcT.at[zd], sent, t_r.at[s], (fr, r ^ 1))

    def t_start():
        for s in (4, 3, 5, 2, 6, 1, 7):
            zd = (z + s) & 7
            wait_for(rcT.at[zd], t_r.at[s])
            zT[zd] = (cT[c, zd].astype(f32) + rcT[zd].astype(f32)).astype(bf16)
            remote(zT.at[zd], rzT.at[s - 1], sent, t_r.at[8], (zd * 4 + x, r))

    plane = x * RS + r

    def t_last():
        wait_for(rcT.at[z], t_r.at[0])
        total = cT[c, z].astype(f32) + rcT[z].astype(f32)
        wait_for(rzT, t_r.at[8])
        for s in range(1, ZS):
            total = total + rzT[s - 1].astype(f32)
        total = jnp.concatenate([total.astype(bf16), jnp.zeros((32, 128), bf16)], axis=0)
        it, jt = iota2(512, C)
        xt, dt, ut = it >> 7, (it >> 4) & 7, it & 15
        source = jnp.where(ut < 3, dt * 3 + ut, jnp.where(ut < 6, 24 + (ut - 3) * 8 + dt, 48 + dt))
        perm_t = one_at((ut < 7) & (jt == xt * 56 + source))
        finT_s[...] = nn(perm_t, total).reshape(32, 16, 128).astype(bf16)

        def step(n, carry):
            dest = (plane + n) & 31
            remote(finT_s.at[dest], finT_r.at[plane], sent, t_r.at[9], (z * 4 + (dest >> 3), dest & 7))
            return carry

        lax.fori_loop(1, 32, step, 0)
        finT_r[plane] = finT_s[plane]

    def t_finish():
        wait_for(finT_r.at[pl.ds(0, 31)], t_r.at[9])
        for cc in range(2):
            total = finT_r[cc].astype(f32)
            for chip in range(1, XS * YS):
                total = total + finT_r[2 * chip + cc].astype(f32)
            g_out[pl.ds(24 + cc, 3, stride=2), :] = total[0:3]
            g_out[32 + 3 * cc : 35 + 3 * cc, :] = total[3:6]
            g_out[40 + cc : 41 + cc, :] = total[6:7]

    for h in chalo:
        h.wait_recv()
    shifted = (
        tuple(cots),
        (masked(halo_c[0], not_bottom), masked(halo_c[1], not_bottom)),
    )
    cots_of = (
        (3, 1, 1), (2, 1, 0), (3, 1, 0),
        (1, 0, 1), (0, 0, 0), (1, 0, 0),
        (3, 0, 1), (2, 0, 0), (3, 0, 0),
    )
    turned_cells = [fourth[64 * cell : 64 * cell + 64].T.astype(bf16) for cell in range(4)]
    for t, (cell, rs, cs) in enumerate(cots_of):
        gd[t * C : (t + 1) * C, :] = nn(turned_cells[cell], shifted[rs][cs])

    pack_rows(read_d, cD, 144)
    core_start(cD, rcD, 0)

    below = shifted[1]
    grad_fourth = jnp.concatenate(
        grad_own[0]
        + [
            grad_own[1][0] + down_tap(0, 1, below[0]),
            grad_own[1][1] + down_tap(0, 0, below[1]) + down_tap(0, 2, below[0]),
        ],
        axis=0,
    )

    a2a_wait(a3r.at[0], 2)
    phalo = [remote(a3r.at[0], hp.at[1], sent, hr.at[5], (fr, up))]

    grad_res = act_grad(residual, grad_fourth)
    grad_res_b = grad_res.astype(bf16)
    gp_[...] = tn(mixed, grad_res_b)
    grad_mixed = nt(grad_res_b, wo[...]).astype(bf16)

    first_start(cD, rcD, yD, rlD, 0, 144, (1,))

    perm_frames = one_at(j256 == (i256 & 3) * 64 + 2 * k8 + f8)
    a4s[...] = pack(nn(perm_frames, fourth_b)).astype(bf16)
    a2a_start(a4s, a4r, 3)

    a2a_wait(a3r.at[1], 4)
    phalo.append(remote(a3r.at[1], hp.at[0], sent, hr.at[4], (fr, down)))

    grad_w = nt(grad_mixed, value)
    grad_s = (
        weights * (grad_w - jnp.sum(grad_w * weights, axis=-1, keepdims=True)) * scale
    ).astype(bf16)
    grad_v = tn(weights_b, grad_mixed).astype(bf16)
    grad_q = nn(grad_s, key).astype(bf16)
    grad_k = tn(grad_s, query).astype(bf16)
    grad_proj = jnp.concatenate([grad_q, grad_k, grad_v], axis=1)
    grad_n = nt(grad_proj, wq[...]).astype(bf16).astype(f32)
    gq_[...] = tn(norm_b, grad_proj)
    grad_t = grad_res + rms_grad(norm_t, inv_t, grad_n)
    grad_tb = grad_t.astype(bf16)
    grad_tb32 = grad_tb.astype(f32)


    first_start(cD, rcD, yD, rlD, 0, 144, (0,))
    turned_second = second.astype(f32).T.astype(bf16)
    gt[0:C, :] = nn(turned_second, frame_shift(grad_tb32, -2).astype(bf16))
    gt[C : 2 * C, :] = nn(turned_second, frame_shift(grad_tb32, -1).astype(bf16))
    gt[2 * C :, :] = nn(turned_second, grad_tb)
    t_pack()

    grad_second = nt(grad_tb, wtk[2])
    grad_second = grad_second + frame_shift(nt(grad_tb, wtk[1]), -1)
    grad_second = grad_second + frame_shift(nt(grad_tb, wtk[0]), -2)
    grad_sb = (grad_t + act_grad(sp, grad_second)).astype(bf16)

    first_halves(cD, rcD, yD, ryD, 0, 144, (1,))
    def turn_rows(hh, rows):
        put(tmp, unpack(rows.astype(f32)))
        cells = [every_fourth(tmp, ww) for ww in range(4)]
        for b in range(3):
            pair = jnp.concatenate([cells[b], cells[b + 1]], axis=0)
            at_[b, :, 128 * hh : 128 * hh + 128] = pair.T.astype(bf16)

    def space_taps(a):
        for b in range(3):
            gs_[(3 * a + b) * C : (3 * a + b + 1) * C, :] = nn(at_[b, :, 128 * a : 128 * a + 256], grad_sb)

    turn_rows(1, a3r[0])
    turn_rows(2, a3r[1])
    space_taps(1)
    t_start()
    first_halves(cD, rcD, yD, ryD, 0, 144, (0,))

    for h in phalo:
        h.wait_recv()
    turn_rows(0, masked(hp[0], not_top))
    turn_rows(3, masked(hp[1], not_bottom))
    for a in (0, 2):
        space_taps(a)
    pack_rows(read_2, c2, 72)
    core_start(c2, rc2, 1)

    first_relay(cD, rcD, yD, rlD, ryD, 0, 144)
    direct_start(c2, rc2, y2, ry2, 1, 72)

    for h in range(2):
        first_wait(rcD, ryD, 0, h, 144)
        for p in range(2):
            total = first_total(cD, rcD, ryD, h, p, 144).astype(bf16)
            zD[h, 2 * p] = total[:144]
            zD[h, 2 * p + 1] = total[144:]
        second_start(zD, rzD, 0, h)
    gap = jnp.zeros((8, 128), f32)
    for h in range(2):
        direct_wait(rc2, ry2, 1, h)
        for p in range(2):
            total = first_total(c2, rc2, ry2, h, p, 72)
            zE[h, 2 * p] = jnp.concatenate([total[:72], gap], axis=0).astype(bf16)
            zE[h, 2 * p + 1] = jnp.concatenate([total[72:], gap], axis=0).astype(bf16)
        second_start(zE, rzE, 1, h)

    a2a_wait(a4r, 3)
    put(tmp, unpack(a4r[...].astype(f32)))
    first_col = lax.broadcasted_iota(jnp.int32, (32, C), 0) == 0
    cells_of = [
        [
            [
                jnp.concatenate(
                    [tmp[u, pl.ds(4 * f + 2 * hh + wp, 32, stride=8), :] for u in range(2)], axis=1
                ).astype(bf16)
                for wp in range(2)
            ]
            for hh in range(2)
        ]
        for f in range(2)
    ]
    for f in range(2):
        for wp in range(2):
            lrow_s[f, wp] = cells_of[f][1][wp]
    lhalo = remote(lrow_s, lrow_r, sent, hr.at[3], (fr, down))
    it, jt = iota2(128, C)
    dt, ut = it >> 4, it & 15
    perm_d = one_at(jt == jnp.where(ut < 9, 0, 63) + dt * 9 + ut)
    perm_e = one_at((ut < 9) & (jt == dt * 9 + ut))
    perm_r = one_at((ut >= 9) & (ut < 11) & (jt == 70 + dt * 9 + ut))

    def widened(total, rows):
        return jnp.concatenate([total.astype(bf16), jnp.zeros((C - rows, 128), bf16)], axis=0)

    for h in range(2):
        total_d = widened(second_total(zD, rzD, 0, h), 144)
        finD_s[h] = nn(perm_d, total_d).reshape(RS, 16, 128).astype(bf16)
        last_start(finD_s, finD_r, 0, h)
        total = widened(second_total(zE, rzE, 1, h), 80)
        finE_s[h] = (nn(perm_e, total) + nn(perm_r, total_d)).reshape(RS, 16, 128).astype(bf16)
        last_start(finE_s, finE_r, 1, h)
        if h == 0:
            t_last()

    lhalo.wait_recv()
    taps_in = []
    for a in range(3):
        here = [
            [masked(lrow_r[f, wp], not_top) if a == 0 else cells_of[f][a - 1][wp] for wp in range(2)]
            for f in range(2)
        ]
        for b in range(3):
            picked = [here[f][1 if b != 1 else 0].astype(f32) for f in range(2)]
            if b == 0:
                picked = [jnp.where(first_col, 0.0, pltpu.roll(v, 1, axis=0)) for v in picked]
            taps_in.append(jnp.concatenate(picked, axis=0).astype(bf16))
    latent = None
    for t in range(9):
        term = nn(taps_in[t], wd[t * C : (t + 1) * C, :])
        latent = term if latent is None else latent + term
    for f in range(2):
        lat_out[f, 0] = latent[32 * f : 32 * f + 32].astype(bf16)

    last_wait(finD_r, 0)
    for cc in range(2):
        total = last_total(finD_r, cc)
        g_out[pl.ds(48 + 2 * cc, 9, stride=4), :] = total[0:9]
        g_out[pl.ds(49 + 2 * cc, 7, stride=4), :] = total[9:16]
    t_finish()
    last_wait(finE_r, 1)
    for cc in range(2):
        total = last_total(finE_r, cc)
        g_out[pl.ds(cc, 9, stride=2), :] = total[0:9]
        g_out[pl.ds(77 + 2 * cc, 2, stride=4), :] = total[9:11]
    for h in halo + chalo + phalo + [lhalo]:
        h.wait_send()
    for send in (a1s, a2s, a3s.at[0], a3s.at[1], a4s):
        wait_for(send.at[pl.ds(0, FR - 1)], sent)
    for ref in (rcD, rlD, ryD, rzD, rc2, ry2, rzE, rcT, rzT, finT_s.at[pl.ds(0, 31)]):
        wait_for(ref, sent)
    for fin_s in (finD_s, finE_s):
        for h in range(2):
            wait_for(fin_s.at[h, pl.ds(0, 7)], sent)
            pl.when(jnp.logical_not(own[h]))(lambda fin_s=fin_s, h=h: wait_for(fin_s.at[h, 0], sent))


starts = (0, 24, 32, 40, 48)


def outputs(lat, g, lat_out, *outs):
    lat_out[...] = lat[...]
    for at, out in zip(starts, outs):
        out[...] = g[at : at + out.shape[0], :]


def per_device(frames_in, w_space, w_time, w_qkv, w_out, w_down, cotangent):
    def vb(*shape):
        return pltpu.VMEM(shape, bf16)

    def vf(*shape):
        return pltpu.VMEM(shape, f32)

    dma = pltpu.SemaphoreType.DMA
    scratch = [
        vb(2, 2, 64, C), vb(9 * C, C), vb(3 * C, C), vb(C, 3 * C), vb(C, C), vb(9 * C, 512), vb(2, 1, 32, 512),
        vb(2, 2, 64, C),
        vb(FR, 16, 128), vb(FR, 16, 128), vb(FR, 16, 128), vb(FR, 16, 128),
        vb(2, FR, 16, 128), vb(2, FR, 16, 128), vb(FR, 16, 128), vb(FR, 16, 128),
        vf(2, C, 128), vb(2, 2, 32, C), vb(2, 2, 32, C), vf(C, 128),
        vb(2, 64, 512), vb(2, 64, 512), vb(2, FR, 16, 128), vb(3, C, 512),
        vf(9 * C, 512), vf(3 * C, C), vf(C, 3 * C), vf(C, C), vf(9 * C, C),
    ]
    for rows in (144, 72):
        n = 4 * rows
        scratch += [vb(2, 2, 4, n, 128), vb(2, 4, n, 128), vb(2, 3, n, 128)]
        if rows == 144:
            scratch += [vb(2, 2, n // 2, 128), vb(2, 2, n, 128), vb(2, 4, 144, 128), vb(2, 3, 144, 128)]
            scratch += [vb(2, 8, 224, 128), vb(8, 224, 128), vb(8, 224, 128), vb(7, 224, 128)]
            scratch += [vb(32, 16, 128), vb(32, 16, 128)]
        else:
            scratch += [vb(2, 3, n, 128)]
    scratch += [vb(2, 4, 80, 128), vb(2, 3, 80, 128)]
    scratch += [vb(2, 8, 16, 128), vb(16, 16, 128), vb(2, 8, 16, 128), vb(16, 16, 128)]
    scratch += [
        dma((7,)), dma, dma((6,)), dma((5,)), dma((16,)), dma((4,)), dma((4,)), dma((4,)), dma((2,)), dma((10,)),
    ]
    anywhere = pl.BlockSpec(memory_space=pl.ANY)
    inside = pl.BlockSpec(memory_space=pltpu.VMEM)
    latent, grads = pl.pallas_call(
        kernel,
        out_shape=(vb(2, 1, 32, 512), vf(88, 128)),
        in_specs=[anywhere] * 7,
        out_specs=(inside, inside),
        scratch_shapes=scratch,
        compiler_params=pltpu.CompilerParams(has_side_effects=True, collective_id=0, vmem_limit_bytes=56 * 1024 * 1024),
        cost_estimate=pl.CostEstimate(flops=3 * 10**9, bytes_accessed=10**7, transcendentals=10**6),
    )(frames_in, w_space, w_time, w_qkv, w_out, w_down, cotangent)
    latent = pltpu.with_memory_space_constraint(latent, pltpu.VMEM)
    grads = pltpu.with_memory_space_constraint(grads, pltpu.VMEM)
    rows = (18, 6, 6, 2, 36)
    shapes = [latent.shape] + [(n, 128) for n in rows]
    results = pl.pallas_call(
        outputs,
        out_shape=[jax.ShapeDtypeStruct(v, f32 if i else bf16) for i, v in enumerate(shapes)],
        in_specs=[inside] * 2,
        out_specs=[inside] * 6,
    )(latent, grads)
    return (results[0],) + tuple(v.reshape(-1) for v in results[1:])


def solution(mesh):
    held = P("frame", "row", None, None)
    flat = P(("frame", "row"))
    return jax.shard_map(
        per_device,
        mesh=mesh,
        in_specs=(held, P(), P(), P(), P(), P(), held),
        out_specs=(held, flat, flat, flat, flat, flat),
        check_vma=False,
    )
```

```python
import math

import jax
import jax.numpy as jnp
from jax import lax
from jax.experimental import pallas as pl
from jax.experimental.pallas import tpu as pltpu
from jax.sharding import PartitionSpec as P

epsilon = 1e-06
f32 = jnp.float32
bf16 = jnp.bfloat16
MESH = pl.DeviceIdType.MESH
C = 256
FR, XS, ZS, YS, RS = 32, 4, 8, 4, 8


def nn(a, b):
    return jnp.dot(a, b, preferred_element_type=f32)


def nt(a, b):
    return lax.dot_general(a, b, (((1,), (1,)), ((), ())), preferred_element_type=f32)


def tn(a, b):
    return lax.dot_general(a, b, (((0,), (0,)), ((), ())), preferred_element_type=f32)


def inv_rms(v):
    return lax.rsqrt(jnp.mean(v * v, axis=-1, keepdims=True) + epsilon)


def sigmoid(n):
    return 1.0 / (1.0 + jnp.exp(-n))


def act(v):
    n = v * inv_rms(v)
    return n * sigmoid(n)


def rms_grad(normal, inv, upstream):
    return inv * (upstream - normal * jnp.mean(upstream * normal, axis=-1, keepdims=True))


def act_grad(v, upstream):
    inv = inv_rms(v)
    n = v * inv
    s = sigmoid(n)
    return rms_grad(n, inv, upstream * (s * (1.0 + n * (1.0 - s))))


def iota2(rows, cols):
    return (
        lax.broadcasted_iota(jnp.int32, (rows, cols), 0),
        lax.broadcasted_iota(jnp.int32, (rows, cols), 1),
    )


def one_at(hit):
    return jnp.where(hit, 1.0, 0.0).astype(bf16)


def frame_shift(v, by):
    frame = lax.broadcasted_iota(jnp.int32, v.shape, 0) & 63
    moved = pltpu.roll(v, by % v.shape[0], axis=0)
    keep = frame >= by if by > 0 else frame < 64 + by
    return jnp.where(keep, moved, 0.0)


def pack(m):
    m = m.reshape(FR, 8, C)
    return jnp.concatenate([m[:, :, :128], m[:, :, 128:]], axis=1)


def unpack(t):
    low = t[:, :8, :].reshape(C, 128)
    high = t[:, 8:16, :].reshape(C, 128)
    return jnp.concatenate([low, high], axis=1)


def put(ref, m):
    ref[0] = m[:, :128]
    ref[1] = m[:, 128:]


def every_fourth(ref, start):
    return jnp.concatenate([ref[u, pl.ds(start, 64, stride=4), :] for u in range(2)], axis=1)


def kernel(
    x_hbm, wsp_hbm, wt_hbm, wq_hbm, wo_hbm, wd_hbm, cot_hbm,
    lat_out, g_out,
    xv, wsp, wt, wq, wo, wd, cotv,
    halo_x,
    a1s, a1r, a2s, a2r, a3s, a3r, a4s, a4r,
    tmp, lrow_s, lrow_r, rows8, cc_, halo_c, hp, at_,
    gd, gt, gq_, gp_, gs_,
    cD, rcD, yD, rlD, ryD, zD, rzD,
    cT, rcT, zT, rzT, finT_s, finT_r,
    c2, rc2, y2, ry2,
    zE, rzE,
    finD_s, finD_r, finE_s, finE_r,
    lsem, sent, hr, ar, cs_r, ys_r, rl_r, zs_r, fs_r, t_r,
):
    fr = lax.axis_index("frame")
    r = lax.axis_index("row")
    z, x = fr >> 2, fr & 3
    y, c = r >> 1, r & 1

    def remote(src, dst, ssem, rsem, dev):
        cp = pltpu.make_async_remote_copy(
            src_ref=src, dst_ref=dst, send_sem=ssem, recv_sem=rsem, device_id=dev, device_id_type=MESH
        )
        cp.start()
        return cp

    def wait_for(ref, sem):
        pltpu.make_async_copy(ref, ref, sem).wait()

    up, down = (r + RS - 1) & 7, (r + 1) & 7
    turned = (y - z) & 3
    last = (turned * 4 + x, (4 + turned) * 4 + x)
    own = (last[0] == fr, last[1] == fr)

    places = (y, x)

    barrier = pltpu.get_barrier_semaphore()

    def tell(dev):
        pl.semaphore_signal(barrier, inc=1, device_id=dev, device_id_type=MESH)

    def far_first(n):
        t = n >> 2
        dz = 4 + (1 - 2 * (t & 1)) * ((t + 1) >> 1)
        return ((z + dz) & 7) * 4 + ((x + n + 1) & 3)

    lax.fori_loop(0, FR - 1, lambda n, carry: (tell((far_first(n), r)), carry)[1], 0)
    for dest in (up, down):
        tell((fr, dest))
    for s in range(2, RS - 1):
        tell((fr, (r + s) & 7))
    loads = []
    for i, (src, dst) in enumerate(
        ((cot_hbm, cotv), (x_hbm, xv), (wsp_hbm, wsp), (wd_hbm, wd), (wt_hbm, wt), (wq_hbm, wq), (wo_hbm, wo))
    ):
        cp = pltpu.make_async_copy(src, dst, lsem.at[i])
        cp.start()
        loads.append(cp)

    def a2a_start(send, recv, i):
        def step(n, carry):
            k = far_first(n)
            remote(send.at[k], recv.at[fr], sent, ar.at[i], (k, r))
            return carry

        lax.fori_loop(0, FR - 1, step, 0)
        recv[fr] = send[fr]

    def a2a_wait(recv, i):
        wait_for(recv.at[pl.ds(0, FR - 1)], ar.at[i])

    i256, j256 = iota2(C, C)
    k8, f8, h8, w8 = i256 >> 3, (i256 >> 2) & 1, (i256 >> 1) & 1, i256 & 1
    perm_cells = one_at(j256 == h8 * 128 + f8 * 64 + 2 * k8 + w8)
    i512, j512 = iota2(512, C)
    u16 = i512 & 15
    f16, q16 = u16 >> 2, u16 & 3
    jcol = (i512 >> 4) + (u16 >> 3)
    perm_cot = one_at((jcol < 32) & (j512 == q16 * 64 + (f16 & 1) * 32 + jcol))
    loads[0].wait()
    cot_rows = jnp.concatenate(
        [cotv[f, 0, :, 128 * q : 128 * q + 128] for q in range(4) for f in range(2)], axis=0
    )
    a2s[...] = nn(perm_cot, cot_rows).reshape(FR, 16, 128).astype(bf16)

    loads[1].wait()
    xf = jnp.concatenate([xv[0, 0], xv[1, 0], xv[0, 1], xv[1, 1]], axis=0).astype(f32)
    first = act(xf).astype(bf16)
    ip, jp = iota2(C, 128)
    wpos = 2 * (ip >> 3) - 1 + (ip & 3)
    perm_patch = one_at((wpos >= 0) & (wpos < 64) & (jp == ((ip >> 2) & 1) * 64 + wpos))
    a3s[0] = pack(nn(perm_patch, first[:128])).astype(bf16)
    a3s[1] = pack(nn(perm_patch, first[128:])).astype(bf16)
    loads[2].wait()

    def tap(a, b):
        return wsp[(3 * a + b) * C : (3 * a + b + 1) * C, :]

    parts = []
    for b in range(3):
        mid = nn(first, tap(1, b))
        other = jnp.concatenate([nn(first[128:], tap(2, b)), nn(first[:128], tap(0, b))], axis=0)
        parts.append(mid + other)
    pl.semaphore_wait(
        barrier, (FR - 1) + (RS - 1)
    )
    halo = [
        remote(x_hbm.at[:, 1], halo_x.at[0], sent, hr.at[0], (fr, down)),
        remote(x_hbm.at[:, 0], halo_x.at[1], sent, hr.at[1], (fr, up)),
    ]
    a2a_start(a2s, a2r, 1)
    halo[0].wait_recv()
    halo[1].wait_recv()
    top = act(jnp.concatenate([halo_x[0, 0], halo_x[0, 1]], axis=0).astype(f32))
    top = jnp.where(r > 0, top, 0.0).astype(bf16)
    bottom = act(jnp.concatenate([halo_x[1, 0], halo_x[1, 1]], axis=0).astype(f32))
    bottom = jnp.where(r < RS - 1, bottom, 0.0).astype(bf16)
    for b in range(3):
        parts[b] = parts[b] + jnp.concatenate([nn(top, tap(0, b)), nn(bottom, tap(2, b))], axis=0)
    col = i256 & 63
    spatial = xf + parts[1]
    spatial = spatial + jnp.where(col > 0, pltpu.roll(parts[0], 1, axis=0), 0.0)
    spatial = spatial + jnp.where(col < 63, pltpu.roll(parts[2], C - 1, axis=0), 0.0)
    a1s[...] = pack(nn(perm_cells, spatial.astype(bf16))).astype(bf16)
    a2a_start(a1s, a1r, 0)
    a2a_start(a3s.at[0], a3r.at[0], 2)

    a2a_wait(a2r, 1)
    got = a2r[...].astype(f32)
    cots = []
    for u in range(2):
        rows8[...] = got[:, 8 * u : 8 * u + 8, :].reshape(C, 128)
        cots.append(
            jnp.concatenate([rows8[pl.ds(q, 64, stride=4), :] for q in range(4)], axis=1).astype(bf16)
        )
        cc_[u] = cots[u]
    cot_cell = cots[0]
    chalo = [remote(cc_, halo_c, sent, hr.at[2], (fr, up))]
    a2a_start(a3s.at[1], a3r.at[1], 4)
    not_top, not_left = r > 0, fr > 0
    not_bottom, not_right = r < RS - 1, fr < FR - 1

    def masked(v, keep):
        return jnp.where(keep, v.astype(f32), 0.0).astype(bf16)

    for i in range(3, 7):
        loads[i].wait()

    def down_tap(a, b, v):
        return nt(v, wd[(3 * a + b) * C : (3 * a + b + 1) * C, :])

    grad_own = [
        [down_tap(a, 1, cots[0]), down_tap(a, 0, cots[1]) + down_tap(a, 2, cots[0])] for a in (1, 2)
    ]

    a2a_wait(a1r, 0)
    put(tmp, unpack(a1r[...].astype(f32)))
    sp = jnp.concatenate([every_fourth(tmp, cell) for cell in range(4)], axis=0)
    second = act(sp).astype(bf16)
    wtk = [wt[k * C : (k + 1) * C, :] for k in range(3)]
    temporal = sp + nn(second, wtk[2])
    temporal = temporal + frame_shift(nn(second, wtk[1]), 1)
    temporal = temporal + frame_shift(nn(second, wtk[0]), 2)
    temporal = temporal.astype(bf16).astype(f32)
    inv_t = inv_rms(temporal)
    norm_t = temporal * inv_t
    norm_b = norm_t.astype(bf16)

    proj = nn(norm_b, wq[...]).astype(bf16)
    query, key, value = proj[:, :C], proj[:, C : 2 * C], proj[:, 2 * C :]
    scale = 1.0 / math.sqrt(C)
    logits = nt(query, key) * scale
    allowed = ((i256 >> 6) == (j256 >> 6)) & (i256 >= j256)
    logits = jnp.where(allowed, logits, -1e30)
    exponent = jnp.exp(logits - jnp.max(logits, axis=-1, keepdims=True))
    weights = exponent / jnp.sum(exponent, axis=-1, keepdims=True)
    weights_b = weights.astype(bf16)
    mixed = nn(weights_b, value).astype(bf16)
    attended = nn(mixed, wo[...]).astype(bf16).astype(f32)
    residual = (temporal + attended).astype(bf16).astype(f32)
    fourth = act(residual)

    fourth_b = fourth.astype(bf16)

    def pack_rows(read, cbuf, rows):
        def step(p, carry):
            s1, pair = p >> 1, p & 1
            at = pl.multiple_of(pair * (2 * rows), 16)
            pairs = ((s1 * 4 + 2 * pair, s1 * 4 + 2 * pair + 1), (16 + 8 * pair + s1, 20 + 8 * pair + s1))
            for h, (one, two) in enumerate(pairs):
                for cc in range(2):
                    both = jnp.concatenate([read(one, cc), read(two, cc)], axis=0)
                    cbuf[cc, h, s1, pl.ds(at, 2 * rows), :] = both.astype(bf16)
            return carry

        lax.fori_loop(0, 8, step, 0)

    def read_d(block, cc):
        at = pl.multiple_of(block * 72, 8)
        return jnp.concatenate(
            [gd[pl.ds(at, 72), cc * 256 + q * 128 : cc * 256 + q * 128 + 128] for q in range(2)], axis=0
        )

    def read_1(block, cc):
        a24, a8 = pl.multiple_of(block * 24, 8), pl.multiple_of(block * 8, 8)
        pieces = [gt[pl.ds(a24, 24), cc * 128 : cc * 128 + 128]]
        pieces += [gq_[pl.ds(a8, 8), cc * 384 + m * 128 : cc * 384 + m * 128 + 128] for m in range(3)]
        pieces += [gp_[pl.ds(a8, 8), cc * 128 : cc * 128 + 128]]
        return jnp.concatenate(pieces, axis=0)

    def read_2(block, cc):
        at = pl.multiple_of(block * 72, 8)
        return gs_[pl.ds(at, 72), cc * 128 : cc * 128 + 128]

    def part(axis, place):
        return (place - z) & 3 if axis == 0 else place

    def core_start(cbuf, rc, i):
        for s in (2, 1, 3, 0):
            for h in range(2):
                j = part(h, (places[h] + s) & 3)
                remote(cbuf.at[1 - c, h, j], rc.at[h, j], sent, cs_r.at[8 * i + 4 * h + s], (fr, r ^ 1))


    def along(axis, j):
        return (fr, 2 * j + c) if axis == 0 else (z * 4 + j, r)

    def pair_sum(cbuf, rc, h, s, p, rows):
        j = part(h, (places[h] + s) & 3)
        here = slice(2 * rows * p, 2 * rows * (p + 1))
        return cbuf[c, h, j, here, :].astype(f32) + rc[h, j, here, :].astype(f32)

    def core_wait(rc, i, s, h):
        j = part(h, (places[h] + s) & 3)
        wait_for(rc.at[h, j], cs_r.at[8 * i + 4 * h + s])

    def send_half(yb, ry, i, h, way, p, rows):
        half = pl.ds(2 * rows * p, 2 * rows)
        place = (places[h] + (1, 3)[way]) & 3
        remote(
            yb.at[h, way, half], ry.at[h, way, half], sent, ys_r.at[2 * i + h], along(h, place)
        )

    def first_start(cbuf, rc, yb, rl, i, rows, hs):
        for h in hs:
            core_wait(rc, i, 2, h)
            for p in range(2):
                half = slice(2 * rows * p, 2 * rows * (p + 1))
                yb[h, 2, half, :] = pair_sum(cbuf, rc, h, 2, p, rows).astype(bf16)
                place = (places[h] + (1, 3)[p]) & 3
                remote(
                    yb.at[h, 2, pl.ds(2 * rows * p, 2 * rows)], rl.at[h, p],
                    sent, rl_r.at[4 * i + 2 * h + p], along(h, place),
                )

    def first_halves(cbuf, rc, yb, ry, i, rows, hs):
        for way in range(2):
            for h in hs:
                p = 1 - way
                core_wait(rc, i, (1, 3)[way], h)
                half = slice(2 * rows * p, 2 * rows * (p + 1))
                yb[h, way, half, :] = pair_sum(cbuf, rc, h, (1, 3)[way], p, rows).astype(bf16)
                send_half(yb, ry, i, h, way, p, rows)

    def direct_start(cbuf, rc, yb, ry, i, rows):
        for s, slot in ((2, 2), (1, 0), (3, 1)):
            for h in range(2):
                core_wait(rc, i, s, h)
                for p in range(2):
                    half = slice(2 * rows * p, 2 * rows * (p + 1))
                    yb[h, slot, half, :] = pair_sum(cbuf, rc, h, s, p, rows).astype(bf16)
                place = (places[h] + s) & 3
                remote(yb.at[h, slot], ry.at[h, slot], sent, ys_r.at[2 * i + h], along(h, place))

    def direct_wait(rc, ry, i, h):
        core_wait(rc, i, 0, h)
        wait_for(ry.at[h], ys_r.at[2 * i + h])

    def first_relay(cbuf, rc, yb, rl, ry, i, rows):
        for h in range(2):
            for way in range(2):
                wait_for(rl.at[h, way], rl_r.at[4 * i + 2 * h + way])
                half = slice(2 * rows * way, 2 * rows * (way + 1))
                total = pair_sum(cbuf, rc, h, (1, 3)[way], way, rows) + rl[h, way].astype(f32)
                yb[h, way, half, :] = total.astype(bf16)
                send_half(yb, ry, i, h, way, way, rows)

    def first_total(cbuf, rc, ry, h, p, rows):
        half = slice(2 * rows * p, 2 * rows * (p + 1))
        total = pair_sum(cbuf, rc, h, 0, p, rows)
        for way in range(ry.shape[1]):
            total = total + ry[h, way, half, :].astype(f32)
        return total

    def first_wait(rc, ry, i, h, rows):
        core_wait(rc, i, 0, h)
        wait_for(ry.at[h], ys_r.at[2 * i + h])

    def second_start(zbuf, rz, i, h):
        for s in (1, 2, 3):
            j = (places[1 - h] + s) & 3
            remote(zbuf.at[h, part(1 - h, j)], rz.at[h, s - 1], sent, zs_r.at[2 * i + h], along(1 - h, j))

    def second_total(zbuf, rz, i, h):
        total = zbuf[h, part(1 - h, places[1 - h])].astype(f32)
        wait_for(rz.at[h], zs_r.at[2 * i + h])
        for s in range(3):
            total = total + rz[h, s].astype(f32)
        return total

    mine = 2 * z + c

    def last_start(fin_s, fin_r, i, h):
        for s in range(RS):
            dest = (r + s) & 7

            def send(dest=dest):
                remote(fin_s.at[h, dest], fin_r.at[mine], sent, fs_r.at[i], (last[h], dest))

            if s:
                send()
            else:
                pl.when(jnp.logical_not(own[h]))(send)

                @pl.when(own[h])
                def _():
                    fin_r[mine] = fin_s[h, r]

    def last_wait(fin_r, i):
        @pl.when(own[0] | own[1])
        def _():
            wait_for(fin_r.at[pl.ds(0, 15)], fs_r.at[i])

        @pl.when(jnp.logical_not(own[0] | own[1]))
        def _():
            wait_for(fin_r, fs_r.at[i])

    def last_total(fin_r, cc):
        total = fin_r[cc].astype(f32)
        for zs in range(1, ZS):
            total = total + fin_r[2 * zs + cc].astype(f32)
        return total

    def t_pack():
        def step(p, carry):
            zd, pair = p >> 1, p & 1
            at = pl.multiple_of(pair * 112, 16)
            block = zd * 4 + 2 * pair
            for cc in range(2):
                both = jnp.concatenate([read_1(block, cc), read_1(block + 1, cc)], axis=0)
                cT[cc, zd, pl.ds(at, 112), :] = both.astype(bf16)
            return carry

        lax.fori_loop(0, 16, step, 0)
        for s in (4, 3, 5, 2, 6, 1, 7, 0):
            zd = (z + s) & 7
            remote(cT.at[1 - c, zd], rcT.at[zd], sent, t_r.at[s], (fr, r ^ 1))

    def t_start():
        for s in (4, 3, 5, 2, 6, 1, 7):
            zd = (z + s) & 7
            wait_for(rcT.at[zd], t_r.at[s])
            zT[zd] = (cT[c, zd].astype(f32) + rcT[zd].astype(f32)).astype(bf16)
            remote(zT.at[zd], rzT.at[s - 1], sent, t_r.at[8], (zd * 4 + x, r))

    plane = x * RS + r

    def t_last():
        wait_for(rcT.at[z], t_r.at[0])
        total = cT[c, z].astype(f32) + rcT[z].astype(f32)
        wait_for(rzT, t_r.at[8])
        for s in range(1, ZS):
            total = total + rzT[s - 1].astype(f32)
        total = jnp.concatenate([total.astype(bf16), jnp.zeros((32, 128), bf16)], axis=0)
        it, jt = iota2(512, C)
        xt, dt, ut = it >> 7, (it >> 4) & 7, it & 15
        source = jnp.where(ut < 3, dt * 3 + ut, jnp.where(ut < 6, 24 + (ut - 3) * 8 + dt, 48 + dt))
        perm_t = one_at((ut < 7) & (jt == xt * 56 + source))
        finT_s[...] = nn(perm_t, total).reshape(32, 16, 128).astype(bf16)

        def step(n, carry):
            dest = (plane + n) & 31
            remote(finT_s.at[dest], finT_r.at[plane], sent, t_r.at[9], (z * 4 + (dest >> 3), dest & 7))
            return carry

        lax.fori_loop(1, 32, step, 0)
        finT_r[plane] = finT_s[plane]

    def t_finish():
        wait_for(finT_r.at[pl.ds(0, 31)], t_r.at[9])
        for cc in range(2):
            total = finT_r[cc].astype(f32)
            for chip in range(1, XS * YS):
                total = total + finT_r[2 * chip + cc].astype(f32)
            g_out[pl.ds(24 + cc, 3, stride=2), :] = total[0:3]
            g_out[32 + 3 * cc : 35 + 3 * cc, :] = total[3:6]
            g_out[40 + cc : 41 + cc, :] = total[6:7]

    for h in chalo:
        h.wait_recv()
    shifted = (
        tuple(cots),
        (masked(halo_c[0], not_bottom), masked(halo_c[1], not_bottom)),
    )
    cots_of = (
        (3, 1, 1), (2, 1, 0), (3, 1, 0),
        (1, 0, 1), (0, 0, 0), (1, 0, 0),
        (3, 0, 1), (2, 0, 0), (3, 0, 0),
    )
    turned_cells = [fourth[64 * cell : 64 * cell + 64].T.astype(bf16) for cell in range(4)]
    for t, (cell, rs, cs) in enumerate(cots_of):
        gd[t * C : (t + 1) * C, :] = nn(turned_cells[cell], shifted[rs][cs])

    pack_rows(read_d, cD, 144)
    core_start(cD, rcD, 0)

    below = shifted[1]
    grad_fourth = jnp.concatenate(
        grad_own[0]
        + [
            grad_own[1][0] + down_tap(0, 1, below[0]),
            grad_own[1][1] + down_tap(0, 0, below[1]) + down_tap(0, 2, below[0]),
        ],
        axis=0,
    )

    a2a_wait(a3r.at[0], 2)
    phalo = [remote(a3r.at[0], hp.at[1], sent, hr.at[5], (fr, up))]

    grad_res = act_grad(residual, grad_fourth)
    grad_res_b = grad_res.astype(bf16)
    gp_[...] = tn(mixed, grad_res_b)
    grad_mixed = nt(grad_res_b, wo[...]).astype(bf16)

    first_start(cD, rcD, yD, rlD, 0, 144, (1,))

    perm_frames = one_at(j256 == (i256 & 3) * 64 + 2 * k8 + f8)
    a4s[...] = pack(nn(perm_frames, fourth_b)).astype(bf16)
    a2a_start(a4s, a4r, 3)

    a2a_wait(a3r.at[1], 4)
    phalo.append(remote(a3r.at[1], hp.at[0], sent, hr.at[4], (fr, down)))

    grad_w = nt(grad_mixed, value)
    grad_s = (
        weights * (grad_w - jnp.sum(grad_w * weights, axis=-1, keepdims=True)) * scale
    ).astype(bf16)
    grad_v = tn(weights_b, grad_mixed).astype(bf16)
    grad_q = nn(grad_s, key).astype(bf16)
    grad_k = tn(grad_s, query).astype(bf16)
    grad_proj = jnp.concatenate([grad_q, grad_k, grad_v], axis=1)
    grad_n = nt(grad_proj, wq[...]).astype(bf16).astype(f32)
    gq_[...] = tn(norm_b, grad_proj)
    grad_t = grad_res + rms_grad(norm_t, inv_t, grad_n)
    grad_tb = grad_t.astype(bf16)
    grad_tb32 = grad_tb.astype(f32)


    first_start(cD, rcD, yD, rlD, 0, 144, (0,))
    turned_second = second.astype(f32).T.astype(bf16)
    gt[0:C, :] = nn(turned_second, frame_shift(grad_tb32, -2).astype(bf16))
    gt[C : 2 * C, :] = nn(turned_second, frame_shift(grad_tb32, -1).astype(bf16))
    gt[2 * C :, :] = nn(turned_second, grad_tb)
    t_pack()

    grad_second = nt(grad_tb, wtk[2])
    grad_second = grad_second + frame_shift(nt(grad_tb, wtk[1]), -1)
    grad_second = grad_second + frame_shift(nt(grad_tb, wtk[0]), -2)
    grad_sb = (grad_t + act_grad(sp, grad_second)).astype(bf16)

    first_halves(cD, rcD, yD, ryD, 0, 144, (1,))
    def turn_rows(hh, rows):
        put(tmp, unpack(rows.astype(f32)))
        cells = [every_fourth(tmp, ww) for ww in range(4)]
        for b in range(3):
            pair = jnp.concatenate([cells[b], cells[b + 1]], axis=0)
            at_[b, :, 128 * hh : 128 * hh + 128] = pair.T.astype(bf16)

    def space_taps(a):
        for b in range(3):
            gs_[(3 * a + b) * C : (3 * a + b + 1) * C, :] = nn(at_[b, :, 128 * a : 128 * a + 256], grad_sb)

    turn_rows(1, a3r[0])
    turn_rows(2, a3r[1])
    space_taps(1)
    first_halves(cD, rcD, yD, ryD, 0, 144, (0,))
    t_start()

    for h in phalo:
        h.wait_recv()
    turn_rows(0, masked(hp[0], not_top))
    turn_rows(3, masked(hp[1], not_bottom))
    for a in (0, 2):
        space_taps(a)
    pack_rows(read_2, c2, 72)
    core_start(c2, rc2, 1)

    first_relay(cD, rcD, yD, rlD, ryD, 0, 144)
    direct_start(c2, rc2, y2, ry2, 1, 72)

    for h in range(2):
        first_wait(rcD, ryD, 0, h, 144)
        for p in range(2):
            total = first_total(cD, rcD, ryD, h, p, 144).astype(bf16)
            zD[h, 2 * p] = total[:144]
            zD[h, 2 * p + 1] = total[144:]
        second_start(zD, rzD, 0, h)
    a2a_wait(a4r, 3)
    put(tmp, unpack(a4r[...].astype(f32)))
    first_col = lax.broadcasted_iota(jnp.int32, (32, C), 0) == 0
    cells_of = [
        [
            [
                jnp.concatenate(
                    [tmp[u, pl.ds(4 * f + 2 * hh + wp, 32, stride=8), :] for u in range(2)], axis=1
                ).astype(bf16)
                for wp in range(2)
            ]
            for hh in range(2)
        ]
        for f in range(2)
    ]
    for f in range(2):
        for wp in range(2):
            lrow_s[f, wp] = cells_of[f][1][wp]
    lhalo = remote(lrow_s, lrow_r, sent, hr.at[3], (fr, down))
    gap = jnp.zeros((8, 128), f32)
    for h in range(2):
        direct_wait(rc2, ry2, 1, h)
        for p in range(2):
            total = first_total(c2, rc2, ry2, h, p, 72)
            zE[h, 2 * p] = jnp.concatenate([total[:72], gap], axis=0).astype(bf16)
            zE[h, 2 * p + 1] = jnp.concatenate([total[72:], gap], axis=0).astype(bf16)
        second_start(zE, rzE, 1, h)

    it, jt = iota2(128, C)
    dt, ut = it >> 4, it & 15
    perm_d = one_at(jt == jnp.where(ut < 9, 0, 63) + dt * 9 + ut)
    perm_e = one_at((ut < 9) & (jt == dt * 9 + ut))
    perm_r = one_at((ut >= 9) & (ut < 11) & (jt == 70 + dt * 9 + ut))

    def widened(total, rows):
        return jnp.concatenate([total.astype(bf16), jnp.zeros((C - rows, 128), bf16)], axis=0)

    for h in range(2):
        total_d = widened(second_total(zD, rzD, 0, h), 144)
        finD_s[h] = nn(perm_d, total_d).reshape(RS, 16, 128).astype(bf16)
        last_start(finD_s, finD_r, 0, h)
        total = widened(second_total(zE, rzE, 1, h), 80)
        finE_s[h] = (nn(perm_e, total) + nn(perm_r, total_d)).reshape(RS, 16, 128).astype(bf16)
        last_start(finE_s, finE_r, 1, h)
        if h == 0:
            t_last()

    lhalo.wait_recv()
    taps_in = []
    for a in range(3):
        here = [
            [masked(lrow_r[f, wp], not_top) if a == 0 else cells_of[f][a - 1][wp] for wp in range(2)]
            for f in range(2)
        ]
        for b in range(3):
            picked = [here[f][1 if b != 1 else 0].astype(f32) for f in range(2)]
            if b == 0:
                picked = [jnp.where(first_col, 0.0, pltpu.roll(v, 1, axis=0)) for v in picked]
            taps_in.append(jnp.concatenate(picked, axis=0).astype(bf16))
    latent = None
    for t in range(9):
        term = nn(taps_in[t], wd[t * C : (t + 1) * C, :])
        latent = term if latent is None else latent + term
    for f in range(2):
        lat_out[f, 0] = latent[32 * f : 32 * f + 32].astype(bf16)

    last_wait(finD_r, 0)
    for cc in range(2):
        total = last_total(finD_r, cc)
        g_out[pl.ds(48 + 2 * cc, 9, stride=4), :] = total[0:9]
        g_out[pl.ds(49 + 2 * cc, 7, stride=4), :] = total[9:16]
    t_finish()
    last_wait(finE_r, 1)
    for cc in range(2):
        total = last_total(finE_r, cc)
        g_out[pl.ds(cc, 9, stride=2), :] = total[0:9]
        g_out[pl.ds(77 + 2 * cc, 2, stride=4), :] = total[9:11]
    for h in halo + chalo + phalo + [lhalo]:
        h.wait_send()
    for send in (a1s, a2s, a3s.at[0], a3s.at[1], a4s):
        wait_for(send.at[pl.ds(0, FR - 1)], sent)
    for ref in (rcD, rlD, ryD, rzD, rc2, ry2, rzE, rcT, rzT, finT_s.at[pl.ds(0, 31)]):
        wait_for(ref, sent)
    for fin_s in (finD_s, finE_s):
        for h in range(2):
            wait_for(fin_s.at[h, pl.ds(0, 7)], sent)
            pl.when(jnp.logical_not(own[h]))(lambda fin_s=fin_s, h=h: wait_for(fin_s.at[h, 0], sent))


starts = (0, 24, 32, 40, 48)


def outputs(lat, g, lat_out, *outs):
    lat_out[...] = lat[...]
    for at, out in zip(starts, outs):
        out[...] = g[at : at + out.shape[0], :]


def per_device(frames_in, w_space, w_time, w_qkv, w_out, w_down, cotangent):
    def vb(*shape):
        return pltpu.VMEM(shape, bf16)

    def vf(*shape):
        return pltpu.VMEM(shape, f32)

    dma = pltpu.SemaphoreType.DMA
    scratch = [
        vb(2, 2, 64, C), vb(9 * C, C), vb(3 * C, C), vb(C, 3 * C), vb(C, C), vb(9 * C, 512), vb(2, 1, 32, 512),
        vb(2, 2, 64, C),
        vb(FR, 16, 128), vb(FR, 16, 128), vb(FR, 16, 128), vb(FR, 16, 128),
        vb(2, FR, 16, 128), vb(2, FR, 16, 128), vb(FR, 16, 128), vb(FR, 16, 128),
        vf(2, C, 128), vb(2, 2, 32, C), vb(2, 2, 32, C), vf(C, 128),
        vb(2, 64, 512), vb(2, 64, 512), vb(2, FR, 16, 128), vb(3, C, 512),
        vf(9 * C, 512), vf(3 * C, C), vf(C, 3 * C), vf(C, C), vf(9 * C, C),
    ]
    for rows in (144, 72):
        n = 4 * rows
        scratch += [vb(2, 2, 4, n, 128), vb(2, 4, n, 128), vb(2, 3, n, 128)]
        if rows == 144:
            scratch += [vb(2, 2, n // 2, 128), vb(2, 2, n, 128), vb(2, 4, 144, 128), vb(2, 3, 144, 128)]
            scratch += [vb(2, 8, 224, 128), vb(8, 224, 128), vb(8, 224, 128), vb(7, 224, 128)]
            scratch += [vb(32, 16, 128), vb(32, 16, 128)]
        else:
            scratch += [vb(2, 3, n, 128)]
    scratch += [vb(2, 4, 80, 128), vb(2, 3, 80, 128)]
    scratch += [vb(2, 8, 16, 128), vb(16, 16, 128), vb(2, 8, 16, 128), vb(16, 16, 128)]
    scratch += [
        dma((7,)), dma, dma((6,)), dma((5,)), dma((16,)), dma((4,)), dma((4,)), dma((4,)), dma((2,)), dma((10,)),
    ]
    anywhere = pl.BlockSpec(memory_space=pl.ANY)
    inside = pl.BlockSpec(memory_space=pltpu.VMEM)
    latent, grads = pl.pallas_call(
        kernel,
        out_shape=(vb(2, 1, 32, 512), vf(88, 128)),
        in_specs=[anywhere] * 7,
        out_specs=(inside, inside),
        scratch_shapes=scratch,
        compiler_params=pltpu.CompilerParams(has_side_effects=True, collective_id=0, vmem_limit_bytes=56 * 1024 * 1024),
        cost_estimate=pl.CostEstimate(flops=3 * 10**9, bytes_accessed=10**7, transcendentals=10**6),
    )(frames_in, w_space, w_time, w_qkv, w_out, w_down, cotangent)
    latent = pltpu.with_memory_space_constraint(latent, pltpu.VMEM)
    grads = pltpu.with_memory_space_constraint(grads, pltpu.VMEM)
    rows = (18, 6, 6, 2, 36)
    shapes = [latent.shape] + [(n, 128) for n in rows]
    results = pl.pallas_call(
        outputs,
        out_shape=[jax.ShapeDtypeStruct(v, f32 if i else bf16) for i, v in enumerate(shapes)],
        in_specs=[inside] * 2,
        out_specs=[inside] * 6,
    )(latent, grads)
    return (results[0],) + tuple(v.reshape(-1) for v in results[1:])


def solution(mesh):
    held = P("frame", "row", None, None)
    flat = P(("frame", "row"))
    return jax.shard_map(
        per_device,
        mesh=mesh,
        in_specs=(held, P(), P(), P(), P(), P(), held),
        out_specs=(held, flat, flat, flat, flat, flat),
        check_vma=False,
    )
```
